32 devices in a mesh: grp: 2 (over x), seq: 8 (over z, y), mp: 2 (over core).
Axes of the slice: x: 2, y: 2, z: 4, core: 2. Of those that a mesh axis runs over, the one named last changes fastest.
Arguments:
- frames: bfloat16 [1536, 8192], P(('grp', 'seq'), 'mp'), may hold values from -80 to 80
- token_session: int32 [1536], P(('grp', 'seq')), may hold values from 0 to 127, as said below
- ln_gain: float32 [8192], P('mp'), may hold values from 0.3 to 1.7
- w_key: bfloat16 [8192, 512], P('mp'), may hold values from -0.0625 to 0.0625
- w_value: bfloat16 [8192, 512], P('mp'), may hold values from -0.0625 to 0.0625
- k_bias: float32 [512], P('mp'), may hold values from -4 to 4
- v_bias: float32 [512], P('mp'), may hold values from -4 to 4
- queries: bfloat16 [128, 4096], P(('grp', 'seq'), 'mp'), may hold values from -4 to 4
- cache_key: bfloat16 [128, 128, 512], P(('grp', 'seq'), None, 'mp'), may hold values from -11 to 11
- cache_value: bfloat16 [128, 128, 512], P(('grp', 'seq'), None, 'mp'), may hold values from -6 to 6
- cache_start: int32 [128], P(('grp', 'seq')), may hold values from 0 to 127
- cache_len: int32 [128], P(('grp', 'seq')), may hold values from 1 to 128
Outputs:
- attended: bfloat16 [128, 4096], P(('grp', 'seq'), 'mp')
The draws below stay inside these ranges and needn't reach their ends.
Inputs may be any that keep to these rules, and one draw needn't show every extreme that they name: `token_session`: each new frame token names a session; within the rows of one device at most 16 rows name sessions of one block of 8 consecutive sessions, and in every draw one such block gets exactly 16 rows from every device.
All inputs are finite; a program needn't handle non-finite values.
Results may differ from the reference program's by a relative error of at most 0.0023.
The reference program's roundings to bfloat16 on the way count: a program that leaves them out, or rounds other values in their place, can miss the bound.
Values may be sent and summed in bfloat16 or wider, within the bound.
No kernel may reach another device: no remote copies, remote signals or barrier semaphores. Data moves between devices by JAX's collectives and lax.ppermute only.
A program may use at most 64 MiB of HBM per device.

```python
import jax
import jax.numpy as jnp
from jax import lax

D = 8192
HEAD = 128
GROUP = 8
KV_HEADS = 4
ENC_DEV = 96
STR_DEV = 8
WIN = 128
CAP = 16
ROWS = 1536
STREAMS = 128
QH = 32


def draw_frames(key, part):
    key_rows, key_cols, key_base = jax.random.split(jax.random.fold_in(key, 3), 3)
    row_scale = jnp.exp(jax.random.uniform(key_rows, (ROWS, 1), jnp.float32) * jnp.log(10.0))
    col_scale = jnp.exp(jax.random.uniform(key_cols, (1, D), jnp.float32) * jnp.log(10.0))
    base = jnp.clip(jax.random.normal(key_base, (ROWS, D), jnp.float32), -4.0, 4.0)
    return (0.2 * base * row_scale * col_scale).astype(jnp.bfloat16)


def draw_token_session(key, part):
    blocks = ROWS // ENC_DEV
    partition_count = STREAMS // STR_DEV
    count_of_slots = partition_count * CAP
    busiest_prng_key, credit_prng_key, perturb_prng_key, selection_prng_key, displacement_prng_key = jax.random.split(jax.random.fold_in(key, 11), 5)
    busiest_slot = jax.random.randint(busiest_prng_key, (), 0, partition_count)
    extra_credit = jax.random.randint(credit_prng_key, (partition_count,), 0, 3) * 1024
    extra_credit = jnp.where(jnp.arange(partition_count, dtype=jnp.int32) == busiest_slot, 8192, extra_credit)
    slot_partition = jnp.arange(count_of_slots, dtype=jnp.int32) // CAP
    random_perturbation = jax.random.randint(perturb_prng_key, (blocks, count_of_slots), 0, 1024)
    slot_score_values = (extra_credit[slot_partition][None, :] + random_perturbation) * count_of_slots + jnp.arange(count_of_slots, dtype=jnp.int32)[None, :]
    unused, picked = lax.top_k(slot_score_values, ENC_DEV)
    target = picked // CAP
    choose = jax.random.randint(selection_prng_key, (blocks, ENC_DEV), 0, 2 * STR_DEV)
    local = jnp.where(choose < STR_DEV, choose, (choose - STR_DEV) // 2)
    offsets = jax.random.randint(displacement_prng_key, (partition_count,), 0, STR_DEV)
    local = jnp.mod(local + offsets[target], STR_DEV)
    return (target * STR_DEV + local).reshape(ROWS).astype(jnp.int32)


def draw_queries(key, part):
    key_base = jax.random.fold_in(key, 13)
    base = jnp.clip(jax.random.normal(key_base, (STREAMS, KV_HEADS, GROUP, HEAD), jnp.float32), -4.0, 4.0)
    return base.reshape(STREAMS, KV_HEADS * GROUP * HEAD).astype(jnp.bfloat16)


def draw_cache_key(key, part):
    key_base = jax.random.fold_in(jax.random.fold_in(key, 17), 0)
    base = jnp.clip(jax.random.normal(key_base, (STREAMS, WIN, KV_HEADS, HEAD), jnp.float32), -4.0, 4.0)
    return base.reshape(STREAMS, WIN, KV_HEADS * HEAD).astype(jnp.bfloat16)


def plant(drawn, key, least, high):
    spot = [jax.random.randint(jax.random.fold_in(key, axis), (), 0, length) for axis, length in enumerate(drawn.shape)]
    widest = drawn.shape.index(max(drawn.shape))
    beside = spot[:widest] + [(spot[widest] + 1) % drawn.shape[widest]] + spot[widest + 1:]
    return drawn.at[tuple(spot)].set(least).at[tuple(beside)].set(high)


def block_levels(rng, shape, pieces, low, high):
    gain, own = 1.0, jax.random.fold_in(rng, 6)
    for axis_at, blocks in pieces:
        heights = jnp.exp(jax.random.uniform(jax.random.fold_in(own, axis_at), (blocks,), jnp.float32, low / len(pieces), high / len(pieces)))
        gain = gain * jnp.repeat(heights, shape[axis_at] // blocks).reshape([-1 if axis == axis_at else 1 for axis in range(len(shape))])
    return gain


def centred(key, dims, scale, bound, cuts=(), kind=jnp.bfloat16):
    entries = scale * jax.random.normal(key, dims, jnp.float32)
    if cuts:
        entries = entries * block_levels(key, dims, cuts, -0.22, 0.18)
    return jnp.clip(entries, -bound, bound).astype(kind)


def setup_inputs(seed: int = 0) -> dict:
    arg_keys = jax.random.split(jax.random.key(seed), 13)
    frames = draw_frames(jax.random.fold_in(arg_keys[12], 71), 0)
    token_session = draw_token_session(jax.random.fold_in(arg_keys[12], 71), 0)
    ln_gain = jnp.clip(0.3 + 1.40000004 * jax.random.uniform(arg_keys[2], (D,), jnp.float32) ** block_levels(arg_keys[2], (D,), ((0, 2),), -0.2, 0.2), 0.3, 1.7)
    w_key = centred(arg_keys[3], (D, KV_HEADS * HEAD), D ** -0.5, 0.0625, ((0, 2),))
    w_value = centred(arg_keys[4], (D, KV_HEADS * HEAD), D ** -0.5, 0.0625, ((0, 2),))
    k_bias = centred(arg_keys[5], (KV_HEADS * HEAD,), 1.0, 4.0, ((0, 2),), jnp.float32)
    v_bias = centred(arg_keys[6], (KV_HEADS * HEAD,), 1.0, 4.0, ((0, 2),), jnp.float32)
    queries = draw_queries(jax.random.fold_in(arg_keys[12], 71), 0)
    cache_key = draw_cache_key(jax.random.fold_in(arg_keys[12], 71), 0)
    cache_value = centred(arg_keys[9], (STREAMS, WIN, KV_HEADS * HEAD), 1.0, 6.0, ((0, 16), (2, 2)))
    cache_start = plant(jax.random.randint(arg_keys[10], (STREAMS,), 0, WIN), jax.random.fold_in(arg_keys[10], 1), 0, WIN - 1).astype(jnp.int32)
    cache_len = plant(jax.random.randint(arg_keys[11], (STREAMS,), 1, WIN + 1), jax.random.fold_in(arg_keys[11], 1), 1, WIN).astype(jnp.int32)
    return dict(frames=frames, token_session=token_session, ln_gain=ln_gain, w_key=w_key, w_value=w_value, k_bias=k_bias, v_bias=v_bias, queries=queries, cache_key=cache_key, cache_value=cache_value, cache_start=cache_start, cache_len=cache_len)


epsilon = 1e-06

def project_block(frame_rows, ln_gain, w_key, w_value, k_bias, v_bias):
    values32 = frame_rows.astype(jnp.float32)
    inverse_rms = lax.rsqrt(lax.optimization_barrier(jnp.mean(values32 * values32, axis=1)) + epsilon)
    normed = (values32 * inverse_rms[:, None] * ln_gain[None, :]).astype(jnp.bfloat16)
    new_keys = jnp.dot(normed, w_key, preferred_element_type=jnp.float32) + k_bias[None, :]
    new_values = jnp.dot(normed, w_value, preferred_element_type=jnp.float32) + v_bias[None, :]
    return (new_keys.astype(jnp.bfloat16), new_values.astype(jnp.bfloat16))

def reference(frames, token_session, ln_gain, w_key, w_value, k_bias, v_bias, queries, cache_key, cache_value, cache_start, cache_len):
    blocks = frames.reshape(ROWS // ENC_DEV, ENC_DEV, D)

    def one_block(frame_block):
        return project_block(frame_block, ln_gain, w_key, w_value, k_bias, v_bias)
    new_keys, new_values = lax.map(one_block, blocks)
    new_keys = new_keys.reshape(ROWS, KV_HEADS, HEAD).astype(jnp.float32)
    new_values = new_values.reshape(ROWS, KV_HEADS, HEAD).astype(jnp.float32)
    score_scale = HEAD ** (-0.5)
    query_heads = queries.astype(jnp.float32).reshape(STREAMS, KV_HEADS, GROUP, HEAD)
    cached_keys = cache_key.astype(jnp.float32).reshape(STREAMS, WIN, KV_HEADS, HEAD)
    cached_values = cache_value.astype(jnp.float32).reshape(STREAMS, WIN, KV_HEADS, HEAD)
    cached_scores = jnp.einsum('sghd,swgd->sghw', query_heads, cached_keys) * score_scale
    positions = jnp.arange(WIN, dtype=jnp.int32)
    live_slots = jnp.mod(positions[None, :] - cache_start[:, None], WIN) < cache_len[:, None]
    cached_scores = jnp.where(live_slots[:, None, None, :], cached_scores, -jnp.inf)
    row_queries = query_heads[token_session]
    fresh_scores = jnp.einsum('rghd,rgd->rgh', row_queries, new_keys) * score_scale
    fresh_largest = jax.ops.segment_max(fresh_scores, token_session, num_segments=STREAMS)
    largest = jnp.maximum(lax.optimization_barrier(jnp.max(cached_scores, axis=3)), fresh_largest)
    cached_exp = jnp.exp(cached_scores - largest[..., None])
    fresh_exp = jnp.exp(fresh_scores - largest[token_session])
    totals = lax.optimization_barrier(jnp.sum(cached_exp, axis=3)) + jax.ops.segment_sum(fresh_exp, token_session, num_segments=STREAMS)
    cached_weights = (cached_exp / totals[..., None]).astype(jnp.bfloat16)
    fresh_weights = (fresh_exp / totals[token_session]).astype(jnp.bfloat16)
    attended = jnp.einsum('sghw,swgd->sghd', cached_weights.astype(jnp.float32), cached_values)
    fresh_terms = fresh_weights.astype(jnp.float32)[..., None] * new_values[:, :, None, :]
    attended = attended + jax.ops.segment_sum(fresh_terms, token_session, num_segments=STREAMS)
    return attended.reshape(STREAMS, QH * HEAD).astype(jnp.bfloat16)
```

```python
import functools

import jax
import jax.numpy as jnp
from jax import lax
from jax.experimental import pallas as pl
from jax.experimental.pallas import tpu as pltpu
from jax.sharding import PartitionSpec as P

HEAD = 128
GROUP = 8

epsilon = 1e-06


def params(mib):
    return pltpu.CompilerParams(vmem_limit_bytes=mib << 20)


def cost(flops, nbytes):
    return pl.CostEstimate(flops=flops, bytes_accessed=nbytes, transcendentals=0)


def nt_dot(a, b):
    return lax.dot_general(a, b, (((1,), (1,)), ((), ())), preferred_element_type=jnp.float32)


def dot(a, b):
    return jnp.dot(a, b, preferred_element_type=jnp.float32)


def squares_kernel(frames_ref, out_ref):
    columns = frames_ref.shape[1]
    total = None
    for at in range(0, columns, HEAD):
        part = frames_ref[:, at : at + HEAD].astype(jnp.float32)
        part = part * part
        total = part if total is None else total + part
    out_ref[...] = total


def partial_squares(frames):
    rows, columns = frames.shape
    return pl.pallas_call(
        squares_kernel,
        out_shape=jax.ShapeDtypeStruct((rows, HEAD), jnp.float32),
        compiler_params=params(8),
        cost_estimate=cost(2 * rows * columns, 2 * rows * columns),
        name="partial_squares",
    )(frames)


def halves(index_ref, normed, w_ref, sent_ref, kept_ref):
    mine = index_ref[0]
    width = sent_ref.shape[1]
    for half, out_ref in ((1 - mine, sent_ref), (mine, kept_ref)):
        columns = pl.ds(pl.multiple_of(half * width, width), width)
        out_ref[...] = dot(normed, w_ref[:, columns])


def key_kernel(
    features, index_ref, frames_ref, own_ref, other_ref, gain_ref, w_ref, normed_ref, sent_ref, kept_ref
):
    squares = jnp.sum(own_ref[...] + other_ref[...], axis=1, keepdims=True)
    inverse_rms = lax.rsqrt(squares / features + epsilon)
    normed_ref[...] = (
        frames_ref[...].astype(jnp.float32) * inverse_rms * gain_ref[...]
    ).astype(jnp.bfloat16)
    halves(index_ref, normed_ref[...], w_ref, sent_ref, kept_ref)


def value_kernel(index_ref, normed_ref, w_ref, sent_ref, kept_ref):
    halves(index_ref, normed_ref[...], w_ref, sent_ref, kept_ref)


SMEM = pl.BlockSpec(memory_space=pltpu.SMEM)
VMEM = pl.BlockSpec(memory_space=pltpu.VMEM)


def project_keys(index, frames, own, other, gain, w, features):
    rows, columns = frames.shape
    width = w.shape[1] // 2
    half = jax.ShapeDtypeStruct((rows, width), jnp.float32)
    return pl.pallas_call(
        functools.partial(key_kernel, features),
        out_shape=(jax.ShapeDtypeStruct(frames.shape, jnp.bfloat16), half, half),
        in_specs=[SMEM] + [VMEM] * 5,
        out_specs=(VMEM, VMEM, VMEM),
        compiler_params=params(16),
        cost_estimate=cost(4 * rows * columns * width, 2 * w.size),
        name="project_keys",
    )(index, frames, own, other, gain, w)


def project_values(index, normed, w):
    rows, columns = normed.shape
    width = w.shape[1] // 2
    half = jax.ShapeDtypeStruct((rows, width), jnp.float32)
    return pl.pallas_call(
        value_kernel,
        out_shape=(half, half),
        in_specs=[SMEM] + [VMEM] * 2,
        out_specs=(VMEM, VMEM),
        compiler_params=params(16),
        cost_estimate=cost(4 * rows * columns * width, 2 * w.size),
        name="project_values",
    )(index, normed, w)


def pack_kernel(
    per_shard,
    capacity,
    here_ref,
    session_ref,
    kept_key_ref,
    got_key_ref,
    kept_value_ref,
    got_value_ref,
    key_bias_ref,
    value_bias_ref,
    out_ref,
):
    partitions, _, _ = out_ref.shape
    rows, width = kept_key_ref.shape
    slots = partitions * capacity
    session = session_ref[...]
    target = lax.div(session, per_shard)
    local = session - target * per_shard
    to = lax.broadcasted_iota(jnp.int32, (partitions, rows), 0) == target
    to = to.astype(jnp.float32)
    earlier = lax.broadcasted_iota(jnp.int32, (rows, rows), 0) < lax.broadcasted_iota(
        jnp.int32, (rows, rows), 1
    )
    ahead = dot(to.astype(jnp.bfloat16), earlier.astype(jnp.bfloat16))
    order = jnp.sum(to * ahead, axis=0, keepdims=True).astype(jnp.int32)
    place = lax.broadcasted_iota(jnp.int32, (slots, rows), 0)
    pick = (place == target * capacity + order).astype(jnp.bfloat16)
    lane = (place == here_ref[0] * capacity + order).astype(jnp.bfloat16)
    ids = nt_dot((to * (local + 1).astype(jnp.float32)).astype(jnp.bfloat16), lane)
    key = (kept_key_ref[...] + got_key_ref[...] + key_bias_ref[...]).astype(jnp.bfloat16)
    value = (kept_value_ref[...] + got_value_ref[...] + value_bias_ref[...]).astype(jnp.bfloat16)
    at = 0
    for source in (key, value):
        laid = dot(pick, source).astype(jnp.bfloat16).reshape(partitions, capacity, width)
        for column in range(0, width, HEAD):
            out_ref[:, at : at + capacity, :] = laid[:, :, column : column + HEAD]
            at += capacity
    ids = ids.astype(jnp.bfloat16)
    extra = out_ref.shape[1] - at
    row = lax.broadcasted_iota(jnp.int32, (partitions, extra, HEAD), 1)
    block = jnp.zeros((partitions, extra, HEAD), jnp.float32)
    for j in range(slots // HEAD):
        part = ids[:, j * HEAD : (j + 1) * HEAD].astype(jnp.float32)
        block = jnp.where(row == j, part[:, None, :], block)
    out_ref[:, at:, :] = block.astype(jnp.bfloat16)


def pack(here, session, kept_key, got_key, kept_value, got_value, key_bias, value_bias, sizes):
    partitions, per_shard, capacity = sizes
    rows, width = kept_key.shape
    id_rows = -(-partitions * capacity // HEAD)
    block = 2 * width // HEAD * capacity + -(-id_rows // 8) * 8
    return pl.pallas_call(
        functools.partial(pack_kernel, per_shard, capacity),
        out_shape=jax.ShapeDtypeStruct((partitions, block, HEAD), jnp.bfloat16),
        in_specs=[SMEM] + [VMEM] * 7,
        out_specs=VMEM,
        compiler_params=params(8),
        cost_estimate=cost(4 * rows * width * partitions * capacity, 16 * rows * width),
        name="pack",
    )(here, session, kept_key, got_key, kept_value, got_value, key_bias, value_bias)


def queries_of(queries_ref, head):
    columns = [
        queries_ref[:, at * HEAD : (at + 1) * HEAD].astype(jnp.float32)
        for at in range(head * GROUP, (head + 1) * GROUP)
    ]
    return jnp.concatenate(columns, axis=0).astype(jnp.bfloat16)


def cached_kernel(start_ref, len_ref, queries_ref, key_ref, out_ref):
    heads, rows, window = out_ref.shape
    sessions = queries_ref.shape[0]
    row_session = lax.broadcasted_iota(jnp.int32, (rows, window), 0) % sessions
    slot = lax.broadcasted_iota(jnp.int32, (rows, window), 1)
    live = []
    for session in range(sessions):
        since = slot - start_ref[session]
        since = jnp.where(since < 0, since + window, since)
        live.append(since < len_ref[session])
    for head in range(heads):
        query = queries_of(queries_ref, head)
        total = jnp.full((rows, window), -jnp.inf, jnp.float32)
        for session in range(sessions):
            key = key_ref[session, :, head * HEAD : (head + 1) * HEAD]
            score = nt_dot(query, key) * (HEAD**-0.5)
            total = jnp.where((row_session == session) & live[session], score, total)
        out_ref[head] = total


def cached_scores(start, length, queries, cache_key):
    sessions, window, width = cache_key.shape
    heads = width // HEAD
    return pl.pallas_call(
        cached_kernel,
        out_shape=jax.ShapeDtypeStruct((heads, GROUP * sessions, window), jnp.float32),
        in_specs=[SMEM, SMEM, VMEM, VMEM],
        out_specs=VMEM,
        compiler_params=params(8),
        cost_estimate=cost(2 * GROUP * sessions * cache_key.size, 2 * cache_key.size),
        name="cached_scores",
    )(start, length, queries, cache_key)


def attend_kernel(capacity, got_ref, queries_ref, score_ref, cache_ref, out_ref):
    heads, rows, window = score_ref.shape
    sessions = queries_ref.shape[0]
    partitions = got_ref.shape[0]
    slots = partitions * capacity
    at = 2 * heads * capacity
    ids = jnp.concatenate(
        [
            jnp.sum(got_ref[:, at + j : at + j + 1, :].astype(jnp.float32), axis=0)
            for j in range(slots // HEAD)
        ],
        axis=1,
    ).astype(jnp.int32)
    own = lax.broadcasted_iota(jnp.int32, (rows, slots), 0) % sessions + 1 == ids
    row_session = lax.broadcasted_iota(jnp.int32, (rows, window), 0) % sessions
    for head in range(heads):
        query = queries_of(queries_ref, head)
        key = got_ref[:, head * capacity : (head + 1) * capacity, :].reshape(slots, HEAD)
        first = (heads + head) * capacity
        value = got_ref[:, first : first + capacity, :].reshape(slots, HEAD)
        cached = score_ref[head]
        fresh = jnp.where(own, nt_dot(query, key) * (HEAD**-0.5), -jnp.inf)
        largest = jnp.maximum(
            jnp.max(cached, axis=1, keepdims=True), jnp.max(fresh, axis=1, keepdims=True)
        )
        cached = jnp.exp(cached - largest)
        fresh = jnp.exp(fresh - largest)
        total = jnp.sum(cached, axis=1, keepdims=True) + jnp.sum(fresh, axis=1, keepdims=True)
        cached = cached / total
        attended = dot((fresh / total).astype(jnp.bfloat16), value)
        for session in range(sessions):
            weights = jnp.where(row_session == session, cached, 0.0).astype(jnp.bfloat16)
            attended += dot(weights, cache_ref[session, :, head * HEAD : (head + 1) * HEAD])
        for q in range(GROUP):
            column = (head * GROUP + q) * HEAD
            out_ref[:, column : column + HEAD] = attended[
                q * sessions : (q + 1) * sessions
            ].astype(jnp.bfloat16)


def attend(got, queries, scores, cache_value, capacity):
    return pl.pallas_call(
        functools.partial(attend_kernel, capacity),
        out_shape=jax.ShapeDtypeStruct(queries.shape, jnp.bfloat16),
        in_specs=[VMEM] * 4,
        out_specs=VMEM,
        compiler_params=params(8),
        cost_estimate=cost(4 * queries.shape[0] * GROUP * cache_value.size, 2 * cache_value.size),
        name="attend",
    )(got, queries, scores, cache_value)


def project(frame_rows, ln_gain, w_key, w_value, k_bias, v_bias):
    values32 = frame_rows.astype(jnp.float32)
    partial_squares = jnp.sum(values32 * values32, axis=1)
    squares = lax.psum(partial_squares, "mp")
    inverse_rms = lax.rsqrt(squares / (frame_rows.shape[1] * lax.axis_size("mp")) + epsilon)
    normed = (values32 * inverse_rms[:, None] * ln_gain[None, :]).astype(jnp.bfloat16)
    part_key = jnp.dot(normed, w_key, preferred_element_type=jnp.float32)
    part_value = jnp.dot(normed, w_value, preferred_element_type=jnp.float32)
    key_sums, value_sums = (
        lax.psum_scatter(part_key, "mp", scatter_dimension=1, tiled=True),
        lax.psum_scatter(part_value, "mp", scatter_dimension=1, tiled=True),
    )
    new_keys = (key_sums + k_bias[None, :]).astype(jnp.bfloat16)
    new_values = (value_sums + v_bias[None, :]).astype(jnp.bfloat16)
    return (new_keys, new_values)


def slot_sources(token_session, per_shard, partition_count, capacity):
    row_count = token_session.shape[0]
    target = token_session // per_shard
    one_hot = (target[:, None] == jnp.arange(partition_count, dtype=jnp.int32)[None, :]).astype(
        jnp.int32
    )
    order_in = jnp.sum((jnp.cumsum(one_hot, axis=0) - one_hot) * one_hot, axis=1)
    slot_index = target * capacity + order_in
    matches = (
        slot_index[None, :] == jnp.arange(partition_count * capacity, dtype=jnp.int32)[:, None]
    )
    source = jnp.sum(jnp.where(matches, jnp.arange(row_count, dtype=jnp.int32)[None, :], 0), axis=1)
    filled = jnp.any(matches, axis=1)
    sessions = jnp.where(filled, jnp.mod(token_session[source], per_shard), -1)
    return (source, filled, sessions)


def general(
    frames,
    token_session,
    ln_gain,
    w_key,
    w_value,
    k_bias,
    v_bias,
    queries,
    cache_key,
    cache_value,
    cache_start,
    cache_len,
):
    partition_count = lax.axis_size(("grp", "seq"))
    per_shard = queries.shape[0]
    rows_here = frames.shape[0]
    capacity = max(2, 5 * rows_here // (2 * partition_count) + 1)
    source, filled, sessions = slot_sources(token_session, per_shard, partition_count, capacity)
    session_slots = sessions.reshape(partition_count, capacity)
    nothing = jnp.zeros((), jnp.bfloat16)
    own_keys, own_values = project(frames, ln_gain, w_key, w_value, k_bias, v_bias)
    send_keys = jnp.where(filled[:, None], own_keys[source], nothing).reshape(
        partition_count, capacity, -1
    )
    send_values = jnp.where(filled[:, None], own_values[source], nothing).reshape(
        partition_count, capacity, -1
    )
    got_keys, got_values, got_sessions = (
        lax.all_to_all(send_keys, ("grp", "seq"), split_axis=0, concat_axis=0, tiled=True),
        lax.all_to_all(send_values, ("grp", "seq"), split_axis=0, concat_axis=0, tiled=True),
        lax.all_to_all(session_slots, ("grp", "seq"), split_axis=0, concat_axis=0, tiled=True),
    )
    new_keys = got_keys.reshape(partition_count * capacity, -1)
    new_values = got_values.reshape(partition_count * capacity, -1)
    new_sessions = got_sessions.reshape(-1)
    heads_kv = new_keys.shape[1] // HEAD
    window = cache_key.shape[1]
    score_scale = HEAD ** (-0.5)
    query_heads = queries.reshape(per_shard, heads_kv, GROUP, HEAD)
    cached_keys = cache_key.reshape(per_shard, window, heads_kv, HEAD)
    cached_values = cache_value.reshape(per_shard, window, heads_kv, HEAD)
    fresh_keys = new_keys.reshape(-1, heads_kv, HEAD)
    fresh_values = new_values.reshape(-1, heads_kv, HEAD)
    cached_scores = (
        jnp.einsum("sghd,swgd->sghw", query_heads, cached_keys, preferred_element_type=jnp.float32)
        * score_scale
    )
    positions = jnp.arange(window, dtype=jnp.int32)
    live_slots = jnp.mod(positions[None, :] - cache_start[:, None], window) < cache_len[:, None]
    cached_scores = jnp.where(live_slots[:, None, None, :], cached_scores, -jnp.inf)
    fresh_scores = (
        jnp.einsum("sghd,ngd->sghn", query_heads, fresh_keys, preferred_element_type=jnp.float32)
        * score_scale
    )
    own_rows = new_sessions[None, :] == jnp.arange(per_shard, dtype=jnp.int32)[:, None]
    fresh_scores = jnp.where(own_rows[:, None, None, :], fresh_scores, -jnp.inf)
    largest = jnp.maximum(jnp.max(cached_scores, axis=3), jnp.max(fresh_scores, axis=3))
    cached_exp = jnp.exp(cached_scores - largest[..., None])
    fresh_exp = jnp.exp(fresh_scores - largest[..., None])
    totals = jnp.sum(cached_exp, axis=3) + jnp.sum(fresh_exp, axis=3)
    cached_weights = (cached_exp / totals[..., None]).astype(jnp.bfloat16)
    fresh_weights = (fresh_exp / totals[..., None]).astype(jnp.bfloat16)
    attended = jnp.einsum(
        "sghw,swgd->sghd", cached_weights, cached_values, preferred_element_type=jnp.float32
    )
    attended = attended + jnp.einsum(
        "sghn,ngd->sghd", fresh_weights, fresh_values, preferred_element_type=jnp.float32
    )
    return attended.reshape(per_shard, -1).astype(jnp.bfloat16)


def local(
    frames,
    token_session,
    ln_gain,
    w_key,
    w_value,
    k_bias,
    v_bias,
    queries,
    cache_key,
    cache_value,
    cache_start,
    cache_len,
):
    partitions = lax.axis_size(("grp", "seq"))
    shares = lax.axis_size("mp")
    per_shard = queries.shape[0]
    rows = frames.shape[0]
    capacity = max(2, 5 * rows // (2 * partitions) + 1)
    if shares != 2 or per_shard % 8 or capacity % 16 or partitions * capacity % HEAD:
        return general(
            frames, token_session, ln_gain, w_key, w_value, k_bias, v_bias, queries, cache_key, cache_value,
            cache_start, cache_len,
        )
    swap = [(0, 1), (1, 0)]
    index = lax.axis_index("mp").astype(jnp.int32).reshape(1)
    here = lax.axis_index(("grp", "seq")).astype(jnp.int32).reshape(1)
    own = partial_squares(frames)
    other = lax.ppermute(own, "mp", swap)
    normed, sent_key, kept_key = project_keys(
        index, frames, own, other, ln_gain[None, :], w_key, frames.shape[1] * shares
    )
    got_key = lax.ppermute(sent_key, "mp", swap)
    sent_value, kept_value = project_values(index, normed, w_value)
    got_value = lax.ppermute(sent_value, "mp", swap)
    blocks = pack(
        here, token_session[None, :], kept_key, got_key, kept_value, got_value, k_bias[None, :],
        v_bias[None, :], (partitions, per_shard, capacity),
    )
    got = lax.all_to_all(blocks, ("grp", "seq"), split_axis=0, concat_axis=0, tiled=True)
    scores = cached_scores(cache_start, cache_len, queries, cache_key)
    return attend(got, queries, scores, cache_value, capacity)


def solution(mesh):
    return jax.shard_map(
        local,
        mesh=mesh,
        in_specs=(
            P(("grp", "seq"), "mp"),
            P(("grp", "seq")),
            P("mp"),
            P("mp", None),
            P("mp", None),
            P("mp"),
            P("mp"),
            P(("grp", "seq"), "mp"),
            P(("grp", "seq"), None, "mp"),
            P(("grp", "seq"), None, "mp"),
            P(("grp", "seq")),
            P(("grp", "seq")),
        ),
        out_specs=P(("grp", "seq"), "mp"),
        check_vma=False,
    )
```

```python
import functools

import jax
import jax.numpy as jnp
from jax import lax
from jax.experimental import pallas as pl
from jax.experimental.pallas import tpu as pltpu
from jax.sharding import PartitionSpec as P

HEAD = 128
GROUP = 8

epsilon = 1e-06


def params(mib):
    return pltpu.CompilerParams(vmem_limit_bytes=mib << 20)


def cost(flops, nbytes):
    return pl.CostEstimate(flops=flops, bytes_accessed=nbytes, transcendentals=0)


def nt_dot(a, b):
    return lax.dot_general(a, b, (((1,), (1,)), ((), ())), preferred_element_type=jnp.float32)


def dot(a, b):
    return jnp.dot(a, b, preferred_element_type=jnp.float32)


SMEM = pl.BlockSpec(memory_space=pltpu.SMEM)
VMEM = pl.BlockSpec(memory_space=pltpu.VMEM)
HBM = pl.BlockSpec(memory_space=pltpu.HBM)


def in_hbm(array):
    return pltpu.with_memory_space_constraint(array, pltpu.HBM)


def squares_kernel(frames_ref, out_ref, held_ref, arrived):
    chunks, columns = arrived.shape[0], frames_ref.shape[1]
    wide = columns // chunks
    copies = []
    for chunk in range(chunks):
        part = (slice(None), pl.ds(chunk * wide, wide))
        copies.append(
            pltpu.make_async_copy(frames_ref.at[part], held_ref.at[part], arrived.at[chunk])
        )
        copies[-1].start()
    total = None
    for chunk in range(chunks):
        copies[chunk].wait()
        for at in range(chunk * wide, (chunk + 1) * wide, HEAD):
            part = held_ref[:, at : at + HEAD].astype(jnp.float32)
            part = part * part
            total = part if total is None else total + part
    out_ref[...] = total


def partial_squares(frames):
    rows, columns = frames.shape
    chunks = 2 if columns % (2 * HEAD) == 0 else 1
    return pl.pallas_call(
        squares_kernel,
        out_shape=(jax.ShapeDtypeStruct((rows, HEAD), jnp.float32), jax.ShapeDtypeStruct(frames.shape, frames.dtype)),
        in_specs=[HBM],
        out_specs=(VMEM, VMEM),
        scratch_shapes=[pltpu.SemaphoreType.DMA((chunks,))],
        compiler_params=params(8),
        cost_estimate=cost(2 * rows * columns, 2 * rows * columns),
        name="partial_squares",
    )(in_hbm(frames))


def products(normed_ref, half, key_ref, value_ref, out_ref):
    width = key_ref.shape[1] // 2
    columns = pl.ds(pl.multiple_of(half * width, width), width)
    out_ref[:, :width] = dot(normed_ref[...], key_ref[:, columns])
    out_ref[:, width:] = dot(normed_ref[...], value_ref[:, columns])


def send_kernel(
    features, index_ref, frames_ref, own_ref, other_ref, gain_ref, key_ref, value_ref, normed_ref, out_ref
):
    squares = jnp.sum(own_ref[...] + other_ref[...], axis=1, keepdims=True)
    inverse_rms = lax.rsqrt(squares / features + epsilon)
    normed_ref[...] = (
        frames_ref[...].astype(jnp.float32) * inverse_rms * gain_ref[...]
    ).astype(jnp.bfloat16)
    products(normed_ref, 1 - index_ref[0], key_ref, value_ref, out_ref)


def send_products(index, frames, own, other, gain, key, value, features):
    rows, columns = frames.shape
    width = key.shape[1]
    return pl.pallas_call(
        functools.partial(send_kernel, features),
        out_shape=(
            jax.ShapeDtypeStruct(frames.shape, jnp.bfloat16),
            jax.ShapeDtypeStruct((rows, width), jnp.float32),
        ),
        in_specs=[SMEM] + [VMEM] * 6,
        out_specs=(VMEM, VMEM),
        compiler_params=params(16),
        cost_estimate=cost(2 * rows * columns * width, 2 * key.size),
        name="send_products",
    )(index, frames, own, other, gain, key, value)


def keep_kernel(index_ref, normed_ref, key_ref, value_ref, out_ref):
    products(normed_ref, index_ref[0], key_ref, value_ref, out_ref)


def keep_products(index, normed, key, value):
    rows, columns = normed.shape
    width = key.shape[1]
    return pl.pallas_call(
        keep_kernel,
        out_shape=jax.ShapeDtypeStruct((rows, width), jnp.float32),
        in_specs=[SMEM] + [VMEM] * 3,
        out_specs=VMEM,
        compiler_params=params(16),
        cost_estimate=cost(2 * rows * columns * width, 2 * key.size),
        name="keep_products",
    )(index, normed, key, value)


def route_kernel(
    per_shard,
    capacity,
    here_ref,
    session_ref,
    w_key_ref,
    w_value_ref,
    pick_ref,
    ids_ref,
    held_key_ref,
    held_value_ref,
    held_session,
    arrived,
):
    copies = []
    for at, (source, held) in enumerate(
        ((session_ref, held_session), (w_key_ref, held_key_ref), (w_value_ref, held_value_ref))
    ):
        copies.append(pltpu.make_async_copy(source, held, arrived.at[at]))
        copies[-1].start()
    copies[0].wait()
    slots, rows = pick_ref.shape
    partitions = slots // capacity
    session = held_session[...]
    target = lax.div(session, per_shard)
    local = session - target * per_shard
    to = lax.broadcasted_iota(jnp.int32, (partitions, rows), 0) == target
    to = to.astype(jnp.float32)
    earlier = lax.broadcasted_iota(jnp.int32, (rows, rows), 0) < lax.broadcasted_iota(
        jnp.int32, (rows, rows), 1
    )
    ahead = dot(to.astype(jnp.bfloat16), earlier.astype(jnp.bfloat16))
    order = jnp.sum(to * ahead, axis=0, keepdims=True).astype(jnp.int32)
    place = lax.broadcasted_iota(jnp.int32, (slots, rows), 0)
    pick_ref[...] = (place == target * capacity + order).astype(jnp.bfloat16)
    lane = (place == here_ref[0] * capacity + order).astype(jnp.bfloat16)
    ids = nt_dot((to * (local + 1).astype(jnp.float32)).astype(jnp.bfloat16), lane)
    row = lax.broadcasted_iota(jnp.int32, ids_ref.shape, 1)
    block = jnp.zeros(ids_ref.shape, jnp.float32)
    for j in range(slots // HEAD):
        part = ids[:, j * HEAD : (j + 1) * HEAD]
        block = jnp.where(row == j, part[:, None, :], block)
    ids_ref[...] = block
    for copy in copies[1:]:
        copy.wait()


def route(here, session, w_key, w_value, partitions, per_shard, capacity):
    rows, slots = session.shape[1], partitions * capacity
    id_rows = -(-slots // (8 * HEAD)) * 8
    return pl.pallas_call(
        functools.partial(route_kernel, per_shard, capacity),
        out_shape=(
            jax.ShapeDtypeStruct((slots, rows), jnp.bfloat16),
            jax.ShapeDtypeStruct((partitions, id_rows, HEAD), jnp.float32),
            jax.ShapeDtypeStruct(w_key.shape, w_key.dtype),
            jax.ShapeDtypeStruct(w_value.shape, w_value.dtype),
        ),
        in_specs=[SMEM, HBM, HBM, HBM],
        out_specs=(VMEM, VMEM, VMEM, VMEM),
        scratch_shapes=[pltpu.VMEM(session.shape, session.dtype), pltpu.SemaphoreType.DMA((3,))],
        compiler_params=params(16),
        cost_estimate=cost(4 * rows * rows * slots, 2 * w_key.size),
        name="route",
    )(here, in_hbm(session), in_hbm(w_key), in_hbm(w_value))


def pack_kernel(
    pick_ref,
    ids_ref,
    kept_ref,
    got_ref,
    key_bias_ref,
    value_bias_ref,
    out_ref,
):
    partitions = out_ref.shape[0]
    slots = pick_ref.shape[0]
    capacity = slots // partitions
    width = key_bias_ref.shape[1]
    sums = kept_ref[...] + got_ref[...]
    key = (sums[:, :width] + key_bias_ref[...]).astype(jnp.bfloat16)
    value = (sums[:, width:] + value_bias_ref[...]).astype(jnp.bfloat16)
    at = 0
    for source in (key, value):
        laid = dot(pick_ref[...], source).astype(jnp.bfloat16).reshape(partitions, capacity, width)
        for column in range(0, width, HEAD):
            out_ref[:, at : at + capacity, :] = laid[:, :, column : column + HEAD]
            at += capacity
    out_ref[:, at:, :] = ids_ref[...].astype(jnp.bfloat16)


def pack(pick, ids, kept, got, key_bias, value_bias):
    rows, width = kept.shape
    partitions, id_rows, _ = ids.shape
    capacity = pick.shape[0] // partitions
    block = width // HEAD * capacity + id_rows
    return pl.pallas_call(
        pack_kernel,
        out_shape=jax.ShapeDtypeStruct((partitions, block, HEAD), jnp.bfloat16),
        in_specs=[VMEM] * 6,
        out_specs=VMEM,
        compiler_params=params(8),
        cost_estimate=cost(2 * rows * width * partitions * capacity, 8 * rows * width),
        name="pack",
    )(pick, ids, kept, got, key_bias, value_bias)


def queries_of(queries_ref, head):
    columns = [
        queries_ref[:, at * HEAD : (at + 1) * HEAD].astype(jnp.float32)
        for at in range(head * GROUP, (head + 1) * GROUP)
    ]
    return jnp.concatenate(columns, axis=0).astype(jnp.bfloat16)


def cached_kernel(start_ref, len_ref, queries_ref, key_ref, out_ref, laid_ref):
    heads, rows, window = out_ref.shape
    sessions = queries_ref.shape[0]
    row_session = lax.broadcasted_iota(jnp.int32, (rows, window), 0) % sessions
    slot = lax.broadcasted_iota(jnp.int32, (rows, window), 1)
    live = []
    for session in range(sessions):
        since = slot - start_ref[session]
        since = jnp.where(since < 0, since + window, since)
        live.append(since < len_ref[session])
    for head in range(heads):
        query = queries_of(queries_ref, head)
        laid_ref[head] = query
        total = jnp.full((rows, window), -jnp.inf, jnp.float32)
        for session in range(sessions):
            key = key_ref[session, :, head * HEAD : (head + 1) * HEAD]
            score = nt_dot(query, key) * (HEAD**-0.5)
            total = jnp.where((row_session == session) & live[session], score, total)
        out_ref[head] = total


def cached_scores(start, length, queries, cache_key):
    sessions, window, width = cache_key.shape
    heads = width // HEAD
    return pl.pallas_call(
        cached_kernel,
        out_shape=(
            jax.ShapeDtypeStruct((heads, GROUP * sessions, window), jnp.float32),
            jax.ShapeDtypeStruct((heads, GROUP * sessions, HEAD), jnp.bfloat16),
        ),
        in_specs=[SMEM, SMEM, VMEM, VMEM],
        out_specs=(VMEM, VMEM),
        compiler_params=params(8),
        cost_estimate=cost(2 * GROUP * sessions * cache_key.size, 2 * cache_key.size),
        name="cached_scores",
    )(start, length, queries, cache_key)


def attend_kernel(capacity, got_ref, queries_ref, score_ref, cache_ref, out_ref):
    heads, rows, window = score_ref.shape
    sessions = cache_ref.shape[0]
    partitions = got_ref.shape[0]
    slots = partitions * capacity
    at = 2 * heads * capacity
    ids = jnp.concatenate(
        [
            jnp.sum(got_ref[:, at + j : at + j + 1, :].astype(jnp.float32), axis=0)
            for j in range(slots // HEAD)
        ],
        axis=1,
    ).astype(jnp.int32)
    own = lax.broadcasted_iota(jnp.int32, (rows, slots), 0) % sessions + 1 == ids
    row_session = lax.broadcasted_iota(jnp.int32, (rows, window), 0) % sessions
    for head in range(heads):
        query = queries_ref[head]
        key = got_ref[:, head * capacity : (head + 1) * capacity, :].reshape(slots, HEAD)
        first = (heads + head) * capacity
        value = got_ref[:, first : first + capacity, :].reshape(slots, HEAD)
        cached = score_ref[head]
        fresh = jnp.where(own, nt_dot(query, key) * (HEAD**-0.5), -jnp.inf)
        largest = jnp.maximum(
            jnp.max(cached, axis=1, keepdims=True), jnp.max(fresh, axis=1, keepdims=True)
        )
        cached = jnp.exp(cached - largest)
        fresh = jnp.exp(fresh - largest)
        total = jnp.sum(cached, axis=1, keepdims=True) + jnp.sum(fresh, axis=1, keepdims=True)
        cached = cached / total
        attended = dot((fresh / total).astype(jnp.bfloat16), value)
        for session in range(sessions):
            weights = jnp.where(row_session == session, cached, 0.0).astype(jnp.bfloat16)
            attended += dot(weights, cache_ref[session, :, head * HEAD : (head + 1) * HEAD])
        for q in range(GROUP):
            column = (head * GROUP + q) * HEAD
            out_ref[:, column : column + HEAD] = attended[
                q * sessions : (q + 1) * sessions
            ].astype(jnp.bfloat16)


def attend(got, queries, scores, cache_value, capacity):
    return pl.pallas_call(
        functools.partial(attend_kernel, capacity),
        out_shape=jax.ShapeDtypeStruct(
            (cache_value.shape[0], queries.shape[0] * GROUP * HEAD), jnp.bfloat16
        ),
        in_specs=[VMEM] * 4,
        out_specs=VMEM,
        compiler_params=params(8),
        cost_estimate=cost(4 * queries.shape[1] * cache_value.size, 2 * cache_value.size),
        name="attend",
    )(got, queries, scores, cache_value)


def project(frame_rows, ln_gain, w_key, w_value, k_bias, v_bias):
    values32 = frame_rows.astype(jnp.float32)
    partial_squares = jnp.sum(values32 * values32, axis=1)
    squares = lax.psum(partial_squares, "mp")
    inverse_rms = lax.rsqrt(squares / (frame_rows.shape[1] * lax.axis_size("mp")) + epsilon)
    normed = (values32 * inverse_rms[:, None] * ln_gain[None, :]).astype(jnp.bfloat16)
    part_key = jnp.dot(normed, w_key, preferred_element_type=jnp.float32)
    part_value = jnp.dot(normed, w_value, preferred_element_type=jnp.float32)
    key_sums, value_sums = (
        lax.psum_scatter(part_key, "mp", scatter_dimension=1, tiled=True),
        lax.psum_scatter(part_value, "mp", scatter_dimension=1, tiled=True),
    )
    new_keys = (key_sums + k_bias[None, :]).astype(jnp.bfloat16)
    new_values = (value_sums + v_bias[None, :]).astype(jnp.bfloat16)
    return (new_keys, new_values)


def slot_sources(token_session, per_shard, partition_count, capacity):
    row_count = token_session.shape[0]
    target = token_session // per_shard
    one_hot = (target[:, None] == jnp.arange(partition_count, dtype=jnp.int32)[None, :]).astype(
        jnp.int32
    )
    order_in = jnp.sum((jnp.cumsum(one_hot, axis=0) - one_hot) * one_hot, axis=1)
    slot_index = target * capacity + order_in
    matches = (
        slot_index[None, :] == jnp.arange(partition_count * capacity, dtype=jnp.int32)[:, None]
    )
    source = jnp.sum(jnp.where(matches, jnp.arange(row_count, dtype=jnp.int32)[None, :], 0), axis=1)
    filled = jnp.any(matches, axis=1)
    sessions = jnp.where(filled, jnp.mod(token_session[source], per_shard), -1)
    return (source, filled, sessions)


def general(
    frames,
    token_session,
    ln_gain,
    w_key,
    w_value,
    k_bias,
    v_bias,
    queries,
    cache_key,
    cache_value,
    cache_start,
    cache_len,
):
    partition_count = lax.axis_size(("grp", "seq"))
    per_shard = queries.shape[0]
    rows_here = frames.shape[0]
    capacity = max(2, 5 * rows_here // (2 * partition_count) + 1)
    source, filled, sessions = slot_sources(token_session, per_shard, partition_count, capacity)
    session_slots = sessions.reshape(partition_count, capacity)
    nothing = jnp.zeros((), jnp.bfloat16)
    own_keys, own_values = project(frames, ln_gain, w_key, w_value, k_bias, v_bias)
    send_keys = jnp.where(filled[:, None], own_keys[source], nothing).reshape(
        partition_count, capacity, -1
    )
    send_values = jnp.where(filled[:, None], own_values[source], nothing).reshape(
        partition_count, capacity, -1
    )
    got_keys, got_values, got_sessions = (
        lax.all_to_all(send_keys, ("grp", "seq"), split_axis=0, concat_axis=0, tiled=True),
        lax.all_to_all(send_values, ("grp", "seq"), split_axis=0, concat_axis=0, tiled=True),
        lax.all_to_all(session_slots, ("grp", "seq"), split_axis=0, concat_axis=0, tiled=True),
    )
    new_keys = got_keys.reshape(partition_count * capacity, -1)
    new_values = got_values.reshape(partition_count * capacity, -1)
    new_sessions = got_sessions.reshape(-1)
    heads_kv = new_keys.shape[1] // HEAD
    window = cache_key.shape[1]
    score_scale = HEAD ** (-0.5)
    query_heads = queries.reshape(per_shard, heads_kv, GROUP, HEAD)
    cached_keys = cache_key.reshape(per_shard, window, heads_kv, HEAD)
    cached_values = cache_value.reshape(per_shard, window, heads_kv, HEAD)
    fresh_keys = new_keys.reshape(-1, heads_kv, HEAD)
    fresh_values = new_values.reshape(-1, heads_kv, HEAD)
    cached_scores = (
        jnp.einsum("sghd,swgd->sghw", query_heads, cached_keys, preferred_element_type=jnp.float32)
        * score_scale
    )
    positions = jnp.arange(window, dtype=jnp.int32)
    live_slots = jnp.mod(positions[None, :] - cache_start[:, None], window) < cache_len[:, None]
    cached_scores = jnp.where(live_slots[:, None, None, :], cached_scores, -jnp.inf)
    fresh_scores = (
        jnp.einsum("sghd,ngd->sghn", query_heads, fresh_keys, preferred_element_type=jnp.float32)
        * score_scale
    )
    own_rows = new_sessions[None, :] == jnp.arange(per_shard, dtype=jnp.int32)[:, None]
    fresh_scores = jnp.where(own_rows[:, None, None, :], fresh_scores, -jnp.inf)
    largest = jnp.maximum(jnp.max(cached_scores, axis=3), jnp.max(fresh_scores, axis=3))
    cached_exp = jnp.exp(cached_scores - largest[..., None])
    fresh_exp = jnp.exp(fresh_scores - largest[..., None])
    totals = jnp.sum(cached_exp, axis=3) + jnp.sum(fresh_exp, axis=3)
    cached_weights = (cached_exp / totals[..., None]).astype(jnp.bfloat16)
    fresh_weights = (fresh_exp / totals[..., None]).astype(jnp.bfloat16)
    attended = jnp.einsum(
        "sghw,swgd->sghd", cached_weights, cached_values, preferred_element_type=jnp.float32
    )
    attended = attended + jnp.einsum(
        "sghn,ngd->sghd", fresh_weights, fresh_values, preferred_element_type=jnp.float32
    )
    return attended.reshape(per_shard, -1).astype(jnp.bfloat16)


def local(
    frames,
    token_session,
    ln_gain,
    w_key,
    w_value,
    k_bias,
    v_bias,
    queries,
    cache_key,
    cache_value,
    cache_start,
    cache_len,
):
    partitions = lax.axis_size(("grp", "seq"))
    shares = lax.axis_size("mp")
    per_shard = queries.shape[0]
    rows = frames.shape[0]
    capacity = max(2, 5 * rows // (2 * partitions) + 1)
    if shares != 2 or per_shard % 8 or capacity % 16 or partitions * capacity % HEAD:
        return general(
            frames, token_session, ln_gain, w_key, w_value, k_bias, v_bias, queries, cache_key, cache_value,
            cache_start, cache_len,
        )
    swap = [(0, 1), (1, 0)]
    index = lax.axis_index("mp").astype(jnp.int32).reshape(1)
    here = lax.axis_index(("grp", "seq")).astype(jnp.int32).reshape(1)
    own, held = partial_squares(frames)
    other = lax.ppermute(own, "mp", swap)
    pick, ids, held_key, held_value = route(
        here, token_session[None, :], w_key, w_value, partitions, per_shard, capacity
    )
    normed, sent = send_products(
        index, held, own, other, ln_gain[None, :], held_key, held_value, frames.shape[1] * shares
    )
    arrived = lax.ppermute(sent, "mp", swap)
    kept = keep_products(index, normed, held_key, held_value)
    blocks = pack(pick, ids, kept, arrived, k_bias[None, :], v_bias[None, :])
    got = lax.all_to_all(blocks, ("grp", "seq"), split_axis=0, concat_axis=0, tiled=True)
    scores, laid = cached_scores(cache_start, cache_len, queries, cache_key)
    return attend(got, laid, scores, cache_value, capacity)


def solution(mesh):
    return jax.shard_map(
        local,
        mesh=mesh,
        in_specs=(
            P(("grp", "seq"), "mp"),
            P(("grp", "seq")),
            P("mp"),
            P("mp", None),
            P("mp", None),
            P("mp"),
            P("mp"),
            P(("grp", "seq"), "mp"),
            P(("grp", "seq"), None, "mp"),
            P(("grp", "seq"), None, "mp"),
            P(("grp", "seq")),
            P(("grp", "seq")),
        ),
        out_specs=P(("grp", "seq"), "mp"),
        check_vma=False,
    )
```

```python
import functools

import jax
import jax.numpy as jnp
from jax import lax
from jax.experimental import pallas as pl
from jax.experimental.pallas import tpu as pltpu
from jax.sharding import PartitionSpec as P

HEAD = 128
GROUP = 8

epsilon = 1e-06


def params(mib):
    return pltpu.CompilerParams(vmem_limit_bytes=mib << 20)


def cost(flops, nbytes):
    return pl.CostEstimate(flops=flops, bytes_accessed=nbytes, transcendentals=0)


def nt_dot(a, b):
    return lax.dot_general(a, b, (((1,), (1,)), ((), ())), preferred_element_type=jnp.float32)


def dot(a, b):
    return jnp.dot(a, b, preferred_element_type=jnp.float32)


SMEM = pl.BlockSpec(memory_space=pltpu.SMEM)
VMEM = pl.BlockSpec(memory_space=pltpu.VMEM)
HBM = pl.BlockSpec(memory_space=pltpu.HBM)


def in_hbm(array):
    return pltpu.with_memory_space_constraint(array, pltpu.HBM)


def squares_kernel(frames_ref, out_ref, held_ref, arrived):
    chunks, columns = arrived.shape[0], frames_ref.shape[1]
    wide = columns // chunks
    copies = []
    for chunk in range(chunks):
        part = (slice(None), pl.ds(chunk * wide, wide))
        copies.append(
            pltpu.make_async_copy(frames_ref.at[part], held_ref.at[part], arrived.at[chunk])
        )
        copies[-1].start()
    total = None
    for chunk in range(chunks):
        copies[chunk].wait()
        for at in range(chunk * wide, (chunk + 1) * wide, HEAD):
            part = held_ref[:, at : at + HEAD].astype(jnp.float32)
            part = part * part
            total = part if total is None else total + part
    out_ref[...] = total


def partial_squares(frames):
    rows, columns = frames.shape
    chunks = 2 if columns % (2 * HEAD) == 0 else 1
    return pl.pallas_call(
        squares_kernel,
        out_shape=(jax.ShapeDtypeStruct((rows, HEAD), jnp.float32), jax.ShapeDtypeStruct(frames.shape, frames.dtype)),
        in_specs=[HBM],
        out_specs=(VMEM, VMEM),
        scratch_shapes=[pltpu.SemaphoreType.DMA((chunks,))],
        compiler_params=params(8),
        cost_estimate=cost(2 * rows * columns, 2 * rows * columns),
        name="partial_squares",
    )(in_hbm(frames))


def products(normed_ref, half, key_ref, value_ref, out_ref):
    width = key_ref.shape[1] // 2
    columns = pl.ds(pl.multiple_of(half * width, width), width)
    out_ref[:, :width] = dot(normed_ref[...], key_ref[:, columns])
    out_ref[:, width:] = dot(normed_ref[...], value_ref[:, columns])


def send_kernel(
    features, index_ref, frames_ref, own_ref, other_ref, gain_ref, key_ref, value_ref, normed_ref, out_ref
):
    squares = jnp.sum(own_ref[...] + other_ref[...], axis=1, keepdims=True)
    inverse_rms = lax.rsqrt(squares / features + epsilon)
    normed_ref[...] = (
        frames_ref[...].astype(jnp.float32) * inverse_rms * gain_ref[...]
    ).astype(jnp.bfloat16)
    products(normed_ref, 1 - index_ref[0], key_ref, value_ref, out_ref)


def send_products(index, frames, own, other, gain, key, value, features):
    rows, columns = frames.shape
    width = key.shape[1]
    return pl.pallas_call(
        functools.partial(send_kernel, features),
        out_shape=(
            jax.ShapeDtypeStruct(frames.shape, jnp.bfloat16),
            jax.ShapeDtypeStruct((rows, width), jnp.float32),
        ),
        in_specs=[SMEM] + [VMEM] * 6,
        out_specs=(VMEM, VMEM),
        compiler_params=params(16),
        cost_estimate=cost(2 * rows * columns * width, 2 * key.size),
        name="send_products",
    )(index, frames, own, other, gain, key, value)


def keep_kernel(index_ref, normed_ref, key_ref, value_ref, out_ref):
    products(normed_ref, index_ref[0], key_ref, value_ref, out_ref)


def keep_products(index, normed, key, value):
    rows, columns = normed.shape
    width = key.shape[1]
    return pl.pallas_call(
        keep_kernel,
        out_shape=jax.ShapeDtypeStruct((rows, width), jnp.float32),
        in_specs=[SMEM] + [VMEM] * 3,
        out_specs=VMEM,
        compiler_params=params(16),
        cost_estimate=cost(2 * rows * columns * width, 2 * key.size),
        name="keep_products",
    )(index, normed, key, value)


def route_kernel(
    per_shard,
    capacity,
    here_ref,
    session_ref,
    w_key_ref,
    w_value_ref,
    pick_ref,
    ids_ref,
    held_key_ref,
    held_value_ref,
    held_session,
    arrived,
):
    copies = []
    for at, (source, held) in enumerate(
        ((session_ref, held_session), (w_key_ref, held_key_ref), (w_value_ref, held_value_ref))
    ):
        copies.append(pltpu.make_async_copy(source, held, arrived.at[at]))
        copies[-1].start()
    copies[0].wait()
    slots, rows = pick_ref.shape
    partitions = slots // capacity
    session = held_session[...]
    target = lax.div(session, per_shard)
    local = session - target * per_shard
    to = lax.broadcasted_iota(jnp.int32, (partitions, rows), 0) == target
    to = to.astype(jnp.float32)
    earlier = lax.broadcasted_iota(jnp.int32, (rows, rows), 0) < lax.broadcasted_iota(
        jnp.int32, (rows, rows), 1
    )
    ahead = dot(to.astype(jnp.bfloat16), earlier.astype(jnp.bfloat16))
    order = jnp.sum(to * ahead, axis=0, keepdims=True).astype(jnp.int32)
    place = lax.broadcasted_iota(jnp.int32, (slots, rows), 0)
    pick_ref[...] = (place == target * capacity + order).astype(jnp.bfloat16)
    lane = (place == here_ref[0] * capacity + order).astype(jnp.bfloat16)
    ids = nt_dot((to * (local + 1).astype(jnp.float32)).astype(jnp.bfloat16), lane)
    row = lax.broadcasted_iota(jnp.int32, ids_ref.shape, 1)
    block = jnp.zeros(ids_ref.shape, jnp.float32)
    for j in range(slots // HEAD):
        part = ids[:, j * HEAD : (j + 1) * HEAD]
        block = jnp.where(row == j, part[:, None, :], block)
    ids_ref[...] = block
    for copy in copies[1:]:
        copy.wait()


def route(here, session, w_key, w_value, partitions, per_shard, capacity):
    rows, slots = session.shape[1], partitions * capacity
    id_rows = -(-slots // (8 * HEAD)) * 8
    return pl.pallas_call(
        functools.partial(route_kernel, per_shard, capacity),
        out_shape=(
            jax.ShapeDtypeStruct((slots, rows), jnp.bfloat16),
            jax.ShapeDtypeStruct((partitions, id_rows, HEAD), jnp.float32),
            jax.ShapeDtypeStruct(w_key.shape, w_key.dtype),
            jax.ShapeDtypeStruct(w_value.shape, w_value.dtype),
        ),
        in_specs=[SMEM, HBM, HBM, HBM],
        out_specs=(VMEM, VMEM, VMEM, VMEM),
        scratch_shapes=[pltpu.VMEM(session.shape, session.dtype), pltpu.SemaphoreType.DMA((3,))],
        compiler_params=params(16),
        cost_estimate=cost(4 * rows * rows * slots, 2 * w_key.size),
        name="route",
    )(here, in_hbm(session), in_hbm(w_key), in_hbm(w_value))


def pack_kernel(
    pick_ref,
    ids_ref,
    kept_ref,
    got_ref,
    key_bias_ref,
    value_bias_ref,
    out_ref,
):
    partitions = out_ref.shape[0]
    slots = pick_ref.shape[0]
    capacity = slots // partitions
    width = key_bias_ref.shape[1]
    sums = kept_ref[...] + got_ref[...]
    key = (sums[:, :width] + key_bias_ref[...]).astype(jnp.bfloat16)
    value = (sums[:, width:] + value_bias_ref[...]).astype(jnp.bfloat16)
    at = 0
    for source in (key, value):
        laid = dot(pick_ref[...], source).astype(jnp.bfloat16).reshape(partitions, capacity, width)
        for column in range(0, width, HEAD):
            part = laid[:, :, column : column + HEAD]
            out_ref[:, at : at + capacity // 2] = part.reshape(partitions, capacity // 2, 2, HEAD)
            at += capacity // 2
    out_ref[:, at] = ids_ref[:, :2, :].astype(jnp.bfloat16)


def pack(pick, ids, kept, got, key_bias, value_bias):
    rows, width = kept.shape
    partitions, id_rows, _ = ids.shape
    capacity = pick.shape[0] // partitions
    block = width // HEAD * capacity // 2 + 1
    return pl.pallas_call(
        pack_kernel,
        out_shape=jax.ShapeDtypeStruct((partitions, block, 2, HEAD), jnp.bfloat16),
        in_specs=[VMEM] * 6,
        out_specs=VMEM,
        compiler_params=params(8),
        cost_estimate=cost(2 * rows * width * partitions * capacity, 8 * rows * width),
        name="pack",
    )(pick, ids, kept, got, key_bias, value_bias)


def queries_of(queries_ref, head):
    columns = [
        queries_ref[:, at * HEAD : (at + 1) * HEAD].astype(jnp.float32)
        for at in range(head * GROUP, (head + 1) * GROUP)
    ]
    return jnp.concatenate(columns, axis=0).astype(jnp.bfloat16)


def cached_kernel(start_ref, len_ref, queries_ref, key_ref, out_ref, laid_ref):
    heads, rows, window = out_ref.shape
    sessions = queries_ref.shape[0]
    row_session = lax.broadcasted_iota(jnp.int32, (rows, window), 0) % sessions
    slot = lax.broadcasted_iota(jnp.int32, (rows, window), 1)
    live = []
    for session in range(sessions):
        since = slot - start_ref[session]
        since = jnp.where(since < 0, since + window, since)
        live.append(since < len_ref[session])
    for head in range(heads):
        query = queries_of(queries_ref, head)
        laid_ref[head] = query
        total = jnp.full((rows, window), -jnp.inf, jnp.float32)
        for session in range(sessions):
            key = key_ref[session, :, head * HEAD : (head + 1) * HEAD]
            score = nt_dot(query, key) * (HEAD**-0.5)
            total = jnp.where((row_session == session) & live[session], score, total)
        out_ref[head] = total


def cached_scores(start, length, queries, cache_key):
    sessions, window, width = cache_key.shape
    heads = width // HEAD
    return pl.pallas_call(
        cached_kernel,
        out_shape=(
            jax.ShapeDtypeStruct((heads, GROUP * sessions, window), jnp.float32),
            jax.ShapeDtypeStruct((heads, GROUP * sessions, HEAD), jnp.bfloat16),
        ),
        in_specs=[SMEM, SMEM, VMEM, VMEM],
        out_specs=(VMEM, VMEM),
        compiler_params=params(8),
        cost_estimate=cost(2 * GROUP * sessions * cache_key.size, 2 * cache_key.size),
        name="cached_scores",
    )(start, length, queries, cache_key)


def attend_kernel(capacity, got_ref, queries_ref, score_ref, cache_ref, out_ref):
    heads, rows, window = score_ref.shape
    sessions = cache_ref.shape[0]
    partitions = got_ref.shape[0]
    slots = partitions * capacity
    at = heads * capacity
    ids = jnp.concatenate(
        [
            jnp.sum(got_ref[:, at, j : j + 1, :].astype(jnp.float32), axis=0)
            for j in range(slots // HEAD)
        ],
        axis=1,
    ).astype(jnp.int32)
    own = lax.broadcasted_iota(jnp.int32, (rows, slots), 0) % sessions + 1 == ids
    row_session = lax.broadcasted_iota(jnp.int32, (rows, window), 0) % sessions
    for head in range(heads):
        query = queries_ref[head]
        key = got_ref[:, head * capacity // 2 : (head + 1) * capacity // 2].reshape(slots, HEAD)
        first = (heads + head) * capacity // 2
        value = got_ref[:, first : first + capacity // 2].reshape(slots, HEAD)
        cached = score_ref[head]
        fresh = jnp.where(own, nt_dot(query, key) * (HEAD**-0.5), -jnp.inf)
        largest = jnp.maximum(
            jnp.max(cached, axis=1, keepdims=True), jnp.max(fresh, axis=1, keepdims=True)
        )
        cached = jnp.exp(cached - largest)
        fresh = jnp.exp(fresh - largest)
        total = jnp.sum(cached, axis=1, keepdims=True) + jnp.sum(fresh, axis=1, keepdims=True)
        cached = cached / total
        attended = dot((fresh / total).astype(jnp.bfloat16), value)
        for session in range(sessions):
            weights = jnp.where(row_session == session, cached, 0.0).astype(jnp.bfloat16)
            attended += dot(weights, cache_ref[session, :, head * HEAD : (head + 1) * HEAD])
        for q in range(GROUP):
            column = (head * GROUP + q) * HEAD
            out_ref[:, column : column + HEAD] = attended[
                q * sessions : (q + 1) * sessions
            ].astype(jnp.bfloat16)


def attend(got, queries, scores, cache_value, capacity):
    return pl.pallas_call(
        functools.partial(attend_kernel, capacity),
        out_shape=jax.ShapeDtypeStruct(
            (cache_value.shape[0], queries.shape[0] * GROUP * HEAD), jnp.bfloat16
        ),
        in_specs=[VMEM] * 4,
        out_specs=VMEM,
        compiler_params=params(8),
        cost_estimate=cost(4 * queries.shape[1] * cache_value.size, 2 * cache_value.size),
        name="attend",
    )(got, queries, scores, cache_value)


def project(frame_rows, ln_gain, w_key, w_value, k_bias, v_bias):
    values32 = frame_rows.astype(jnp.float32)
    partial_squares = jnp.sum(values32 * values32, axis=1)
    squares = lax.psum(partial_squares, "mp")
    inverse_rms = lax.rsqrt(squares / (frame_rows.shape[1] * lax.axis_size("mp")) + epsilon)
    normed = (values32 * inverse_rms[:, None] * ln_gain[None, :]).astype(jnp.bfloat16)
    part_key = jnp.dot(normed, w_key, preferred_element_type=jnp.float32)
    part_value = jnp.dot(normed, w_value, preferred_element_type=jnp.float32)
    key_sums, value_sums = (
        lax.psum_scatter(part_key, "mp", scatter_dimension=1, tiled=True),
        lax.psum_scatter(part_value, "mp", scatter_dimension=1, tiled=True),
    )
    new_keys = (key_sums + k_bias[None, :]).astype(jnp.bfloat16)
    new_values = (value_sums + v_bias[None, :]).astype(jnp.bfloat16)
    return (new_keys, new_values)


def slot_sources(token_session, per_shard, partition_count, capacity):
    row_count = token_session.shape[0]
    target = token_session // per_shard
    one_hot = (target[:, None] == jnp.arange(partition_count, dtype=jnp.int32)[None, :]).astype(
        jnp.int32
    )
    order_in = jnp.sum((jnp.cumsum(one_hot, axis=0) - one_hot) * one_hot, axis=1)
    slot_index = target * capacity + order_in
    matches = (
        slot_index[None, :] == jnp.arange(partition_count * capacity, dtype=jnp.int32)[:, None]
    )
    source = jnp.sum(jnp.where(matches, jnp.arange(row_count, dtype=jnp.int32)[None, :], 0), axis=1)
    filled = jnp.any(matches, axis=1)
    sessions = jnp.where(filled, jnp.mod(token_session[source], per_shard), -1)
    return (source, filled, sessions)


def general(
    frames,
    token_session,
    ln_gain,
    w_key,
    w_value,
    k_bias,
    v_bias,
    queries,
    cache_key,
    cache_value,
    cache_start,
    cache_len,
):
    partition_count = lax.axis_size(("grp", "seq"))
    per_shard = queries.shape[0]
    rows_here = frames.shape[0]
    capacity = max(2, 5 * rows_here // (2 * partition_count) + 1)
    source, filled, sessions = slot_sources(token_session, per_shard, partition_count, capacity)
    session_slots = sessions.reshape(partition_count, capacity)
    nothing = jnp.zeros((), jnp.bfloat16)
    own_keys, own_values = project(frames, ln_gain, w_key, w_value, k_bias, v_bias)
    send_keys = jnp.where(filled[:, None], own_keys[source], nothing).reshape(
        partition_count, capacity, -1
    )
    send_values = jnp.where(filled[:, None], own_values[source], nothing).reshape(
        partition_count, capacity, -1
    )
    got_keys, got_values, got_sessions = (
        lax.all_to_all(send_keys, ("grp", "seq"), split_axis=0, concat_axis=0, tiled=True),
        lax.all_to_all(send_values, ("grp", "seq"), split_axis=0, concat_axis=0, tiled=True),
        lax.all_to_all(session_slots, ("grp", "seq"), split_axis=0, concat_axis=0, tiled=True),
    )
    new_keys = got_keys.reshape(partition_count * capacity, -1)
    new_values = got_values.reshape(partition_count * capacity, -1)
    new_sessions = got_sessions.reshape(-1)
    heads_kv = new_keys.shape[1] // HEAD
    window = cache_key.shape[1]
    score_scale = HEAD ** (-0.5)
    query_heads = queries.reshape(per_shard, heads_kv, GROUP, HEAD)
    cached_keys = cache_key.reshape(per_shard, window, heads_kv, HEAD)
    cached_values = cache_value.reshape(per_shard, window, heads_kv, HEAD)
    fresh_keys = new_keys.reshape(-1, heads_kv, HEAD)
    fresh_values = new_values.reshape(-1, heads_kv, HEAD)
    cached_scores = (
        jnp.einsum("sghd,swgd->sghw", query_heads, cached_keys, preferred_element_type=jnp.float32)
        * score_scale
    )
    positions = jnp.arange(window, dtype=jnp.int32)
    live_slots = jnp.mod(positions[None, :] - cache_start[:, None], window) < cache_len[:, None]
    cached_scores = jnp.where(live_slots[:, None, None, :], cached_scores, -jnp.inf)
    fresh_scores = (
        jnp.einsum("sghd,ngd->sghn", query_heads, fresh_keys, preferred_element_type=jnp.float32)
        * score_scale
    )
    own_rows = new_sessions[None, :] == jnp.arange(per_shard, dtype=jnp.int32)[:, None]
    fresh_scores = jnp.where(own_rows[:, None, None, :], fresh_scores, -jnp.inf)
    largest = jnp.maximum(jnp.max(cached_scores, axis=3), jnp.max(fresh_scores, axis=3))
    cached_exp = jnp.exp(cached_scores - largest[..., None])
    fresh_exp = jnp.exp(fresh_scores - largest[..., None])
    totals = jnp.sum(cached_exp, axis=3) + jnp.sum(fresh_exp, axis=3)
    cached_weights = (cached_exp / totals[..., None]).astype(jnp.bfloat16)
    fresh_weights = (fresh_exp / totals[..., None]).astype(jnp.bfloat16)
    attended = jnp.einsum(
        "sghw,swgd->sghd", cached_weights, cached_values, preferred_element_type=jnp.float32
    )
    attended = attended + jnp.einsum(
        "sghn,ngd->sghd", fresh_weights, fresh_values, preferred_element_type=jnp.float32
    )
    return attended.reshape(per_shard, -1).astype(jnp.bfloat16)


def local(
    frames,
    token_session,
    ln_gain,
    w_key,
    w_value,
    k_bias,
    v_bias,
    queries,
    cache_key,
    cache_value,
    cache_start,
    cache_len,
):
    partitions = lax.axis_size(("grp", "seq"))
    shares = lax.axis_size("mp")
    per_shard = queries.shape[0]
    rows = frames.shape[0]
    capacity = max(2, 5 * rows // (2 * partitions) + 1)
    if shares != 2 or per_shard % 8 or capacity % 16 or partitions * capacity % HEAD:
        return general(
            frames, token_session, ln_gain, w_key, w_value, k_bias, v_bias, queries, cache_key, cache_value,
            cache_start, cache_len,
        )
    swap = [(0, 1), (1, 0)]
    index = lax.axis_index("mp").astype(jnp.int32).reshape(1)
    here = lax.axis_index(("grp", "seq")).astype(jnp.int32).reshape(1)
    own, held = partial_squares(frames)
    other = lax.ppermute(own, "mp", swap)
    pick, ids, held_key, held_value = route(
        here, token_session[None, :], w_key, w_value, partitions, per_shard, capacity
    )
    normed, sent = send_products(
        index, held, own, other, ln_gain[None, :], held_key, held_value, frames.shape[1] * shares
    )
    arrived = lax.ppermute(sent, "mp", swap)
    kept = keep_products(index, normed, held_key, held_value)
    blocks = pack(pick, ids, kept, arrived, k_bias[None, :], v_bias[None, :])
    got = lax.all_to_all(blocks, ("grp", "seq"), split_axis=0, concat_axis=0, tiled=True)
    scores, laid = cached_scores(cache_start, cache_len, queries, cache_key)
    return attend(got, laid, scores, cache_value, capacity)


def solution(mesh):
    return jax.shard_map(
        local,
        mesh=mesh,
        in_specs=(
            P(("grp", "seq"), "mp"),
            P(("grp", "seq")),
            P("mp"),
            P("mp", None),
            P("mp", None),
            P("mp"),
            P("mp"),
            P(("grp", "seq"), "mp"),
            P(("grp", "seq"), None, "mp"),
            P(("grp", "seq"), None, "mp"),
            P(("grp", "seq")),
            P(("grp", "seq")),
        ),
        out_specs=P(("grp", "seq"), "mp"),
        check_vma=False,
    )
```

```python
import functools

import jax
import jax.numpy as jnp
from jax import lax
from jax.experimental import pallas as pl
from jax.experimental.pallas import tpu as pltpu
from jax.sharding import PartitionSpec as P

HEAD = 128
GROUP = 8

epsilon = 1e-06


def params(mib):
    return pltpu.CompilerParams(vmem_limit_bytes=mib << 20)


def cost(flops, nbytes):
    return pl.CostEstimate(flops=flops, bytes_accessed=nbytes, transcendentals=0)


def nt_dot(a, b):
    return lax.dot_general(a, b, (((1,), (1,)), ((), ())), preferred_element_type=jnp.float32)


def dot(a, b):
    return jnp.dot(a, b, preferred_element_type=jnp.float32)


SMEM = pl.BlockSpec(memory_space=pltpu.SMEM)
VMEM = pl.BlockSpec(memory_space=pltpu.VMEM)
HBM = pl.BlockSpec(memory_space=pltpu.HBM)


def in_hbm(array):
    return pltpu.with_memory_space_constraint(array, pltpu.HBM)


def squares_kernel(frames_ref, out_ref, held_ref, arrived):
    chunks, columns = arrived.shape[0], frames_ref.shape[1]
    wide = columns // chunks
    copies = []
    for chunk in range(chunks):
        part = (slice(None), pl.ds(chunk * wide, wide))
        copies.append(
            pltpu.make_async_copy(frames_ref.at[part], held_ref.at[part], arrived.at[chunk])
        )
        copies[-1].start()
    total = None
    for chunk in range(chunks):
        copies[chunk].wait()
        for at in range(chunk * wide, (chunk + 1) * wide, HEAD):
            part = held_ref[:, at : at + HEAD].astype(jnp.float32)
            part = part * part
            total = part if total is None else total + part
    out_ref[...] = total


def partial_squares(frames):
    rows, columns = frames.shape
    chunks = 2 if columns % (2 * HEAD) == 0 else 1
    return pl.pallas_call(
        squares_kernel,
        out_shape=(jax.ShapeDtypeStruct((rows, HEAD), jnp.float32), jax.ShapeDtypeStruct(frames.shape, frames.dtype)),
        in_specs=[HBM],
        out_specs=(VMEM, VMEM),
        scratch_shapes=[pltpu.SemaphoreType.DMA((chunks,))],
        compiler_params=params(8),
        cost_estimate=cost(2 * rows * columns, 2 * rows * columns),
        name="partial_squares",
    )(in_hbm(frames))


def products(normed_ref, half, key_ref, value_ref, out_ref):
    width = key_ref.shape[1] // 2
    columns = pl.ds(pl.multiple_of(half * width, width), width)
    out_ref[:, :width] = dot(normed_ref[...], key_ref[:, columns])
    out_ref[:, width:] = dot(normed_ref[...], value_ref[:, columns])


def send_kernel(
    features, index_ref, frames_ref, own_ref, other_ref, gain_ref, key_ref, value_ref, normed_ref, out_ref
):
    squares = jnp.sum(own_ref[...] + other_ref[...], axis=1, keepdims=True)
    inverse_rms = lax.rsqrt(squares / features + epsilon)
    normed_ref[...] = (
        frames_ref[...].astype(jnp.float32) * inverse_rms * gain_ref[...]
    ).astype(jnp.bfloat16)
    products(normed_ref, 1 - index_ref[0], key_ref, value_ref, out_ref)


def send_products(index, frames, own, other, gain, key, value, features):
    rows, columns = frames.shape
    width = key.shape[1]
    return pl.pallas_call(
        functools.partial(send_kernel, features),
        out_shape=(
            jax.ShapeDtypeStruct(frames.shape, jnp.bfloat16),
            jax.ShapeDtypeStruct((rows, width), jnp.float32),
        ),
        in_specs=[SMEM] + [VMEM] * 6,
        out_specs=(VMEM, VMEM),
        compiler_params=params(16),
        cost_estimate=cost(2 * rows * columns * width, 2 * key.size),
        name="send_products",
    )(index, frames, own, other, gain, key, value)


def keep_kernel(index_ref, normed_ref, key_ref, value_ref, out_ref):
    products(normed_ref, index_ref[0], key_ref, value_ref, out_ref)


def keep_products(index, normed, key, value):
    rows, columns = normed.shape
    width = key.shape[1]
    return pl.pallas_call(
        keep_kernel,
        out_shape=jax.ShapeDtypeStruct((rows, width), jnp.float32),
        in_specs=[SMEM] + [VMEM] * 3,
        out_specs=VMEM,
        compiler_params=params(16),
        cost_estimate=cost(2 * rows * columns * width, 2 * key.size),
        name="keep_products",
    )(index, normed, key, value)


def route(per_shard, capacity, here, session, pick_ref, ids_ref):
    slots, rows = pick_ref.shape
    partitions = slots // capacity
    target = lax.div(session, per_shard)
    local = session - target * per_shard
    to = lax.broadcasted_iota(jnp.int32, (partitions, rows), 0) == target
    to = to.astype(jnp.float32)
    earlier = lax.broadcasted_iota(jnp.int32, (rows, rows), 0) < lax.broadcasted_iota(
        jnp.int32, (rows, rows), 1
    )
    ahead = dot(to.astype(jnp.bfloat16), earlier.astype(jnp.bfloat16))
    order = jnp.sum(to * ahead, axis=0, keepdims=True).astype(jnp.int32)
    place = lax.broadcasted_iota(jnp.int32, (slots, rows), 0)
    pick_ref[...] = (place == target * capacity + order).astype(jnp.bfloat16)
    lane = (place == here * capacity + order).astype(jnp.bfloat16)
    ids = nt_dot((to * (local + 1).astype(jnp.float32)).astype(jnp.bfloat16), lane)
    row = lax.broadcasted_iota(jnp.int32, ids_ref.shape, 1)
    block = jnp.zeros(ids_ref.shape, jnp.float32)
    for j in range(slots // HEAD):
        part = ids[:, j * HEAD : (j + 1) * HEAD]
        block = jnp.where(row == j, part[:, None, :], block)
    ids_ref[...] = block


def queries_of(queries_ref, head):
    columns = [
        queries_ref[:, at * HEAD : (at + 1) * HEAD].astype(jnp.float32)
        for at in range(head * GROUP, (head + 1) * GROUP)
    ]
    return jnp.concatenate(columns, axis=0).astype(jnp.bfloat16)


def score_cache(start_ref, len_ref, queries_ref, key_ref, out_ref, laid_ref):
    heads, rows, window = out_ref.shape
    sessions = queries_ref.shape[0]

    def by_row(ref):
        mine = lax.broadcasted_iota(jnp.int32, (rows, sessions), 0) % sessions
        mine = mine == lax.broadcasted_iota(jnp.int32, (rows, sessions), 1)
        values = jnp.where(mine, ref[...].astype(jnp.float32), 0.0)
        return jnp.sum(values, axis=1, keepdims=True).astype(jnp.int32)

    since = lax.broadcasted_iota(jnp.int32, (rows, window), 1) - by_row(start_ref)
    since = jnp.where(since < 0, since + window, since)
    live = since < by_row(len_ref)
    row_session = lax.broadcasted_iota(jnp.int32, (rows, window), 0) % sessions
    for head in range(heads):
        query = queries_of(queries_ref, head)
        laid_ref[head] = query
        total = jnp.zeros((rows, window), jnp.float32)
        for session in range(sessions):
            key = key_ref[session, :, head * HEAD : (head + 1) * HEAD]
            total = jnp.where(row_session == session, nt_dot(query, key), total)
        out_ref[head] = jnp.where(live, total * (HEAD**-0.5), -jnp.inf)


def beside_kernel(
    per_shard,
    capacity,
    here_ref,
    session_ref,
    start_ref,
    len_ref,
    queries_ref,
    cache_ref,
    w_key_ref,
    w_value_ref,
    held_key_ref,
    held_value_ref,
    pick_ref,
    ids_ref,
    score_ref,
    laid_ref,
    session,
    start,
    length,
    queries,
    cache,
    arrived,
):
    copies = []
    for at, (source, held) in enumerate(
        (
            (session_ref, session),
            (start_ref, start),
            (len_ref, length),
            (queries_ref, queries),
            (cache_ref, cache),
            (w_key_ref, held_key_ref),
            (w_value_ref, held_value_ref),
        )
    ):
        copies.append(pltpu.make_async_copy(source, held, arrived.at[at]))
        copies[-1].start()
    copies[0].wait()
    route(per_shard, capacity, here_ref[0], session[...], pick_ref, ids_ref)
    for copy in copies[1:5]:
        copy.wait()
    score_cache(start, length, queries, cache, score_ref, laid_ref)
    for copy in copies[5:]:
        copy.wait()


def beside(here, session, start, length, queries, cache_key, w_key, w_value, sizes):
    partitions, per_shard, capacity = sizes
    slots, rows = partitions * capacity, session.shape[1]
    sessions, window, width = cache_key.shape
    heads = width // HEAD
    id_rows = -(-slots // (8 * HEAD)) * 8
    copied = (session, start, length, queries, cache_key)
    return pl.pallas_call(
        functools.partial(beside_kernel, per_shard, capacity),
        out_shape=(
            jax.ShapeDtypeStruct(w_key.shape, w_key.dtype),
            jax.ShapeDtypeStruct(w_value.shape, w_value.dtype),
            jax.ShapeDtypeStruct((slots, rows), jnp.bfloat16),
            jax.ShapeDtypeStruct((partitions, id_rows, HEAD), jnp.float32),
            jax.ShapeDtypeStruct((heads, GROUP * sessions, window), jnp.float32),
            jax.ShapeDtypeStruct((heads, GROUP * sessions, HEAD), jnp.bfloat16),
        ),
        in_specs=[SMEM] + [HBM] * 7,
        out_specs=(VMEM,) * 6,
        scratch_shapes=[pltpu.VMEM(array.shape, array.dtype) for array in copied]
        + [pltpu.SemaphoreType.DMA((7,))],
        compiler_params=params(24),
        cost_estimate=cost(2 * GROUP * sessions * cache_key.size, 4 * w_key.size),
        name="beside",
    )(here, *map(in_hbm, copied), in_hbm(w_key), in_hbm(w_value))


def pack_kernel(
    pick_ref,
    ids_ref,
    kept_ref,
    got_ref,
    key_bias_ref,
    value_bias_ref,
    out_ref,
):
    partitions = out_ref.shape[0]
    slots = pick_ref.shape[0]
    capacity = slots // partitions
    width = key_bias_ref.shape[1]
    sums = kept_ref[...] + got_ref[...]
    key = (sums[:, :width] + key_bias_ref[...]).astype(jnp.bfloat16)
    value = (sums[:, width:] + value_bias_ref[...]).astype(jnp.bfloat16)
    at = 0
    for source in (key, value):
        laid = dot(pick_ref[...], source).astype(jnp.bfloat16).reshape(partitions, capacity, width)
        for column in range(0, width, HEAD):
            part = laid[:, :, column : column + HEAD]
            out_ref[:, at : at + capacity // 2] = part.reshape(partitions, capacity // 2, 2, HEAD)
            at += capacity // 2
    out_ref[:, at] = ids_ref[:, :2, :].astype(jnp.bfloat16)


def pack(pick, ids, kept, got, key_bias, value_bias):
    rows, width = kept.shape
    partitions, id_rows, _ = ids.shape
    capacity = pick.shape[0] // partitions
    block = width // HEAD * capacity // 2 + 1
    return pl.pallas_call(
        pack_kernel,
        out_shape=jax.ShapeDtypeStruct((partitions, block, 2, HEAD), jnp.bfloat16),
        in_specs=[VMEM] * 6,
        out_specs=VMEM,
        compiler_params=params(8),
        cost_estimate=cost(2 * rows * width * partitions * capacity, 8 * rows * width),
        name="pack",
    )(pick, ids, kept, got, key_bias, value_bias)


def attend_kernel(capacity, got_ref, queries_ref, score_ref, cache_ref, out_ref):
    heads, rows, window = score_ref.shape
    sessions = cache_ref.shape[0]
    partitions = got_ref.shape[0]
    slots = partitions * capacity
    at = heads * capacity
    ids = jnp.concatenate(
        [
            jnp.sum(got_ref[:, at, j : j + 1, :].astype(jnp.float32), axis=0)
            for j in range(slots // HEAD)
        ],
        axis=1,
    ).astype(jnp.int32)
    own = lax.broadcasted_iota(jnp.int32, (rows, slots), 0) % sessions + 1 == ids
    row_session = lax.broadcasted_iota(jnp.int32, (rows, window), 0) % sessions
    for head in range(heads):
        query = queries_ref[head]
        key = got_ref[:, head * capacity // 2 : (head + 1) * capacity // 2].reshape(slots, HEAD)
        first = (heads + head) * capacity // 2
        value = got_ref[:, first : first + capacity // 2].reshape(slots, HEAD)
        cached = score_ref[head]
        fresh = jnp.where(own, nt_dot(query, key) * (HEAD**-0.5), -jnp.inf)
        largest = jnp.maximum(
            jnp.max(cached, axis=1, keepdims=True), jnp.max(fresh, axis=1, keepdims=True)
        )
        cached = jnp.exp(cached - largest)
        fresh = jnp.exp(fresh - largest)
        total = jnp.sum(cached, axis=1, keepdims=True) + jnp.sum(fresh, axis=1, keepdims=True)
        cached = cached / total
        attended = dot((fresh / total).astype(jnp.bfloat16), value)
        for session in range(sessions):
            weights = jnp.where(row_session == session, cached, 0.0).astype(jnp.bfloat16)
            attended += dot(weights, cache_ref[session, :, head * HEAD : (head + 1) * HEAD])
        for q in range(GROUP):
            column = (head * GROUP + q) * HEAD
            out_ref[:, column : column + HEAD] = attended[
                q * sessions : (q + 1) * sessions
            ].astype(jnp.bfloat16)


def attend(got, queries, scores, cache_value, capacity):
    return pl.pallas_call(
        functools.partial(attend_kernel, capacity),
        out_shape=jax.ShapeDtypeStruct(
            (cache_value.shape[0], queries.shape[0] * GROUP * HEAD), jnp.bfloat16
        ),
        in_specs=[VMEM] * 4,
        out_specs=VMEM,
        compiler_params=params(8),
        cost_estimate=cost(4 * queries.shape[1] * cache_value.size, 2 * cache_value.size),
        name="attend",
    )(got, queries, scores, cache_value)


def project(frame_rows, ln_gain, w_key, w_value, k_bias, v_bias):
    values32 = frame_rows.astype(jnp.float32)
    partial_squares = jnp.sum(values32 * values32, axis=1)
    squares = lax.psum(partial_squares, "mp")
    inverse_rms = lax.rsqrt(squares / (frame_rows.shape[1] * lax.axis_size("mp")) + epsilon)
    normed = (values32 * inverse_rms[:, None] * ln_gain[None, :]).astype(jnp.bfloat16)
    part_key = jnp.dot(normed, w_key, preferred_element_type=jnp.float32)
    part_value = jnp.dot(normed, w_value, preferred_element_type=jnp.float32)
    key_sums, value_sums = (
        lax.psum_scatter(part_key, "mp", scatter_dimension=1, tiled=True),
        lax.psum_scatter(part_value, "mp", scatter_dimension=1, tiled=True),
    )
    new_keys = (key_sums + k_bias[None, :]).astype(jnp.bfloat16)
    new_values = (value_sums + v_bias[None, :]).astype(jnp.bfloat16)
    return (new_keys, new_values)


def slot_sources(token_session, per_shard, partition_count, capacity):
    row_count = token_session.shape[0]
    target = token_session // per_shard
    one_hot = (target[:, None] == jnp.arange(partition_count, dtype=jnp.int32)[None, :]).astype(
        jnp.int32
    )
    order_in = jnp.sum((jnp.cumsum(one_hot, axis=0) - one_hot) * one_hot, axis=1)
    slot_index = target * capacity + order_in
    matches = (
        slot_index[None, :] == jnp.arange(partition_count * capacity, dtype=jnp.int32)[:, None]
    )
    source = jnp.sum(jnp.where(matches, jnp.arange(row_count, dtype=jnp.int32)[None, :], 0), axis=1)
    filled = jnp.any(matches, axis=1)
    sessions = jnp.where(filled, jnp.mod(token_session[source], per_shard), -1)
    return (source, filled, sessions)


def general(
    frames,
    token_session,
    ln_gain,
    w_key,
    w_value,
    k_bias,
    v_bias,
    queries,
    cache_key,
    cache_value,
    cache_start,
    cache_len,
):
    partition_count = lax.axis_size(("grp", "seq"))
    per_shard = queries.shape[0]
    rows_here = frames.shape[0]
    capacity = max(2, 5 * rows_here // (2 * partition_count) + 1)
    source, filled, sessions = slot_sources(token_session, per_shard, partition_count, capacity)
    session_slots = sessions.reshape(partition_count, capacity)
    nothing = jnp.zeros((), jnp.bfloat16)
    own_keys, own_values = project(frames, ln_gain, w_key, w_value, k_bias, v_bias)
    send_keys = jnp.where(filled[:, None], own_keys[source], nothing).reshape(
        partition_count, capacity, -1
    )
    send_values = jnp.where(filled[:, None], own_values[source], nothing).reshape(
        partition_count, capacity, -1
    )
    got_keys, got_values, got_sessions = (
        lax.all_to_all(send_keys, ("grp", "seq"), split_axis=0, concat_axis=0, tiled=True),
        lax.all_to_all(send_values, ("grp", "seq"), split_axis=0, concat_axis=0, tiled=True),
        lax.all_to_all(session_slots, ("grp", "seq"), split_axis=0, concat_axis=0, tiled=True),
    )
    new_keys = got_keys.reshape(partition_count * capacity, -1)
    new_values = got_values.reshape(partition_count * capacity, -1)
    new_sessions = got_sessions.reshape(-1)
    heads_kv = new_keys.shape[1] // HEAD
    window = cache_key.shape[1]
    score_scale = HEAD ** (-0.5)
    query_heads = queries.reshape(per_shard, heads_kv, GROUP, HEAD)
    cached_keys = cache_key.reshape(per_shard, window, heads_kv, HEAD)
    cached_values = cache_value.reshape(per_shard, window, heads_kv, HEAD)
    fresh_keys = new_keys.reshape(-1, heads_kv, HEAD)
    fresh_values = new_values.reshape(-1, heads_kv, HEAD)
    cached_scores = (
        jnp.einsum("sghd,swgd->sghw", query_heads, cached_keys, preferred_element_type=jnp.float32)
        * score_scale
    )
    positions = jnp.arange(window, dtype=jnp.int32)
    live_slots = jnp.mod(positions[None, :] - cache_start[:, None], window) < cache_len[:, None]
    cached_scores = jnp.where(live_slots[:, None, None, :], cached_scores, -jnp.inf)
    fresh_scores = (
        jnp.einsum("sghd,ngd->sghn", query_heads, fresh_keys, preferred_element_type=jnp.float32)
        * score_scale
    )
    own_rows = new_sessions[None, :] == jnp.arange(per_shard, dtype=jnp.int32)[:, None]
    fresh_scores = jnp.where(own_rows[:, None, None, :], fresh_scores, -jnp.inf)
    largest = jnp.maximum(jnp.max(cached_scores, axis=3), jnp.max(fresh_scores, axis=3))
    cached_exp = jnp.exp(cached_scores - largest[..., None])
    fresh_exp = jnp.exp(fresh_scores - largest[..., None])
    totals = jnp.sum(cached_exp, axis=3) + jnp.sum(fresh_exp, axis=3)
    cached_weights = (cached_exp / totals[..., None]).astype(jnp.bfloat16)
    fresh_weights = (fresh_exp / totals[..., None]).astype(jnp.bfloat16)
    attended = jnp.einsum(
        "sghw,swgd->sghd", cached_weights, cached_values, preferred_element_type=jnp.float32
    )
    attended = attended + jnp.einsum(
        "sghn,ngd->sghd", fresh_weights, fresh_values, preferred_element_type=jnp.float32
    )
    return attended.reshape(per_shard, -1).astype(jnp.bfloat16)


def local(
    frames,
    token_session,
    ln_gain,
    w_key,
    w_value,
    k_bias,
    v_bias,
    queries,
    cache_key,
    cache_value,
    cache_start,
    cache_len,
):
    partitions = lax.axis_size(("grp", "seq"))
    shares = lax.axis_size("mp")
    per_shard = queries.shape[0]
    rows = frames.shape[0]
    capacity = max(2, 5 * rows // (2 * partitions) + 1)
    if shares != 2 or per_shard % 8 or capacity % 16 or partitions * capacity % HEAD:
        return general(
            frames, token_session, ln_gain, w_key, w_value, k_bias, v_bias, queries, cache_key, cache_value,
            cache_start, cache_len,
        )
    swap = [(0, 1), (1, 0)]
    index = lax.axis_index("mp").astype(jnp.int32).reshape(1)
    here = lax.axis_index(("grp", "seq")).astype(jnp.int32).reshape(1)
    own, held = partial_squares(frames)
    other = lax.ppermute(own, "mp", swap)
    held_key, held_value, pick, ids, scores, laid = beside(
        here, token_session[None, :], cache_start[None, :], cache_len[None, :], queries, cache_key, w_key,
        w_value, (partitions, per_shard, capacity),
    )
    normed, sent = send_products(
        index, held, own, other, ln_gain[None, :], held_key, held_value, frames.shape[1] * shares
    )
    arrived = lax.ppermute(sent, "mp", swap)
    kept = keep_products(index, normed, held_key, held_value)
    blocks = pack(pick, ids, kept, arrived, k_bias[None, :], v_bias[None, :])
    got = lax.all_to_all(blocks, ("grp", "seq"), split_axis=0, concat_axis=0, tiled=True)
    return attend(got, laid, scores, cache_value, capacity)


def solution(mesh):
    return jax.shard_map(
        local,
        mesh=mesh,
        in_specs=(
            P(("grp", "seq"), "mp"),
            P(("grp", "seq")),
            P("mp"),
            P("mp", None),
            P("mp", None),
            P("mp"),
            P("mp"),
            P(("grp", "seq"), "mp"),
            P(("grp", "seq"), None, "mp"),
            P(("grp", "seq"), None, "mp"),
            P(("grp", "seq")),
            P(("grp", "seq")),
        ),
        out_specs=P(("grp", "seq"), "mp"),
        check_vma=False,
    )
```

```python
import functools

import jax
import jax.numpy as jnp
from jax import lax
from jax.experimental import pallas as pl
from jax.experimental.pallas import tpu as pltpu
from jax.sharding import PartitionSpec as P

HEAD = 128
GROUP = 8

epsilon = 1e-06


def params(mib):
    return pltpu.CompilerParams(vmem_limit_bytes=mib << 20)


def cost(flops, nbytes):
    return pl.CostEstimate(flops=flops, bytes_accessed=nbytes, transcendentals=0)


def nt_dot(a, b):
    return lax.dot_general(a, b, (((1,), (1,)), ((), ())), preferred_element_type=jnp.float32)


def dot(a, b):
    return jnp.dot(a, b, preferred_element_type=jnp.float32)


SMEM = pl.BlockSpec(memory_space=pltpu.SMEM)
VMEM = pl.BlockSpec(memory_space=pltpu.VMEM)
HBM = pl.BlockSpec(memory_space=pltpu.HBM)


def in_hbm(array):
    return pltpu.with_memory_space_constraint(array, pltpu.HBM)


def squares_kernel(frames_ref, out_ref, held_ref, arrived):
    chunks, columns = arrived.shape[0], frames_ref.shape[1]
    wide = columns // chunks
    copies = []
    for chunk in range(chunks):
        part = (slice(None), pl.ds(chunk * wide, wide))
        copies.append(
            pltpu.make_async_copy(frames_ref.at[part], held_ref.at[part], arrived.at[chunk])
        )
        copies[-1].start()
    total = None
    for chunk in range(chunks):
        copies[chunk].wait()
        for at in range(chunk * wide, (chunk + 1) * wide, HEAD):
            part = held_ref[:, at : at + HEAD].astype(jnp.float32)
            part = part * part
            total = part if total is None else total + part
    out_ref[...] = total


def partial_squares(frames):
    rows, columns = frames.shape
    chunks = 2 if columns % (2 * HEAD) == 0 else 1
    return pl.pallas_call(
        squares_kernel,
        out_shape=(jax.ShapeDtypeStruct((rows, HEAD), jnp.float32), jax.ShapeDtypeStruct(frames.shape, frames.dtype)),
        in_specs=[HBM],
        out_specs=(VMEM, VMEM),
        scratch_shapes=[pltpu.SemaphoreType.DMA((chunks,))],
        compiler_params=params(8),
        cost_estimate=cost(2 * rows * columns, 2 * rows * columns),
        name="partial_squares",
    )(in_hbm(frames))


def products(normed_ref, half, key_ref, value_ref, out_ref):
    width = key_ref.shape[1] // 2
    columns = pl.ds(pl.multiple_of(half * width, width), width)
    out_ref[:, :width] = dot(normed_ref[...], key_ref[:, columns])
    out_ref[:, width:] = dot(normed_ref[...], value_ref[:, columns])


def send_kernel(
    features, index_ref, frames_ref, own_ref, other_ref, gain_ref, key_ref, value_ref, normed_ref, out_ref
):
    squares = jnp.sum(own_ref[...] + other_ref[...], axis=1, keepdims=True)
    inverse_rms = lax.rsqrt(squares / features + epsilon)
    normed_ref[...] = (
        frames_ref[...].astype(jnp.float32) * inverse_rms * gain_ref[...]
    ).astype(jnp.bfloat16)
    products(normed_ref, 1 - index_ref[0], key_ref, value_ref, out_ref)


def send_products(index, frames, own, other, gain, key, value, features):
    rows, columns = frames.shape
    width = key.shape[1]
    return pl.pallas_call(
        functools.partial(send_kernel, features),
        out_shape=(
            jax.ShapeDtypeStruct(frames.shape, jnp.bfloat16),
            jax.ShapeDtypeStruct((rows, width), jnp.float32),
        ),
        in_specs=[SMEM] + [VMEM] * 6,
        out_specs=(VMEM, VMEM),
        compiler_params=params(16),
        cost_estimate=cost(2 * rows * columns * width, 2 * key.size),
        name="send_products",
    )(index, frames, own, other, gain, key, value)


def keep_kernel(index_ref, normed_ref, key_ref, value_ref, out_ref):
    products(normed_ref, index_ref[0], key_ref, value_ref, out_ref)


def keep_products(index, normed, key, value):
    rows, columns = normed.shape
    width = key.shape[1]
    return pl.pallas_call(
        keep_kernel,
        out_shape=jax.ShapeDtypeStruct((rows, width), jnp.float32),
        in_specs=[SMEM] + [VMEM] * 3,
        out_specs=VMEM,
        compiler_params=params(16),
        cost_estimate=cost(2 * rows * columns * width, 2 * key.size),
        name="keep_products",
    )(index, normed, key, value)


def max_bits(masks):
    return functools.reduce(lambda a, b: a | b, masks)


def stage_masks(groups, members):
    if groups & (groups - 1) or members & (members - 1) or members < 4:
        return None
    near = sorted((g * members + m for g in range(groups) for m in range(2)), reverse=True)
    far = sorted(range(0, members, 2), reverse=True)
    return tuple(tuple([0] + masks[:-1]) for masks in (near, far))


def route(per_shard, capacity, stages, here, session, pick_ref, ids_ref):
    slots, rows = pick_ref.shape
    partitions = slots // capacity
    near, far = stages
    target = lax.div(session, per_shard)
    local = session - target * per_shard
    apart = target ^ here
    step = [
        sum(jnp.where((apart & max_bits(masks)) == mask, at, 0) for at, mask in enumerate(masks))
        for masks in stages
    ]
    leaves = step[0] * len(far) + step[1]
    lands = step[1] * len(near) + step[0]
    to = lax.broadcasted_iota(jnp.int32, (partitions, rows), 0) == leaves
    to = to.astype(jnp.float32)
    earlier = lax.broadcasted_iota(jnp.int32, (rows, rows), 0) < lax.broadcasted_iota(
        jnp.int32, (rows, rows), 1
    )
    ahead = dot(to.astype(jnp.bfloat16), earlier.astype(jnp.bfloat16))
    order = jnp.sum(to * ahead, axis=0, keepdims=True).astype(jnp.int32)
    place = lax.broadcasted_iota(jnp.int32, (slots, rows), 0)
    pick_ref[...] = (place == leaves * capacity + order).astype(jnp.bfloat16)
    lane = (place == lands * capacity + order).astype(jnp.bfloat16)
    ids = nt_dot((to * (local + 1).astype(jnp.float32)).astype(jnp.bfloat16), lane)
    row = lax.broadcasted_iota(jnp.int32, ids_ref.shape, 1)
    block = jnp.zeros(ids_ref.shape, jnp.float32)
    for j in range(slots // HEAD):
        part = ids[:, j * HEAD : (j + 1) * HEAD]
        block = jnp.where(row == j, part[:, None, :], block)
    ids_ref[...] = block


def queries_of(queries_ref, head):
    columns = [
        queries_ref[:, at * HEAD : (at + 1) * HEAD].astype(jnp.float32)
        for at in range(head * GROUP, (head + 1) * GROUP)
    ]
    return jnp.concatenate(columns, axis=0).astype(jnp.bfloat16)


def score_cache(start_ref, len_ref, queries_ref, key_ref, out_ref, laid_ref):
    heads, rows, window = out_ref.shape
    sessions = queries_ref.shape[0]

    def by_row(ref):
        mine = lax.broadcasted_iota(jnp.int32, (rows, sessions), 0) % sessions
        mine = mine == lax.broadcasted_iota(jnp.int32, (rows, sessions), 1)
        values = jnp.where(mine, ref[...].astype(jnp.float32), 0.0)
        return jnp.sum(values, axis=1, keepdims=True).astype(jnp.int32)

    since = lax.broadcasted_iota(jnp.int32, (rows, window), 1) - by_row(start_ref)
    since = jnp.where(since < 0, since + window, since)
    live = since < by_row(len_ref)
    row_session = lax.broadcasted_iota(jnp.int32, (rows, window), 0) % sessions
    for head in range(heads):
        query = queries_of(queries_ref, head)
        laid_ref[head] = query
        total = jnp.zeros((rows, window), jnp.float32)
        for session in range(sessions):
            key = key_ref[session, :, head * HEAD : (head + 1) * HEAD]
            total = jnp.where(row_session == session, nt_dot(query, key), total)
        out_ref[head] = jnp.where(live, total * (HEAD**-0.5), -jnp.inf)


def beside_kernel(
    per_shard,
    capacity,
    stages,
    here_ref,
    session_ref,
    start_ref,
    len_ref,
    queries_ref,
    cache_ref,
    w_key_ref,
    w_value_ref,
    held_key_ref,
    held_value_ref,
    pick_ref,
    ids_ref,
    score_ref,
    laid_ref,
    session,
    start,
    length,
    queries,
    cache,
    arrived,
):
    copies = []
    for at, (source, held) in enumerate(
        (
            (session_ref, session),
            (start_ref, start),
            (len_ref, length),
            (queries_ref, queries),
            (cache_ref, cache),
            (w_key_ref, held_key_ref),
            (w_value_ref, held_value_ref),
        )
    ):
        copies.append(pltpu.make_async_copy(source, held, arrived.at[at]))
        copies[-1].start()
    copies[0].wait()
    route(per_shard, capacity, stages, here_ref[0], session[...], pick_ref, ids_ref)
    for copy in copies[1:5]:
        copy.wait()
    score_cache(start, length, queries, cache, score_ref, laid_ref)
    for copy in copies[5:]:
        copy.wait()


def beside(here, session, start, length, queries, cache_key, w_key, w_value, sizes):
    partitions, per_shard, capacity, stages = sizes
    slots, rows = partitions * capacity, session.shape[1]
    sessions, window, width = cache_key.shape
    heads = width // HEAD
    id_rows = -(-slots // (8 * HEAD)) * 8
    copied = (session, start, length, queries, cache_key)
    return pl.pallas_call(
        functools.partial(beside_kernel, per_shard, capacity, stages),
        out_shape=(
            jax.ShapeDtypeStruct(w_key.shape, w_key.dtype),
            jax.ShapeDtypeStruct(w_value.shape, w_value.dtype),
            jax.ShapeDtypeStruct((slots, rows), jnp.bfloat16),
            jax.ShapeDtypeStruct((partitions, id_rows, HEAD), jnp.float32),
            jax.ShapeDtypeStruct((heads, GROUP * sessions, window), jnp.float32),
            jax.ShapeDtypeStruct((heads, GROUP * sessions, HEAD), jnp.bfloat16),
        ),
        in_specs=[SMEM] + [HBM] * 7,
        out_specs=(VMEM,) * 6,
        scratch_shapes=[pltpu.VMEM(array.shape, array.dtype) for array in copied]
        + [pltpu.SemaphoreType.DMA((7,))],
        compiler_params=params(24),
        cost_estimate=cost(2 * GROUP * sessions * cache_key.size, 4 * w_key.size),
        name="beside",
    )(here, *map(in_hbm, copied), in_hbm(w_key), in_hbm(w_value))


def pack_kernel(
    pick_ref,
    ids_ref,
    kept_ref,
    got_ref,
    key_bias_ref,
    value_bias_ref,
    *out_refs,
):
    partitions = ids_ref.shape[0]
    far = partitions // len(out_refs)
    slots = pick_ref.shape[0]
    capacity = slots // partitions
    width = key_bias_ref.shape[1]
    sums = kept_ref[...] + got_ref[...]
    key = (sums[:, :width] + key_bias_ref[...]).astype(jnp.bfloat16)
    value = (sums[:, width:] + value_bias_ref[...]).astype(jnp.bfloat16)
    at = 0
    for source in (key, value):
        laid = dot(pick_ref[...], source).astype(jnp.bfloat16).reshape(partitions, capacity, width)
        for column in range(0, width, HEAD):
            part = laid[:, :, column : column + HEAD]
            part = part.reshape(partitions, capacity // 2, 2, HEAD)
            for step, out_ref in enumerate(out_refs):
                out_ref[:, at : at + capacity // 2] = part[step * far : (step + 1) * far]
            at += capacity // 2
    for step, out_ref in enumerate(out_refs):
        out_ref[:, at] = ids_ref[step * far : (step + 1) * far, :2, :].astype(jnp.bfloat16)


def pack(pick, ids, kept, got, key_bias, value_bias, near):
    rows, width = kept.shape
    partitions, id_rows, _ = ids.shape
    capacity = pick.shape[0] // partitions
    block = width // HEAD * capacity // 2 + 1
    return pl.pallas_call(
        pack_kernel,
        out_shape=[jax.ShapeDtypeStruct((partitions // near, block, 2, HEAD), jnp.bfloat16)] * near,
        in_specs=[VMEM] * 6,
        out_specs=[VMEM] * near,
        compiler_params=params(8),
        cost_estimate=cost(2 * rows * width * partitions * capacity, 8 * rows * width),
        name="pack",
    )(pick, ids, kept, got, key_bias, value_bias)


def regroup_kernel(*refs):
    far = refs[0].shape[0]
    got_refs, out_refs = refs[:-far], refs[-far:]
    for step, out_ref in enumerate(out_refs):
        for near, got_ref in enumerate(got_refs):
            out_ref[near] = got_ref[step]


def regroup(blocks):
    far, *block = blocks[0].shape
    return pl.pallas_call(
        regroup_kernel,
        out_shape=[jax.ShapeDtypeStruct((len(blocks), *block), jnp.bfloat16)] * far,
        in_specs=[VMEM] * len(blocks),
        out_specs=[VMEM] * far,
        compiler_params=params(8),
        cost_estimate=cost(0, 4 * len(blocks) * blocks[0].size),
        name="regroup",
    )(*blocks)


def attend_kernel(capacity, queries_ref, score_ref, cache_ref, *refs):
    *got_refs, out_ref = refs
    heads, rows, window = score_ref.shape
    sessions = cache_ref.shape[0]
    partitions = len(got_refs) * got_refs[0].shape[0]
    slots = partitions * capacity
    at = heads * capacity
    ids = jnp.concatenate(
        [
            sum(jnp.sum(ref[:, at, j : j + 1, :].astype(jnp.float32), axis=0) for ref in got_refs)
            for j in range(slots // HEAD)
        ],
        axis=1,
    ).astype(jnp.int32)
    own = lax.broadcasted_iota(jnp.int32, (rows, slots), 0) % sessions + 1 == ids

    def rows_of(vector):
        part = slice(vector * capacity // 2, (vector + 1) * capacity // 2)
        return jnp.concatenate([ref[:, part].reshape(-1, HEAD) for ref in got_refs], axis=0)

    row_session = lax.broadcasted_iota(jnp.int32, (rows, window), 0) % sessions
    for head in range(heads):
        query = queries_ref[head]
        key, value = rows_of(head), rows_of(heads + head)
        cached = score_ref[head]
        fresh = jnp.where(own, nt_dot(query, key) * (HEAD**-0.5), -jnp.inf)
        largest = jnp.maximum(
            jnp.max(cached, axis=1, keepdims=True), jnp.max(fresh, axis=1, keepdims=True)
        )
        cached = jnp.exp(cached - largest)
        fresh = jnp.exp(fresh - largest)
        total = jnp.sum(cached, axis=1, keepdims=True) + jnp.sum(fresh, axis=1, keepdims=True)
        cached = cached / total
        attended = dot((fresh / total).astype(jnp.bfloat16), value)
        for session in range(sessions):
            weights = jnp.where(row_session == session, cached, 0.0).astype(jnp.bfloat16)
            attended += dot(weights, cache_ref[session, :, head * HEAD : (head + 1) * HEAD])
        for q in range(GROUP):
            column = (head * GROUP + q) * HEAD
            out_ref[:, column : column + HEAD] = attended[
                q * sessions : (q + 1) * sessions
            ].astype(jnp.bfloat16)


def attend(got, queries, scores, cache_value, capacity):
    return pl.pallas_call(
        functools.partial(attend_kernel, capacity),
        out_shape=jax.ShapeDtypeStruct(
            (cache_value.shape[0], queries.shape[0] * GROUP * HEAD), jnp.bfloat16
        ),
        in_specs=[VMEM] * (3 + len(got)),
        out_specs=VMEM,
        compiler_params=params(8),
        cost_estimate=cost(4 * queries.shape[1] * cache_value.size, 2 * cache_value.size),
        name="attend",
    )(queries, scores, cache_value, *got)


def project(frame_rows, ln_gain, w_key, w_value, k_bias, v_bias):
    values32 = frame_rows.astype(jnp.float32)
    partial_squares = jnp.sum(values32 * values32, axis=1)
    squares = lax.psum(partial_squares, "mp")
    inverse_rms = lax.rsqrt(squares / (frame_rows.shape[1] * lax.axis_size("mp")) + epsilon)
    normed = (values32 * inverse_rms[:, None] * ln_gain[None, :]).astype(jnp.bfloat16)
    part_key = jnp.dot(normed, w_key, preferred_element_type=jnp.float32)
    part_value = jnp.dot(normed, w_value, preferred_element_type=jnp.float32)
    key_sums, value_sums = (
        lax.psum_scatter(part_key, "mp", scatter_dimension=1, tiled=True),
        lax.psum_scatter(part_value, "mp", scatter_dimension=1, tiled=True),
    )
    new_keys = (key_sums + k_bias[None, :]).astype(jnp.bfloat16)
    new_values = (value_sums + v_bias[None, :]).astype(jnp.bfloat16)
    return (new_keys, new_values)


def slot_sources(token_session, per_shard, partition_count, capacity):
    row_count = token_session.shape[0]
    target = token_session // per_shard
    one_hot = (target[:, None] == jnp.arange(partition_count, dtype=jnp.int32)[None, :]).astype(
        jnp.int32
    )
    order_in = jnp.sum((jnp.cumsum(one_hot, axis=0) - one_hot) * one_hot, axis=1)
    slot_index = target * capacity + order_in
    matches = (
        slot_index[None, :] == jnp.arange(partition_count * capacity, dtype=jnp.int32)[:, None]
    )
    source = jnp.sum(jnp.where(matches, jnp.arange(row_count, dtype=jnp.int32)[None, :], 0), axis=1)
    filled = jnp.any(matches, axis=1)
    sessions = jnp.where(filled, jnp.mod(token_session[source], per_shard), -1)
    return (source, filled, sessions)


def general(
    frames,
    token_session,
    ln_gain,
    w_key,
    w_value,
    k_bias,
    v_bias,
    queries,
    cache_key,
    cache_value,
    cache_start,
    cache_len,
):
    partition_count = lax.axis_size(("grp", "seq"))
    per_shard = queries.shape[0]
    rows_here = frames.shape[0]
    capacity = max(2, 5 * rows_here // (2 * partition_count) + 1)
    source, filled, sessions = slot_sources(token_session, per_shard, partition_count, capacity)
    session_slots = sessions.reshape(partition_count, capacity)
    nothing = jnp.zeros((), jnp.bfloat16)
    own_keys, own_values = project(frames, ln_gain, w_key, w_value, k_bias, v_bias)
    send_keys = jnp.where(filled[:, None], own_keys[source], nothing).reshape(
        partition_count, capacity, -1
    )
    send_values = jnp.where(filled[:, None], own_values[source], nothing).reshape(
        partition_count, capacity, -1
    )
    got_keys, got_values, got_sessions = (
        lax.all_to_all(send_keys, ("grp", "seq"), split_axis=0, concat_axis=0, tiled=True),
        lax.all_to_all(send_values, ("grp", "seq"), split_axis=0, concat_axis=0, tiled=True),
        lax.all_to_all(session_slots, ("grp", "seq"), split_axis=0, concat_axis=0, tiled=True),
    )
    new_keys = got_keys.reshape(partition_count * capacity, -1)
    new_values = got_values.reshape(partition_count * capacity, -1)
    new_sessions = got_sessions.reshape(-1)
    heads_kv = new_keys.shape[1] // HEAD
    window = cache_key.shape[1]
    score_scale = HEAD ** (-0.5)
    query_heads = queries.reshape(per_shard, heads_kv, GROUP, HEAD)
    cached_keys = cache_key.reshape(per_shard, window, heads_kv, HEAD)
    cached_values = cache_value.reshape(per_shard, window, heads_kv, HEAD)
    fresh_keys = new_keys.reshape(-1, heads_kv, HEAD)
    fresh_values = new_values.reshape(-1, heads_kv, HEAD)
    cached_scores = (
        jnp.einsum("sghd,swgd->sghw", query_heads, cached_keys, preferred_element_type=jnp.float32)
        * score_scale
    )
    positions = jnp.arange(window, dtype=jnp.int32)
    live_slots = jnp.mod(positions[None, :] - cache_start[:, None], window) < cache_len[:, None]
    cached_scores = jnp.where(live_slots[:, None, None, :], cached_scores, -jnp.inf)
    fresh_scores = (
        jnp.einsum("sghd,ngd->sghn", query_heads, fresh_keys, preferred_element_type=jnp.float32)
        * score_scale
    )
    own_rows = new_sessions[None, :] == jnp.arange(per_shard, dtype=jnp.int32)[:, None]
    fresh_scores = jnp.where(own_rows[:, None, None, :], fresh_scores, -jnp.inf)
    largest = jnp.maximum(jnp.max(cached_scores, axis=3), jnp.max(fresh_scores, axis=3))
    cached_exp = jnp.exp(cached_scores - largest[..., None])
    fresh_exp = jnp.exp(fresh_scores - largest[..., None])
    totals = jnp.sum(cached_exp, axis=3) + jnp.sum(fresh_exp, axis=3)
    cached_weights = (cached_exp / totals[..., None]).astype(jnp.bfloat16)
    fresh_weights = (fresh_exp / totals[..., None]).astype(jnp.bfloat16)
    attended = jnp.einsum(
        "sghw,swgd->sghd", cached_weights, cached_values, preferred_element_type=jnp.float32
    )
    attended = attended + jnp.einsum(
        "sghn,ngd->sghd", fresh_weights, fresh_values, preferred_element_type=jnp.float32
    )
    return attended.reshape(per_shard, -1).astype(jnp.bfloat16)


def local(
    frames,
    token_session,
    ln_gain,
    w_key,
    w_value,
    k_bias,
    v_bias,
    queries,
    cache_key,
    cache_value,
    cache_start,
    cache_len,
):
    partitions = lax.axis_size(("grp", "seq"))
    shares = lax.axis_size("mp")
    per_shard = queries.shape[0]
    rows = frames.shape[0]
    capacity = max(2, 5 * rows // (2 * partitions) + 1)
    stages = stage_masks(lax.axis_size("grp"), lax.axis_size("seq"))
    if stages is None or shares != 2 or per_shard % 8 or capacity % 16 or partitions * capacity % HEAD:
        return general(
            frames, token_session, ln_gain, w_key, w_value, k_bias, v_bias, queries, cache_key, cache_value,
            cache_start, cache_len,
        )
    swap = [(0, 1), (1, 0)]
    index = lax.axis_index("mp").astype(jnp.int32).reshape(1)
    here = lax.axis_index(("grp", "seq")).astype(jnp.int32).reshape(1)
    own, held = partial_squares(frames)
    other = lax.ppermute(own, "mp", swap)
    held_key, held_value, pick, ids, scores, laid = beside(
        here, token_session[None, :], cache_start[None, :], cache_len[None, :], queries, cache_key, w_key,
        w_value, (partitions, per_shard, capacity, stages),
    )
    normed, sent = send_products(
        index, held, own, other, ln_gain[None, :], held_key, held_value, frames.shape[1] * shares
    )
    arrived = lax.ppermute(sent, "mp", swap)
    kept = keep_products(index, normed, held_key, held_value)
    blocks = pack(pick, ids, kept, arrived, k_bias[None, :], v_bias[None, :], len(stages[0]))

    def step(arrays, masks):
        pairs = [[(i, i ^ mask) for i in range(partitions)] for mask in masks]
        sent = [lax.ppermute(a, ("grp", "seq"), p) for a, p in zip(arrays[1:], pairs[1:])]
        return [arrays[0], *sent]

    got = step(regroup(step(blocks, stages[0])), stages[1])
    return attend(got, laid, scores, cache_value, capacity)


def solution(mesh):
    return jax.shard_map(
        local,
        mesh=mesh,
        in_specs=(
            P(("grp", "seq"), "mp"),
            P(("grp", "seq")),
            P("mp"),
            P("mp", None),
            P("mp", None),
            P("mp"),
            P("mp"),
            P(("grp", "seq"), "mp"),
            P(("grp", "seq"), None, "mp"),
            P(("grp", "seq"), None, "mp"),
            P(("grp", "seq")),
            P(("grp", "seq")),
        ),
        out_specs=P(("grp", "seq"), "mp"),
        check_vma=False,
    )
```

```python
import functools

import jax
import jax.numpy as jnp
from jax import lax
from jax.experimental import pallas as pl
from jax.experimental.pallas import tpu as pltpu
from jax.sharding import PartitionSpec as P

HEAD = 128
GROUP = 8

epsilon = 1e-06


def params(mib):
    return pltpu.CompilerParams(vmem_limit_bytes=mib << 20)


def cost(flops, nbytes):
    return pl.CostEstimate(flops=flops, bytes_accessed=nbytes, transcendentals=0)


def nt_dot(a, b):
    return lax.dot_general(a, b, (((1,), (1,)), ((), ())), preferred_element_type=jnp.float32)


def dot(a, b):
    return jnp.dot(a, b, preferred_element_type=jnp.float32)


SMEM = pl.BlockSpec(memory_space=pltpu.SMEM)
VMEM = pl.BlockSpec(memory_space=pltpu.VMEM)
HBM = pl.BlockSpec(memory_space=pltpu.HBM)


def in_hbm(array):
    return pltpu.with_memory_space_constraint(array, pltpu.HBM)


def squares_kernel(frames_ref, out_ref, held_ref, arrived):
    chunks, columns = arrived.shape[0], frames_ref.shape[1]
    wide = columns // chunks
    copies = []
    for chunk in range(chunks):
        part = (slice(None), pl.ds(chunk * wide, wide))
        copies.append(
            pltpu.make_async_copy(frames_ref.at[part], held_ref.at[part], arrived.at[chunk])
        )
        copies[-1].start()
    total = None
    for chunk in range(chunks):
        copies[chunk].wait()
        for at in range(chunk * wide, (chunk + 1) * wide, HEAD):
            part = held_ref[:, at : at + HEAD].astype(jnp.float32)
            part = part * part
            total = part if total is None else total + part
    out_ref[...] = total


def partial_squares(frames):
    rows, columns = frames.shape
    chunks = 2 if columns % (2 * HEAD) == 0 else 1
    return pl.pallas_call(
        squares_kernel,
        out_shape=(jax.ShapeDtypeStruct((rows, HEAD), jnp.float32), jax.ShapeDtypeStruct(frames.shape, frames.dtype)),
        in_specs=[HBM],
        out_specs=(VMEM, VMEM),
        scratch_shapes=[pltpu.SemaphoreType.DMA((chunks,))],
        compiler_params=params(8),
        cost_estimate=cost(2 * rows * columns, 2 * rows * columns),
        name="partial_squares",
    )(in_hbm(frames))


def products(normed_ref, half, key_ref, value_ref, out_ref):
    width = key_ref.shape[1] // 2
    columns = pl.ds(pl.multiple_of(half * width, width), width)
    out_ref[:, :width] = dot(normed_ref[...], key_ref[:, columns])
    out_ref[:, width:] = dot(normed_ref[...], value_ref[:, columns])


def send_kernel(
    features, index_ref, frames_ref, own_ref, other_ref, gain_ref, key_ref, value_ref, normed_ref, out_ref
):
    squares = jnp.sum(own_ref[...] + other_ref[...], axis=1, keepdims=True)
    inverse_rms = lax.rsqrt(squares / features + epsilon)
    normed_ref[...] = (
        frames_ref[...].astype(jnp.float32) * inverse_rms * gain_ref[...]
    ).astype(jnp.bfloat16)
    products(normed_ref, 1 - index_ref[0], key_ref, value_ref, out_ref)


def send_products(index, frames, own, other, gain, key, value, features):
    rows, columns = frames.shape
    width = key.shape[1]
    return pl.pallas_call(
        functools.partial(send_kernel, features),
        out_shape=(
            jax.ShapeDtypeStruct(frames.shape, jnp.bfloat16),
            jax.ShapeDtypeStruct((rows, width), jnp.float32),
        ),
        in_specs=[SMEM] + [VMEM] * 6,
        out_specs=(VMEM, VMEM),
        compiler_params=params(16),
        cost_estimate=cost(2 * rows * columns * width, 2 * key.size),
        name="send_products",
    )(index, frames, own, other, gain, key, value)


def keep_kernel(index_ref, normed_ref, key_ref, value_ref, out_ref):
    products(normed_ref, index_ref[0], key_ref, value_ref, out_ref)


def keep_products(index, normed, key, value):
    rows, columns = normed.shape
    width = key.shape[1]
    return pl.pallas_call(
        keep_kernel,
        out_shape=jax.ShapeDtypeStruct((rows, width), jnp.float32),
        in_specs=[SMEM] + [VMEM] * 3,
        out_specs=VMEM,
        compiler_params=params(16),
        cost_estimate=cost(2 * rows * columns * width, 2 * key.size),
        name="keep_products",
    )(index, normed, key, value)


def max_bits(masks):
    return functools.reduce(lambda a, b: a | b, masks)


def stage_masks(groups, members):
    if groups & (groups - 1) or members & (members - 1) or members < 4:
        return None
    near = sorted((g * members + m for g in range(groups) for m in range(2)), reverse=True)
    far = sorted(range(0, members, 2), reverse=True)
    return (0, *near[:-1]), (0, far[0], *far[-2:0:-1])


def route(per_shard, capacity, stages, here, session, pick_ref, ids_ref):
    slots, rows = pick_ref.shape
    partitions = slots // capacity
    near, far = stages
    target = lax.div(session, per_shard)
    local = session - target * per_shard
    apart = target ^ here
    step = [
        sum(jnp.where((apart & max_bits(masks)) == mask, at, 0) for at, mask in enumerate(masks))
        for masks in stages
    ]
    leaves = step[0] * len(far) + step[1]
    lands = step[1] * len(near) + step[0]
    to = lax.broadcasted_iota(jnp.int32, (partitions, rows), 0) == leaves
    to = to.astype(jnp.float32)
    earlier = lax.broadcasted_iota(jnp.int32, (rows, rows), 0) < lax.broadcasted_iota(
        jnp.int32, (rows, rows), 1
    )
    ahead = dot(to.astype(jnp.bfloat16), earlier.astype(jnp.bfloat16))
    order = jnp.sum(to * ahead, axis=0, keepdims=True).astype(jnp.int32)
    place = lax.broadcasted_iota(jnp.int32, (slots, rows), 0)
    pick_ref[...] = (place == leaves * capacity + order).astype(jnp.bfloat16)
    lane = (place == lands * capacity + order).astype(jnp.bfloat16)
    ids = nt_dot((to * (local + 1).astype(jnp.float32)).astype(jnp.bfloat16), lane)
    row = lax.broadcasted_iota(jnp.int32, ids_ref.shape, 1)
    block = jnp.zeros(ids_ref.shape, jnp.float32)
    for j in range(slots // HEAD):
        part = ids[:, j * HEAD : (j + 1) * HEAD]
        block = jnp.where(row == j, part[:, None, :], block)
    ids_ref[...] = block


def queries_of(queries_ref, head):
    columns = [
        queries_ref[:, at * HEAD : (at + 1) * HEAD].astype(jnp.float32)
        for at in range(head * GROUP, (head + 1) * GROUP)
    ]
    return jnp.concatenate(columns, axis=0).astype(jnp.bfloat16)


def score_cache(start_ref, len_ref, queries_ref, key_ref, out_ref, laid_ref):
    sessions, window, width = key_ref.shape
    heads, rows = width // HEAD, GROUP * sessions

    def by_row(ref):
        mine = lax.broadcasted_iota(jnp.int32, (rows, sessions), 0) % sessions
        mine = mine == lax.broadcasted_iota(jnp.int32, (rows, sessions), 1)
        values = jnp.where(mine, ref[...].astype(jnp.float32), 0.0)
        return jnp.sum(values, axis=1, keepdims=True).astype(jnp.int32)

    since = lax.broadcasted_iota(jnp.int32, (rows, window), 1) - by_row(start_ref)
    since = jnp.where(since < 0, since + window, since)
    live = since < by_row(len_ref)
    row_session = lax.broadcasted_iota(jnp.int32, (rows, window), 0) % sessions
    laid_ref[...] = jnp.zeros_like(laid_ref)
    for head in range(heads):
        query = queries_of(queries_ref, head)
        laid_ref[head * rows : (head + 1) * rows, head * HEAD : (head + 1) * HEAD] = query
        total = jnp.zeros((rows, window), jnp.float32)
        for session in range(sessions):
            key = key_ref[session, :, head * HEAD : (head + 1) * HEAD]
            total = jnp.where(row_session == session, nt_dot(query, key), total)
        total = jnp.where(live, total * (HEAD**-0.5), -jnp.inf)
        out_ref[head * rows : (head + 1) * rows] = total


def beside_kernel(
    per_shard,
    capacity,
    stages,
    here_ref,
    session_ref,
    start_ref,
    len_ref,
    queries_ref,
    cache_ref,
    w_key_ref,
    w_value_ref,
    held_key_ref,
    held_value_ref,
    pick_ref,
    ids_ref,
    score_ref,
    laid_ref,
    session,
    start,
    length,
    queries,
    cache,
    arrived,
):
    copies = []
    for at, (source, held) in enumerate(
        (
            (session_ref, session),
            (start_ref, start),
            (len_ref, length),
            (queries_ref, queries),
            (cache_ref, cache),
            (w_key_ref, held_key_ref),
            (w_value_ref, held_value_ref),
        )
    ):
        copies.append(pltpu.make_async_copy(source, held, arrived.at[at]))
        copies[-1].start()
    copies[0].wait()
    route(per_shard, capacity, stages, here_ref[0], session[...], pick_ref, ids_ref)
    for copy in copies[1:5]:
        copy.wait()
    score_cache(start, length, queries, cache, score_ref, laid_ref)
    for copy in copies[5:]:
        copy.wait()


def beside(here, session, start, length, queries, cache_key, w_key, w_value, sizes):
    partitions, per_shard, capacity, stages = sizes
    slots, rows = partitions * capacity, session.shape[1]
    sessions, window, width = cache_key.shape
    heads = width // HEAD
    id_rows = -(-slots // (8 * HEAD)) * 8
    copied = (session, start, length, queries, cache_key)
    return pl.pallas_call(
        functools.partial(beside_kernel, per_shard, capacity, stages),
        out_shape=(
            jax.ShapeDtypeStruct(w_key.shape, w_key.dtype),
            jax.ShapeDtypeStruct(w_value.shape, w_value.dtype),
            jax.ShapeDtypeStruct((slots, rows), jnp.bfloat16),
            jax.ShapeDtypeStruct((partitions, id_rows, HEAD), jnp.float32),
            jax.ShapeDtypeStruct((heads * GROUP * sessions, window), jnp.float32),
            jax.ShapeDtypeStruct((heads * GROUP * sessions, width), jnp.bfloat16),
        ),
        in_specs=[SMEM] + [HBM] * 7,
        out_specs=(VMEM,) * 6,
        scratch_shapes=[pltpu.VMEM(array.shape, array.dtype) for array in copied]
        + [pltpu.SemaphoreType.DMA((7,))],
        compiler_params=params(24),
        cost_estimate=cost(2 * GROUP * sessions * cache_key.size, 4 * w_key.size),
        name="beside",
    )(here, *map(in_hbm, copied), in_hbm(w_key), in_hbm(w_value))


def pack_kernel(
    pick_ref,
    ids_ref,
    kept_ref,
    got_ref,
    key_bias_ref,
    value_bias_ref,
    *out_refs,
):
    partitions = ids_ref.shape[0]
    far = partitions // len(out_refs)
    slots = pick_ref.shape[0]
    capacity = slots // partitions
    width = key_bias_ref.shape[1]
    sums = kept_ref[...] + got_ref[...]
    key = (sums[:, :width] + key_bias_ref[...]).astype(jnp.bfloat16)
    value = (sums[:, width:] + value_bias_ref[...]).astype(jnp.bfloat16)
    at = 0
    for source in (key, value):
        laid = dot(pick_ref[...], source).astype(jnp.bfloat16).reshape(partitions, capacity, width)
        for column in range(0, width, HEAD):
            part = laid[:, :, column : column + HEAD]
            part = part.reshape(partitions, capacity // 2, 2, HEAD)
            for step, out_ref in enumerate(out_refs):
                out_ref[:, at : at + capacity // 2] = part[step * far : (step + 1) * far]
            at += capacity // 2
    for step, out_ref in enumerate(out_refs):
        out_ref[:, at] = ids_ref[step * far : (step + 1) * far, :2, :].astype(jnp.bfloat16)


def pack(pick, ids, kept, got, key_bias, value_bias, near):
    rows, width = kept.shape
    partitions, id_rows, _ = ids.shape
    capacity = pick.shape[0] // partitions
    block = width // HEAD * capacity // 2 + 1
    return pl.pallas_call(
        pack_kernel,
        out_shape=[jax.ShapeDtypeStruct((partitions // near, block, 2, HEAD), jnp.bfloat16)] * near,
        in_specs=[VMEM] * 6,
        out_specs=[VMEM] * near,
        compiler_params=params(8),
        cost_estimate=cost(2 * rows * width * partitions * capacity, 8 * rows * width),
        name="pack",
    )(pick, ids, kept, got, key_bias, value_bias)


def regroup_kernel(*refs):
    far = refs[0].shape[0]
    got_refs, out_refs = refs[:-far], refs[-far:]
    for step, out_ref in enumerate(out_refs):
        for near, got_ref in enumerate(got_refs):
            out_ref[near] = got_ref[step]


def regroup(blocks):
    far, *block = blocks[0].shape
    return pl.pallas_call(
        regroup_kernel,
        out_shape=[jax.ShapeDtypeStruct((len(blocks), *block), jnp.bfloat16)] * far,
        in_specs=[VMEM] * len(blocks),
        out_specs=[VMEM] * far,
        compiler_params=params(8),
        cost_estimate=cost(0, 4 * len(blocks) * blocks[0].size),
        name="regroup",
    )(*blocks)


def attend_kernel(capacity, queries_ref, score_ref, cache_ref, *refs):
    *got_refs, out_ref = refs
    rows, window = score_ref.shape
    sessions, _, width = cache_ref.shape
    heads = width // HEAD
    slots = len(got_refs) * got_refs[0].shape[0] * capacity
    at = heads * capacity
    ids = jnp.concatenate(
        [
            sum(jnp.sum(ref[:, at, j : j + 1, :].astype(jnp.float32), axis=0) for ref in got_refs)
            for j in range(slots // HEAD)
        ],
        axis=1,
    ).astype(jnp.int32)
    own = lax.broadcasted_iota(jnp.int32, (rows, slots), 0) % sessions + 1 == ids

    def rows_of(vectors):
        columns = []
        for vector in vectors:
            part = slice(vector * capacity // 2, (vector + 1) * capacity // 2)
            columns.append(
                jnp.concatenate([ref[:, part].reshape(-1, HEAD) for ref in got_refs], axis=0)
            )
        return jnp.concatenate(columns, axis=1)

    cached = score_ref[...]
    fresh = nt_dot(queries_ref[...], rows_of(range(heads))) * (HEAD**-0.5)
    fresh = jnp.where(own, fresh, -jnp.inf)
    largest = jnp.maximum(
        jnp.max(cached, axis=1, keepdims=True), jnp.max(fresh, axis=1, keepdims=True)
    )
    cached = jnp.exp(cached - largest)
    fresh = jnp.exp(fresh - largest)
    total = jnp.sum(cached, axis=1, keepdims=True) + jnp.sum(fresh, axis=1, keepdims=True)
    cached = cached / total
    attended = dot((fresh / total).astype(jnp.bfloat16), rows_of(range(heads, 2 * heads)))
    row_session = lax.broadcasted_iota(jnp.int32, (rows, window), 0) % sessions
    for session in range(0, sessions, 2):
        weights = jnp.concatenate(
            [jnp.where(row_session == session + more, cached, 0.0) for more in range(2)], axis=1
        )
        values = cache_ref[session : session + 2].reshape(2 * window, width)
        attended += dot(weights.astype(jnp.bfloat16), values)
    for head in range(heads):
        for q in range(GROUP):
            row, column = (head * GROUP + q) * sessions, (head * GROUP + q) * HEAD
            out_ref[:, column : column + HEAD] = attended[
                row : row + sessions, head * HEAD : (head + 1) * HEAD
            ].astype(jnp.bfloat16)


def attend(got, queries, scores, cache_value, capacity):
    return pl.pallas_call(
        functools.partial(attend_kernel, capacity),
        out_shape=jax.ShapeDtypeStruct(
            (cache_value.shape[0], queries.shape[1] * GROUP), jnp.bfloat16
        ),
        in_specs=[VMEM] * (3 + len(got)),
        out_specs=VMEM,
        compiler_params=params(8),
        cost_estimate=cost(4 * queries.shape[0] * cache_value.size, 2 * cache_value.size),
        name="attend",
    )(queries, scores, cache_value, *got)


def project(frame_rows, ln_gain, w_key, w_value, k_bias, v_bias):
    values32 = frame_rows.astype(jnp.float32)
    partial_squares = jnp.sum(values32 * values32, axis=1)
    squares = lax.psum(partial_squares, "mp")
    inverse_rms = lax.rsqrt(squares / (frame_rows.shape[1] * lax.axis_size("mp")) + epsilon)
    normed = (values32 * inverse_rms[:, None] * ln_gain[None, :]).astype(jnp.bfloat16)
    part_key = jnp.dot(normed, w_key, preferred_element_type=jnp.float32)
    part_value = jnp.dot(normed, w_value, preferred_element_type=jnp.float32)
    key_sums, value_sums = (
        lax.psum_scatter(part_key, "mp", scatter_dimension=1, tiled=True),
        lax.psum_scatter(part_value, "mp", scatter_dimension=1, tiled=True),
    )
    new_keys = (key_sums + k_bias[None, :]).astype(jnp.bfloat16)
    new_values = (value_sums + v_bias[None, :]).astype(jnp.bfloat16)
    return (new_keys, new_values)


def slot_sources(token_session, per_shard, partition_count, capacity):
    row_count = token_session.shape[0]
    target = token_session // per_shard
    one_hot = (target[:, None] == jnp.arange(partition_count, dtype=jnp.int32)[None, :]).astype(
        jnp.int32
    )
    order_in = jnp.sum((jnp.cumsum(one_hot, axis=0) - one_hot) * one_hot, axis=1)
    slot_index = target * capacity + order_in
    matches = (
        slot_index[None, :] == jnp.arange(partition_count * capacity, dtype=jnp.int32)[:, None]
    )
    source = jnp.sum(jnp.where(matches, jnp.arange(row_count, dtype=jnp.int32)[None, :], 0), axis=1)
    filled = jnp.any(matches, axis=1)
    sessions = jnp.where(filled, jnp.mod(token_session[source], per_shard), -1)
    return (source, filled, sessions)


def general(
    frames,
    token_session,
    ln_gain,
    w_key,
    w_value,
    k_bias,
    v_bias,
    queries,
    cache_key,
    cache_value,
    cache_start,
    cache_len,
):
    partition_count = lax.axis_size(("grp", "seq"))
    per_shard = queries.shape[0]
    rows_here = frames.shape[0]
    capacity = max(2, 5 * rows_here // (2 * partition_count) + 1)
    source, filled, sessions = slot_sources(token_session, per_shard, partition_count, capacity)
    session_slots = sessions.reshape(partition_count, capacity)
    nothing = jnp.zeros((), jnp.bfloat16)
    own_keys, own_values = project(frames, ln_gain, w_key, w_value, k_bias, v_bias)
    send_keys = jnp.where(filled[:, None], own_keys[source], nothing).reshape(
        partition_count, capacity, -1
    )
    send_values = jnp.where(filled[:, None], own_values[source], nothing).reshape(
        partition_count, capacity, -1
    )
    got_keys, got_values, got_sessions = (
        lax.all_to_all(send_keys, ("grp", "seq"), split_axis=0, concat_axis=0, tiled=True),
        lax.all_to_all(send_values, ("grp", "seq"), split_axis=0, concat_axis=0, tiled=True),
        lax.all_to_all(session_slots, ("grp", "seq"), split_axis=0, concat_axis=0, tiled=True),
    )
    new_keys = got_keys.reshape(partition_count * capacity, -1)
    new_values = got_values.reshape(partition_count * capacity, -1)
    new_sessions = got_sessions.reshape(-1)
    heads_kv = new_keys.shape[1] // HEAD
    window = cache_key.shape[1]
    score_scale = HEAD ** (-0.5)
    query_heads = queries.reshape(per_shard, heads_kv, GROUP, HEAD)
    cached_keys = cache_key.reshape(per_shard, window, heads_kv, HEAD)
    cached_values = cache_value.reshape(per_shard, window, heads_kv, HEAD)
    fresh_keys = new_keys.reshape(-1, heads_kv, HEAD)
    fresh_values = new_values.reshape(-1, heads_kv, HEAD)
    cached_scores = (
        jnp.einsum("sghd,swgd->sghw", query_heads, cached_keys, preferred_element_type=jnp.float32)
        * score_scale
    )
    positions = jnp.arange(window, dtype=jnp.int32)
    live_slots = jnp.mod(positions[None, :] - cache_start[:, None], window) < cache_len[:, None]
    cached_scores = jnp.where(live_slots[:, None, None, :], cached_scores, -jnp.inf)
    fresh_scores = (
        jnp.einsum("sghd,ngd->sghn", query_heads, fresh_keys, preferred_element_type=jnp.float32)
        * score_scale
    )
    own_rows = new_sessions[None, :] == jnp.arange(per_shard, dtype=jnp.int32)[:, None]
    fresh_scores = jnp.where(own_rows[:, None, None, :], fresh_scores, -jnp.inf)
    largest = jnp.maximum(jnp.max(cached_scores, axis=3), jnp.max(fresh_scores, axis=3))
    cached_exp = jnp.exp(cached_scores - largest[..., None])
    fresh_exp = jnp.exp(fresh_scores - largest[..., None])
    totals = jnp.sum(cached_exp, axis=3) + jnp.sum(fresh_exp, axis=3)
    cached_weights = (cached_exp / totals[..., None]).astype(jnp.bfloat16)
    fresh_weights = (fresh_exp / totals[..., None]).astype(jnp.bfloat16)
    attended = jnp.einsum(
        "sghw,swgd->sghd", cached_weights, cached_values, preferred_element_type=jnp.float32
    )
    attended = attended + jnp.einsum(
        "sghn,ngd->sghd", fresh_weights, fresh_values, preferred_element_type=jnp.float32
    )
    return attended.reshape(per_shard, -1).astype(jnp.bfloat16)


def local(
    frames,
    token_session,
    ln_gain,
    w_key,
    w_value,
    k_bias,
    v_bias,
    queries,
    cache_key,
    cache_value,
    cache_start,
    cache_len,
):
    partitions = lax.axis_size(("grp", "seq"))
    shares = lax.axis_size("mp")
    per_shard = queries.shape[0]
    rows = frames.shape[0]
    capacity = max(2, 5 * rows // (2 * partitions) + 1)
    stages = stage_masks(lax.axis_size("grp"), lax.axis_size("seq"))
    if stages is None or shares != 2 or per_shard % 8 or capacity % 16 or partitions * capacity % HEAD:
        return general(
            frames, token_session, ln_gain, w_key, w_value, k_bias, v_bias, queries, cache_key, cache_value,
            cache_start, cache_len,
        )
    swap = [(0, 1), (1, 0)]
    index = lax.axis_index("mp").astype(jnp.int32).reshape(1)
    here = lax.axis_index(("grp", "seq")).astype(jnp.int32).reshape(1)
    own, held = partial_squares(frames)
    other = lax.ppermute(own, "mp", swap)
    held_key, held_value, pick, ids, scores, laid = beside(
        here, token_session[None, :], cache_start[None, :], cache_len[None, :], queries, cache_key, w_key,
        w_value, (partitions, per_shard, capacity, stages),
    )
    normed, sent = send_products(
        index, held, own, other, ln_gain[None, :], held_key, held_value, frames.shape[1] * shares
    )
    arrived = lax.ppermute(sent, "mp", swap)
    kept = keep_products(index, normed, held_key, held_value)
    blocks = pack(pick, ids, kept, arrived, k_bias[None, :], v_bias[None, :], len(stages[0]))

    def step(arrays, masks):
        pairs = [[(i, i ^ mask) for i in range(partitions)] for mask in masks]
        sent = [lax.ppermute(a, ("grp", "seq"), p) for a, p in zip(arrays[1:], pairs[1:])]
        return [arrays[0], *sent]

    got = step(regroup(step(blocks, stages[0])), stages[1])
    return attend(got, laid, scores, cache_value, capacity)


def solution(mesh):
    return jax.shard_map(
        local,
        mesh=mesh,
        in_specs=(
            P(("grp", "seq"), "mp"),
            P(("grp", "seq")),
            P("mp"),
            P("mp", None),
            P("mp", None),
            P("mp"),
            P("mp"),
            P(("grp", "seq"), "mp"),
            P(("grp", "seq"), None, "mp"),
            P(("grp", "seq"), None, "mp"),
            P(("grp", "seq")),
            P(("grp", "seq")),
        ),
        out_specs=P(("grp", "seq"), "mp"),
        check_vma=False,
    )
```

```python
import functools

import jax
import jax.numpy as jnp
from jax import lax
from jax.experimental import pallas as pl
from jax.experimental.pallas import tpu as pltpu
from jax.sharding import PartitionSpec as P

HEAD = 128
GROUP = 8

epsilon = 1e-06


def params(mib):
    return pltpu.CompilerParams(vmem_limit_bytes=mib << 20)


def cost(flops, nbytes):
    return pl.CostEstimate(flops=flops, bytes_accessed=nbytes, transcendentals=0)


def nt_dot(a, b):
    return lax.dot_general(a, b, (((1,), (1,)), ((), ())), preferred_element_type=jnp.float32)


def dot(a, b):
    return jnp.dot(a, b, preferred_element_type=jnp.float32)


SMEM = pl.BlockSpec(memory_space=pltpu.SMEM)
VMEM = pl.BlockSpec(memory_space=pltpu.VMEM)
HBM = pl.BlockSpec(memory_space=pltpu.HBM)


def in_hbm(array):
    return pltpu.with_memory_space_constraint(array, pltpu.HBM)


def squares_kernel(frames_ref, out_ref, held_ref, arrived):
    chunks, columns = arrived.shape[0], frames_ref.shape[1]
    wide = columns // chunks
    copies = []
    for chunk in range(chunks):
        part = (slice(None), pl.ds(chunk * wide, wide))
        copies.append(
            pltpu.make_async_copy(frames_ref.at[part], held_ref.at[part], arrived.at[chunk])
        )
        copies[-1].start()
    total = None
    for chunk in range(chunks):
        copies[chunk].wait()
        for at in range(chunk * wide, (chunk + 1) * wide, HEAD):
            part = held_ref[:, at : at + HEAD].astype(jnp.float32)
            part = part * part
            total = part if total is None else total + part
    out_ref[...] = total


def partial_squares(frames):
    rows, columns = frames.shape
    chunks = 2 if columns % (2 * HEAD) == 0 else 1
    return pl.pallas_call(
        squares_kernel,
        out_shape=(jax.ShapeDtypeStruct((rows, HEAD), jnp.float32), jax.ShapeDtypeStruct(frames.shape, frames.dtype)),
        in_specs=[HBM],
        out_specs=(VMEM, VMEM),
        scratch_shapes=[pltpu.SemaphoreType.DMA((chunks,))],
        compiler_params=params(8),
        cost_estimate=cost(2 * rows * columns, 2 * rows * columns),
        name="partial_squares",
    )(in_hbm(frames))


def products(normed_ref, half, key_ref, value_ref, out_ref):
    width = key_ref.shape[1] // 2
    columns = pl.ds(pl.multiple_of(half * width, width), width)
    out_ref[:, :width] = dot(normed_ref[...], key_ref[:, columns])
    out_ref[:, width:] = dot(normed_ref[...], value_ref[:, columns])


def send_kernel(
    features, index_ref, frames_ref, own_ref, other_ref, gain_ref, key_ref, value_ref, normed_ref, out_ref
):
    squares = jnp.sum(own_ref[...] + other_ref[...], axis=1, keepdims=True)
    inverse_rms = lax.rsqrt(squares / features + epsilon)
    normed_ref[...] = (
        frames_ref[...].astype(jnp.float32) * inverse_rms * gain_ref[...]
    ).astype(jnp.bfloat16)
    products(normed_ref, 1 - index_ref[0], key_ref, value_ref, out_ref)


def send_products(index, frames, own, other, gain, key, value, features):
    rows, columns = frames.shape
    width = key.shape[1]
    return pl.pallas_call(
        functools.partial(send_kernel, features),
        out_shape=(
            jax.ShapeDtypeStruct(frames.shape, jnp.bfloat16),
            jax.ShapeDtypeStruct((rows, width), jnp.float32),
        ),
        in_specs=[SMEM] + [VMEM] * 6,
        out_specs=(VMEM, VMEM),
        compiler_params=params(16),
        cost_estimate=cost(2 * rows * columns * width, 2 * key.size),
        name="send_products",
    )(index, frames, own, other, gain, key, value)


def keep_kernel(index_ref, normed_ref, key_ref, value_ref, out_ref):
    products(normed_ref, index_ref[0], key_ref, value_ref, out_ref)


def keep_products(index, normed, key, value):
    rows, columns = normed.shape
    width = key.shape[1]
    return pl.pallas_call(
        keep_kernel,
        out_shape=jax.ShapeDtypeStruct((rows, width), jnp.float32),
        in_specs=[SMEM] + [VMEM] * 3,
        out_specs=VMEM,
        compiler_params=params(16),
        cost_estimate=cost(2 * rows * columns * width, 2 * key.size),
        name="keep_products",
    )(index, normed, key, value)


def max_bits(masks):
    return functools.reduce(lambda a, b: a | b, masks)


def stage_masks(groups, members):
    if groups & (groups - 1) or members & (members - 1) or members < 4:
        return None
    near = sorted((g * members + m for g in range(groups) for m in range(2)), reverse=True)
    far = sorted(range(0, members, 2), reverse=True)
    return (0, *near[:-1]), (0, far[0], *far[-2:0:-1])


def route(per_shard, capacity, stages, here, session, pick_ref, ids_ref):
    slots, rows = pick_ref.shape
    partitions = slots // capacity
    near, far = stages
    target = lax.div(session, per_shard)
    local = session - target * per_shard
    apart = target ^ here
    step = [
        sum(jnp.where((apart & max_bits(masks)) == mask, at, 0) for at, mask in enumerate(masks))
        for masks in stages
    ]
    leaves = step[0] * len(far) + step[1]
    lands = step[1] * len(near) + step[0]
    to = lax.broadcasted_iota(jnp.int32, (partitions, rows), 0) == leaves
    to = to.astype(jnp.float32)
    earlier = lax.broadcasted_iota(jnp.int32, (rows, rows), 0) < lax.broadcasted_iota(
        jnp.int32, (rows, rows), 1
    )
    ahead = dot(to.astype(jnp.bfloat16), earlier.astype(jnp.bfloat16))
    order = jnp.sum(to * ahead, axis=0, keepdims=True).astype(jnp.int32)
    place = lax.broadcasted_iota(jnp.int32, (slots, rows), 0)
    pick_ref[...] = (place == leaves * capacity + order).astype(jnp.bfloat16)
    lane = lands * capacity + order
    parts = slots // HEAD
    block = lax.broadcasted_iota(jnp.int32, (partitions * parts, rows), 0)
    named = block == leaves * parts + lane // HEAD
    named = jnp.where(named, (local + 1).astype(jnp.float32), 0.0).astype(jnp.bfloat16)
    spot = lax.broadcasted_iota(jnp.int32, (HEAD, rows), 0) == lane % HEAD
    ids_ref[...] = nt_dot(named, spot.astype(jnp.bfloat16))


def queries_of(queries_ref, head):
    columns = [
        queries_ref[:, at * HEAD : (at + 1) * HEAD].astype(jnp.float32)
        for at in range(head * GROUP, (head + 1) * GROUP)
    ]
    return jnp.concatenate(columns, axis=0).astype(jnp.bfloat16)


def score_cache(start_ref, len_ref, queries_ref, key_ref, out_ref, laid_ref):
    sessions, window, width = key_ref.shape
    heads, rows = width // HEAD, GROUP * sessions

    def by_row(ref):
        mine = lax.broadcasted_iota(jnp.int32, (rows, sessions), 0) % sessions
        mine = mine == lax.broadcasted_iota(jnp.int32, (rows, sessions), 1)
        values = jnp.where(mine, ref[...].astype(jnp.float32), 0.0)
        return jnp.sum(values, axis=1, keepdims=True).astype(jnp.int32)

    since = lax.broadcasted_iota(jnp.int32, (rows, window), 1) - by_row(start_ref)
    since = jnp.where(since < 0, since + window, since)
    live = since < by_row(len_ref)
    row_session = lax.broadcasted_iota(jnp.int32, (rows, window), 0) % sessions
    laid_ref[...] = jnp.zeros_like(laid_ref)
    for head in range(heads):
        query = queries_of(queries_ref, head)
        laid_ref[head * rows : (head + 1) * rows, head * HEAD : (head + 1) * HEAD] = query
        total = jnp.zeros((rows, window), jnp.float32)
        for session in range(sessions):
            key = key_ref[session, :, head * HEAD : (head + 1) * HEAD]
            total = jnp.where(row_session == session, nt_dot(query, key), total)
        total = jnp.where(live, total * (HEAD**-0.5), -jnp.inf)
        out_ref[head * rows : (head + 1) * rows] = total


def beside_kernel(
    per_shard,
    capacity,
    stages,
    here_ref,
    session_ref,
    start_ref,
    len_ref,
    queries_ref,
    cache_ref,
    w_key_ref,
    w_value_ref,
    held_key_ref,
    held_value_ref,
    pick_ref,
    ids_ref,
    score_ref,
    laid_ref,
    session,
    start,
    length,
    queries,
    cache,
    arrived,
):
    copies = []
    for at, (source, held) in enumerate(
        (
            (session_ref, session),
            (start_ref, start),
            (len_ref, length),
            (queries_ref, queries),
            (cache_ref, cache),
            (w_key_ref, held_key_ref),
            (w_value_ref, held_value_ref),
        )
    ):
        copies.append(pltpu.make_async_copy(source, held, arrived.at[at]))
        copies[-1].start()
    copies[0].wait()
    route(per_shard, capacity, stages, here_ref[0], session[...], pick_ref, ids_ref)
    for copy in copies[1:5]:
        copy.wait()
    score_cache(start, length, queries, cache, score_ref, laid_ref)
    for copy in copies[5:]:
        copy.wait()


def beside(here, session, start, length, queries, cache_key, w_key, w_value, sizes):
    partitions, per_shard, capacity, stages = sizes
    slots, rows = partitions * capacity, session.shape[1]
    sessions, window, width = cache_key.shape
    heads = width // HEAD
    copied = (session, start, length, queries, cache_key)
    return pl.pallas_call(
        functools.partial(beside_kernel, per_shard, capacity, stages),
        out_shape=(
            jax.ShapeDtypeStruct(w_key.shape, w_key.dtype),
            jax.ShapeDtypeStruct(w_value.shape, w_value.dtype),
            jax.ShapeDtypeStruct((slots, rows), jnp.bfloat16),
            jax.ShapeDtypeStruct((partitions * slots // HEAD, HEAD), jnp.float32),
            jax.ShapeDtypeStruct((heads * GROUP * sessions, window), jnp.float32),
            jax.ShapeDtypeStruct((heads * GROUP * sessions, width), jnp.bfloat16),
        ),
        in_specs=[SMEM] + [HBM] * 7,
        out_specs=(VMEM,) * 6,
        scratch_shapes=[pltpu.VMEM(array.shape, array.dtype) for array in copied]
        + [pltpu.SemaphoreType.DMA((7,))],
        compiler_params=params(24),
        cost_estimate=cost(2 * GROUP * sessions * cache_key.size, 4 * w_key.size),
        name="beside",
    )(here, *map(in_hbm, copied), in_hbm(w_key), in_hbm(w_value))


def pack_kernel(pick_ref, ids_ref, kept_ref, got_ref, key_bias_ref, value_bias_ref, *out_refs):
    width = key_bias_ref.shape[1]
    sums = kept_ref[...] + got_ref[...]
    key = (sums[:, :width] + key_bias_ref[...]).astype(jnp.bfloat16)
    value = (sums[:, width:] + value_bias_ref[...]).astype(jnp.bfloat16)
    tall = pick_ref.shape[0] // len(out_refs)
    at = 0
    for source in (key, value):
        laid = dot(pick_ref[...], source).astype(jnp.bfloat16)
        for column in range(0, width, HEAD):
            for step, out_ref in enumerate(out_refs):
                out_ref[at : at + tall, :] = laid[
                    step * tall : (step + 1) * tall, column : column + HEAD
                ]
            at += tall
    named = ids_ref.shape[0] // len(out_refs)
    for step, out_ref in enumerate(out_refs):
        out_ref[at:, :] = ids_ref[step * named : (step + 1) * named, :].astype(jnp.bfloat16)


def pack(pick, ids, kept, got, key_bias, value_bias, near):
    rows, width = kept.shape
    slots = pick.shape[0]
    tall = (width // HEAD * slots + ids.shape[0]) // near
    return pl.pallas_call(
        pack_kernel,
        out_shape=[jax.ShapeDtypeStruct((tall, HEAD), jnp.bfloat16)] * near,
        in_specs=[VMEM] * 6,
        out_specs=[VMEM] * near,
        compiler_params=params(8),
        cost_estimate=cost(2 * rows * width * slots, 8 * rows * width),
        name="pack",
    )(pick, ids, kept, got, key_bias, value_bias)


def regroup_kernel(near, vectors, capacity, *refs):
    got_refs, out_refs = refs[:near], refs[near:]
    far = len(out_refs)
    for vector in range(vectors):
        for step, out_ref in enumerate(out_refs):
            for first, got_ref in enumerate(got_refs):
                to, at = (vector * near + first) * capacity, (vector * far + step) * capacity
                out_ref[to : to + capacity, :] = got_ref[at : at + capacity, :]
    ids = sum(ref[vectors * far * capacity :, :].astype(jnp.float32) for ref in got_refs)
    for out_ref in out_refs:
        out_ref[vectors * near * capacity :, :] = ids.astype(jnp.bfloat16)


def regroup(blocks, far, vectors, capacity):
    near = len(blocks)
    tall = blocks[0].shape[0] + vectors * capacity * (near - far)
    return pl.pallas_call(
        functools.partial(regroup_kernel, near, vectors, capacity),
        out_shape=[jax.ShapeDtypeStruct((tall, HEAD), jnp.bfloat16)] * far,
        in_specs=[VMEM] * near,
        out_specs=[VMEM] * far,
        compiler_params=params(8),
        cost_estimate=cost(0, 4 * near * blocks[0].size),
        name="regroup",
    )(*blocks)


def attend_kernel(near, capacity, queries_ref, score_ref, cache_ref, *refs):
    *got_refs, out_ref = refs
    rows, window = score_ref.shape
    sessions, _, width = cache_ref.shape
    heads = width // HEAD
    tall = near * capacity
    slots = len(got_refs) * tall
    parts = slots // HEAD
    ids = [
        sum(
            ref[2 * heads * tall :, :].astype(jnp.float32)[step * parts + part : step * parts + part + 1]
            for step, ref in enumerate(got_refs)
        )
        for part in range(parts)
    ]
    ids = jnp.concatenate(ids, axis=1).astype(jnp.int32)
    own = lax.broadcasted_iota(jnp.int32, (rows, slots), 0) % sessions + 1 == ids

    def rows_of(vectors):
        columns = []
        for vector in vectors:
            part = slice(vector * tall, (vector + 1) * tall)
            columns.append(jnp.concatenate([ref[part, :] for ref in got_refs], axis=0))
        return jnp.concatenate(columns, axis=1)

    cached = score_ref[...]
    fresh = nt_dot(queries_ref[...], rows_of(range(heads))) * (HEAD**-0.5)
    fresh = jnp.where(own, fresh, -jnp.inf)
    largest = jnp.maximum(
        jnp.max(cached, axis=1, keepdims=True), jnp.max(fresh, axis=1, keepdims=True)
    )
    cached = jnp.exp(cached - largest)
    fresh = jnp.exp(fresh - largest)
    total = jnp.sum(cached, axis=1, keepdims=True) + jnp.sum(fresh, axis=1, keepdims=True)
    cached = cached / total
    attended = dot((fresh / total).astype(jnp.bfloat16), rows_of(range(heads, 2 * heads)))
    row_session = lax.broadcasted_iota(jnp.int32, (rows, window), 0) % sessions
    for session in range(0, sessions, 2):
        weights = jnp.concatenate(
            [jnp.where(row_session == session + more, cached, 0.0) for more in range(2)], axis=1
        )
        values = cache_ref[session : session + 2].reshape(2 * window, width)
        attended += dot(weights.astype(jnp.bfloat16), values)
    for head in range(heads):
        for q in range(GROUP):
            row, column = (head * GROUP + q) * sessions, (head * GROUP + q) * HEAD
            out_ref[:, column : column + HEAD] = attended[
                row : row + sessions, head * HEAD : (head + 1) * HEAD
            ].astype(jnp.bfloat16)


def attend(got, queries, scores, cache_value, near, capacity):
    return pl.pallas_call(
        functools.partial(attend_kernel, near, capacity),
        out_shape=jax.ShapeDtypeStruct(
            (cache_value.shape[0], queries.shape[1] * GROUP), jnp.bfloat16
        ),
        in_specs=[VMEM] * (3 + len(got)),
        out_specs=VMEM,
        compiler_params=params(8),
        cost_estimate=cost(4 * queries.shape[0] * cache_value.size, 2 * cache_value.size),
        name="attend",
    )(queries, scores, cache_value, *got)


def project(frame_rows, ln_gain, w_key, w_value, k_bias, v_bias):
    values32 = frame_rows.astype(jnp.float32)
    partial_squares = jnp.sum(values32 * values32, axis=1)
    squares = lax.psum(partial_squares, "mp")
    inverse_rms = lax.rsqrt(squares / (frame_rows.shape[1] * lax.axis_size("mp")) + epsilon)
    normed = (values32 * inverse_rms[:, None] * ln_gain[None, :]).astype(jnp.bfloat16)
    part_key = jnp.dot(normed, w_key, preferred_element_type=jnp.float32)
    part_value = jnp.dot(normed, w_value, preferred_element_type=jnp.float32)
    key_sums, value_sums = (
        lax.psum_scatter(part_key, "mp", scatter_dimension=1, tiled=True),
        lax.psum_scatter(part_value, "mp", scatter_dimension=1, tiled=True),
    )
    new_keys = (key_sums + k_bias[None, :]).astype(jnp.bfloat16)
    new_values = (value_sums + v_bias[None, :]).astype(jnp.bfloat16)
    return (new_keys, new_values)


def slot_sources(token_session, per_shard, partition_count, capacity):
    row_count = token_session.shape[0]
    target = token_session // per_shard
    one_hot = (target[:, None] == jnp.arange(partition_count, dtype=jnp.int32)[None, :]).astype(
        jnp.int32
    )
    order_in = jnp.sum((jnp.cumsum(one_hot, axis=0) - one_hot) * one_hot, axis=1)
    slot_index = target * capacity + order_in
    matches = (
        slot_index[None, :] == jnp.arange(partition_count * capacity, dtype=jnp.int32)[:, None]
    )
    source = jnp.sum(jnp.where(matches, jnp.arange(row_count, dtype=jnp.int32)[None, :], 0), axis=1)
    filled = jnp.any(matches, axis=1)
    sessions = jnp.where(filled, jnp.mod(token_session[source], per_shard), -1)
    return (source, filled, sessions)


def general(
    frames,
    token_session,
    ln_gain,
    w_key,
    w_value,
    k_bias,
    v_bias,
    queries,
    cache_key,
    cache_value,
    cache_start,
    cache_len,
):
    partition_count = lax.axis_size(("grp", "seq"))
    per_shard = queries.shape[0]
    rows_here = frames.shape[0]
    capacity = max(2, 5 * rows_here // (2 * partition_count) + 1)
    source, filled, sessions = slot_sources(token_session, per_shard, partition_count, capacity)
    session_slots = sessions.reshape(partition_count, capacity)
    nothing = jnp.zeros((), jnp.bfloat16)
    own_keys, own_values = project(frames, ln_gain, w_key, w_value, k_bias, v_bias)
    send_keys = jnp.where(filled[:, None], own_keys[source], nothing).reshape(
        partition_count, capacity, -1
    )
    send_values = jnp.where(filled[:, None], own_values[source], nothing).reshape(
        partition_count, capacity, -1
    )
    got_keys, got_values, got_sessions = (
        lax.all_to_all(send_keys, ("grp", "seq"), split_axis=0, concat_axis=0, tiled=True),
        lax.all_to_all(send_values, ("grp", "seq"), split_axis=0, concat_axis=0, tiled=True),
        lax.all_to_all(session_slots, ("grp", "seq"), split_axis=0, concat_axis=0, tiled=True),
    )
    new_keys = got_keys.reshape(partition_count * capacity, -1)
    new_values = got_values.reshape(partition_count * capacity, -1)
    new_sessions = got_sessions.reshape(-1)
    heads_kv = new_keys.shape[1] // HEAD
    window = cache_key.shape[1]
    score_scale = HEAD ** (-0.5)
    query_heads = queries.reshape(per_shard, heads_kv, GROUP, HEAD)
    cached_keys = cache_key.reshape(per_shard, window, heads_kv, HEAD)
    cached_values = cache_value.reshape(per_shard, window, heads_kv, HEAD)
    fresh_keys = new_keys.reshape(-1, heads_kv, HEAD)
    fresh_values = new_values.reshape(-1, heads_kv, HEAD)
    cached_scores = (
        jnp.einsum("sghd,swgd->sghw", query_heads, cached_keys, preferred_element_type=jnp.float32)
        * score_scale
    )
    positions = jnp.arange(window, dtype=jnp.int32)
    live_slots = jnp.mod(positions[None, :] - cache_start[:, None], window) < cache_len[:, None]
    cached_scores = jnp.where(live_slots[:, None, None, :], cached_scores, -jnp.inf)
    fresh_scores = (
        jnp.einsum("sghd,ngd->sghn", query_heads, fresh_keys, preferred_element_type=jnp.float32)
        * score_scale
    )
    own_rows = new_sessions[None, :] == jnp.arange(per_shard, dtype=jnp.int32)[:, None]
    fresh_scores = jnp.where(own_rows[:, None, None, :], fresh_scores, -jnp.inf)
    largest = jnp.maximum(jnp.max(cached_scores, axis=3), jnp.max(fresh_scores, axis=3))
    cached_exp = jnp.exp(cached_scores - largest[..., None])
    fresh_exp = jnp.exp(fresh_scores - largest[..., None])
    totals = jnp.sum(cached_exp, axis=3) + jnp.sum(fresh_exp, axis=3)
    cached_weights = (cached_exp / totals[..., None]).astype(jnp.bfloat16)
    fresh_weights = (fresh_exp / totals[..., None]).astype(jnp.bfloat16)
    attended = jnp.einsum(
        "sghw,swgd->sghd", cached_weights, cached_values, preferred_element_type=jnp.float32
    )
    attended = attended + jnp.einsum(
        "sghn,ngd->sghd", fresh_weights, fresh_values, preferred_element_type=jnp.float32
    )
    return attended.reshape(per_shard, -1).astype(jnp.bfloat16)


def local(
    frames,
    token_session,
    ln_gain,
    w_key,
    w_value,
    k_bias,
    v_bias,
    queries,
    cache_key,
    cache_value,
    cache_start,
    cache_len,
):
    partitions = lax.axis_size(("grp", "seq"))
    shares = lax.axis_size("mp")
    per_shard = queries.shape[0]
    rows = frames.shape[0]
    capacity = max(2, 5 * rows // (2 * partitions) + 1)
    stages = stage_masks(lax.axis_size("grp"), lax.axis_size("seq"))
    if stages is None or shares != 2 or per_shard % 8 or capacity % 16 or partitions * capacity % HEAD:
        return general(
            frames, token_session, ln_gain, w_key, w_value, k_bias, v_bias, queries, cache_key, cache_value,
            cache_start, cache_len,
        )
    swap = [(0, 1), (1, 0)]
    index = lax.axis_index("mp").astype(jnp.int32).reshape(1)
    here = lax.axis_index(("grp", "seq")).astype(jnp.int32).reshape(1)
    own, held = partial_squares(frames)
    other = lax.ppermute(own, "mp", swap)
    held_key, held_value, pick, ids, scores, laid = beside(
        here, token_session[None, :], cache_start[None, :], cache_len[None, :], queries, cache_key, w_key,
        w_value, (partitions, per_shard, capacity, stages),
    )
    normed, sent = send_products(
        index, held, own, other, ln_gain[None, :], held_key, held_value, frames.shape[1] * shares
    )
    arrived = lax.ppermute(sent, "mp", swap)
    kept = keep_products(index, normed, held_key, held_value)
    blocks = pack(pick, ids, kept, arrived, k_bias[None, :], v_bias[None, :], len(stages[0]))

    def step(arrays, masks):
        pairs = [[(i, i ^ mask) for i in range(partitions)] for mask in masks]
        sent = [lax.ppermute(a, ("grp", "seq"), p) for a, p in zip(arrays[1:], pairs[1:])]
        return [arrays[0], *sent]

    near, far = stages
    vectors = 2 * cache_key.shape[2] // HEAD
    mid = regroup(step(blocks, near), len(far), vectors, capacity)
    return attend(step(mid, far), laid, scores, cache_value, len(near), capacity)


def solution(mesh):
    return jax.shard_map(
        local,
        mesh=mesh,
        in_specs=(
            P(("grp", "seq"), "mp"),
            P(("grp", "seq")),
            P("mp"),
            P("mp", None),
            P("mp", None),
            P("mp"),
            P("mp"),
            P(("grp", "seq"), "mp"),
            P(("grp", "seq"), None, "mp"),
            P(("grp", "seq"), None, "mp"),
            P(("grp", "seq")),
            P(("grp", "seq")),
        ),
        out_specs=P(("grp", "seq"), "mp"),
        check_vma=False,
    )
```

```python
import functools

import jax
import jax.numpy as jnp
from jax import lax
from jax.experimental import pallas as pl
from jax.experimental.pallas import tpu as pltpu
from jax.sharding import PartitionSpec as P

HEAD = 128
GROUP = 8

epsilon = 1e-06


def params(mib):
    return pltpu.CompilerParams(vmem_limit_bytes=mib << 20)


def cost(flops, nbytes):
    return pl.CostEstimate(flops=flops, bytes_accessed=nbytes, transcendentals=0)


def nt_dot(a, b):
    return lax.dot_general(a, b, (((1,), (1,)), ((), ())), preferred_element_type=jnp.float32)


def dot(a, b):
    return jnp.dot(a, b, preferred_element_type=jnp.float32)


SMEM = pl.BlockSpec(memory_space=pltpu.SMEM)
VMEM = pl.BlockSpec(memory_space=pltpu.VMEM)
HBM = pl.BlockSpec(memory_space=pltpu.HBM)


def in_hbm(array):
    return pltpu.with_memory_space_constraint(array, pltpu.HBM)


def squares_kernel(frames_ref, out_ref, held_ref, arrived):
    chunks, columns = arrived.shape[0], frames_ref.shape[1]
    wide = columns // chunks
    copies = []
    for chunk in range(chunks):
        part = (slice(None), pl.ds(chunk * wide, wide))
        copies.append(
            pltpu.make_async_copy(frames_ref.at[part], held_ref.at[part], arrived.at[chunk])
        )
        copies[-1].start()
    total = None
    for chunk in range(chunks):
        copies[chunk].wait()
        for at in range(chunk * wide, (chunk + 1) * wide, HEAD):
            part = held_ref[:, at : at + HEAD].astype(jnp.float32)
            part = part * part
            total = part if total is None else total + part
    out_ref[...] = total


def partial_squares(frames):
    rows, columns = frames.shape
    chunks = 2 if columns % (2 * HEAD) == 0 else 1
    return pl.pallas_call(
        squares_kernel,
        out_shape=(jax.ShapeDtypeStruct((rows, HEAD), jnp.float32), jax.ShapeDtypeStruct(frames.shape, frames.dtype)),
        in_specs=[HBM],
        out_specs=(VMEM, VMEM),
        scratch_shapes=[pltpu.SemaphoreType.DMA((chunks,))],
        compiler_params=params(8),
        cost_estimate=cost(2 * rows * columns, 2 * rows * columns),
        name="partial_squares",
    )(in_hbm(frames))


def products(normed_ref, half, key_ref, value_ref, out_ref):
    width = key_ref.shape[1] // 2
    columns = pl.ds(pl.multiple_of(half * width, width), width)
    out_ref[:, :width] = dot(normed_ref[...], key_ref[:, columns])
    out_ref[:, width:] = dot(normed_ref[...], value_ref[:, columns])


def send_kernel(
    features, index_ref, frames_ref, own_ref, other_ref, gain_ref, key_ref, value_ref, normed_ref, out_ref
):
    squares = jnp.sum(own_ref[...] + other_ref[...], axis=1, keepdims=True)
    inverse_rms = lax.rsqrt(squares / features + epsilon)
    normed_ref[...] = (
        frames_ref[...].astype(jnp.float32) * inverse_rms * gain_ref[...]
    ).astype(jnp.bfloat16)
    products(normed_ref, 1 - index_ref[0], key_ref, value_ref, out_ref)


def send_products(index, frames, own, other, gain, key, value, features):
    rows, columns = frames.shape
    width = key.shape[1]
    return pl.pallas_call(
        functools.partial(send_kernel, features),
        out_shape=(
            jax.ShapeDtypeStruct(frames.shape, jnp.bfloat16),
            jax.ShapeDtypeStruct((rows, width), jnp.float32),
        ),
        in_specs=[SMEM] + [VMEM] * 6,
        out_specs=(VMEM, VMEM),
        compiler_params=params(16),
        cost_estimate=cost(2 * rows * columns * width, 2 * key.size),
        name="send_products",
    )(index, frames, own, other, gain, key, value)


def keep_kernel(index_ref, normed_ref, key_ref, value_ref, out_ref):
    products(normed_ref, index_ref[0], key_ref, value_ref, out_ref)


def keep_products(index, normed, key, value):
    rows, columns = normed.shape
    width = key.shape[1]
    return pl.pallas_call(
        keep_kernel,
        out_shape=jax.ShapeDtypeStruct((rows, width), jnp.float32),
        in_specs=[SMEM] + [VMEM] * 3,
        out_specs=VMEM,
        compiler_params=params(16),
        cost_estimate=cost(2 * rows * columns * width, 2 * key.size),
        name="keep_products",
    )(index, normed, key, value)


def max_bits(masks):
    return functools.reduce(lambda a, b: a | b, masks)


def stage_masks(groups, members):
    if groups & (groups - 1) or members & (members - 1) or members < 4:
        return None
    near = sorted((g * members + m for g in range(groups) for m in range(2)), reverse=True)
    far = sorted(range(0, members, 2), reverse=True)
    return (0, *near[:-1]), (0, far[0], *far[-2:0:-1])


def route(per_shard, capacity, stages, here, session, pick_ref, ids_ref):
    slots, rows = pick_ref.shape
    partitions = slots // capacity
    near, far = stages
    target = lax.div(session, per_shard)
    local = session - target * per_shard
    apart = target ^ here
    step = [
        sum(jnp.where((apart & max_bits(masks)) == mask, at, 0) for at, mask in enumerate(masks))
        for masks in stages
    ]
    leaves = step[0] * len(far) + step[1]
    lands = step[1] * len(near) + step[0]
    to = lax.broadcasted_iota(jnp.int32, (partitions, rows), 0) == leaves
    to = to.astype(jnp.float32)
    earlier = lax.broadcasted_iota(jnp.int32, (rows, rows), 0) < lax.broadcasted_iota(
        jnp.int32, (rows, rows), 1
    )
    ahead = dot(to.astype(jnp.bfloat16), earlier.astype(jnp.bfloat16))
    order = jnp.sum(to * ahead, axis=0, keepdims=True).astype(jnp.int32)
    place = lax.broadcasted_iota(jnp.int32, (slots, rows), 0)
    pick_ref[...] = (place == leaves * capacity + order).astype(jnp.bfloat16)
    lane = lands * capacity + order
    parts = slots // HEAD
    block = lax.broadcasted_iota(jnp.int32, (partitions * parts, rows), 0)
    named = block == leaves * parts + lane // HEAD
    named = jnp.where(named, (local + 1).astype(jnp.float32), 0.0).astype(jnp.bfloat16)
    spot = lax.broadcasted_iota(jnp.int32, (HEAD, rows), 0) == lane % HEAD
    ids_ref[...] = nt_dot(named, spot.astype(jnp.bfloat16))


def queries_of(queries_ref, head):
    columns = [
        queries_ref[:, at * HEAD : (at + 1) * HEAD].astype(jnp.float32)
        for at in range(head * GROUP, (head + 1) * GROUP)
    ]
    return jnp.concatenate(columns, axis=0).astype(jnp.bfloat16)


def score_cache(start_ref, len_ref, queries_ref, key_ref, out_ref, laid_ref):
    sessions, window, width = key_ref.shape
    heads, rows = width // HEAD, GROUP * sessions

    def by_row(ref):
        mine = lax.broadcasted_iota(jnp.int32, (rows, sessions), 0) % sessions
        mine = mine == lax.broadcasted_iota(jnp.int32, (rows, sessions), 1)
        values = jnp.where(mine, ref[...].astype(jnp.float32), 0.0)
        return jnp.sum(values, axis=1, keepdims=True).astype(jnp.int32)

    since = lax.broadcasted_iota(jnp.int32, (rows, window), 1) - by_row(start_ref)
    since = jnp.where(since < 0, since + window, since)
    live = since < by_row(len_ref)
    row_session = lax.broadcasted_iota(jnp.int32, (rows, window), 0) % sessions
    laid_ref[...] = jnp.zeros_like(laid_ref)
    for head in range(heads):
        query = queries_of(queries_ref, head)
        laid_ref[head * rows : (head + 1) * rows, head * HEAD : (head + 1) * HEAD] = query
        total = jnp.zeros((rows, window), jnp.float32)
        for session in range(sessions):
            key = key_ref[session, :, head * HEAD : (head + 1) * HEAD]
            total = jnp.where(row_session == session, nt_dot(query, key), total)
        total = jnp.where(live, total * (HEAD**-0.5), -jnp.inf)
        out_ref[head * rows : (head + 1) * rows] = total


def beside_kernel(
    per_shard,
    capacity,
    stages,
    here_ref,
    session_ref,
    w_key_ref,
    w_value_ref,
    held_key_ref,
    held_value_ref,
    pick_ref,
    ids_ref,
    session,
    arrived,
):
    copies = []
    for at, (source, held) in enumerate(
        (
            (session_ref, session),
            (w_key_ref, held_key_ref),
            (w_value_ref, held_value_ref),
        )
    ):
        copies.append(pltpu.make_async_copy(source, held, arrived.at[at]))
        copies[-1].start()
    copies[0].wait()
    route(per_shard, capacity, stages, here_ref[0], session[...], pick_ref, ids_ref)
    for copy in copies[1:]:
        copy.wait()


def beside(here, session, w_key, w_value, sizes):
    partitions, per_shard, capacity, stages = sizes
    slots, rows = partitions * capacity, session.shape[1]
    return pl.pallas_call(
        functools.partial(beside_kernel, per_shard, capacity, stages),
        out_shape=(
            jax.ShapeDtypeStruct(w_key.shape, w_key.dtype),
            jax.ShapeDtypeStruct(w_value.shape, w_value.dtype),
            jax.ShapeDtypeStruct((slots, rows), jnp.bfloat16),
            jax.ShapeDtypeStruct((partitions * slots // HEAD, HEAD), jnp.float32),
        ),
        in_specs=[SMEM] + [HBM] * 3,
        out_specs=(VMEM,) * 4,
        scratch_shapes=[pltpu.VMEM(session.shape, session.dtype), pltpu.SemaphoreType.DMA((3,))],
        compiler_params=params(24),
        cost_estimate=cost(4 * rows * rows * slots, 4 * w_key.size),
        name="beside",
    )(here, in_hbm(session), in_hbm(w_key), in_hbm(w_value))


def cached_scores(start, length, queries, cache_key):
    sessions, window, width = cache_key.shape
    rows = width // HEAD * GROUP * sessions
    return pl.pallas_call(
        score_cache,
        out_shape=(
            jax.ShapeDtypeStruct((rows, window), jnp.float32),
            jax.ShapeDtypeStruct((rows, width), jnp.bfloat16),
        ),
        in_specs=[VMEM] * 4,
        out_specs=(VMEM, VMEM),
        compiler_params=params(8),
        cost_estimate=cost(2 * GROUP * sessions * cache_key.size, 2 * cache_key.size),
        name="cached_scores",
    )(start, length, queries, cache_key)


def pack_kernel(pick_ref, ids_ref, kept_ref, got_ref, key_bias_ref, value_bias_ref, *out_refs):
    width = key_bias_ref.shape[1]
    sums = kept_ref[...] + got_ref[...]
    key = (sums[:, :width] + key_bias_ref[...]).astype(jnp.bfloat16)
    value = (sums[:, width:] + value_bias_ref[...]).astype(jnp.bfloat16)
    tall = pick_ref.shape[0] // len(out_refs)
    at = 0
    for source in (key, value):
        laid = dot(pick_ref[...], source).astype(jnp.bfloat16)
        for column in range(0, width, HEAD):
            for step, out_ref in enumerate(out_refs):
                out_ref[at : at + tall, :] = laid[
                    step * tall : (step + 1) * tall, column : column + HEAD
                ]
            at += tall
    named = ids_ref.shape[0] // len(out_refs)
    for step, out_ref in enumerate(out_refs):
        out_ref[at:, :] = ids_ref[step * named : (step + 1) * named, :].astype(jnp.bfloat16)


def pack(pick, ids, kept, got, key_bias, value_bias, near):
    rows, width = kept.shape
    slots = pick.shape[0]
    tall = (width // HEAD * slots + ids.shape[0]) // near
    return pl.pallas_call(
        pack_kernel,
        out_shape=[jax.ShapeDtypeStruct((tall, HEAD), jnp.bfloat16)] * near,
        in_specs=[VMEM] * 6,
        out_specs=[VMEM] * near,
        compiler_params=params(8),
        cost_estimate=cost(2 * rows * width * slots, 8 * rows * width),
        name="pack",
    )(pick, ids, kept, got, key_bias, value_bias)


def regroup_kernel(near, vectors, capacity, *refs):
    got_refs, out_refs = refs[:near], refs[near:]
    far = len(out_refs)
    for vector in range(vectors):
        for step, out_ref in enumerate(out_refs):
            for first, got_ref in enumerate(got_refs):
                to, at = (vector * near + first) * capacity, (vector * far + step) * capacity
                out_ref[to : to + capacity, :] = got_ref[at : at + capacity, :]
    ids = sum(ref[vectors * far * capacity :, :].astype(jnp.float32) for ref in got_refs)
    for out_ref in out_refs:
        out_ref[vectors * near * capacity :, :] = ids.astype(jnp.bfloat16)


def regroup(blocks, far, vectors, capacity):
    near = len(blocks)
    tall = blocks[0].shape[0] + vectors * capacity * (near - far)
    return pl.pallas_call(
        functools.partial(regroup_kernel, near, vectors, capacity),
        out_shape=[jax.ShapeDtypeStruct((tall, HEAD), jnp.bfloat16)] * far,
        in_specs=[VMEM] * near,
        out_specs=[VMEM] * far,
        compiler_params=params(8),
        cost_estimate=cost(0, 4 * near * blocks[0].size),
        name="regroup",
    )(*blocks)


def attend_kernel(near, capacity, queries_ref, score_ref, cache_ref, *refs):
    *got_refs, out_ref = refs
    rows, window = score_ref.shape
    sessions, _, width = cache_ref.shape
    heads = width // HEAD
    tall = near * capacity
    slots = len(got_refs) * tall
    parts = slots // HEAD
    ids = [
        sum(
            ref[2 * heads * tall :, :].astype(jnp.float32)[step * parts + part : step * parts + part + 1]
            for step, ref in enumerate(got_refs)
        )
        for part in range(parts)
    ]
    ids = jnp.concatenate(ids, axis=1).astype(jnp.int32)
    own = lax.broadcasted_iota(jnp.int32, (rows, slots), 0) % sessions + 1 == ids

    def rows_of(vectors):
        columns = []
        for vector in vectors:
            part = slice(vector * tall, (vector + 1) * tall)
            columns.append(jnp.concatenate([ref[part, :] for ref in got_refs], axis=0))
        return jnp.concatenate(columns, axis=1)

    cached = score_ref[...]
    fresh = nt_dot(queries_ref[...], rows_of(range(heads))) * (HEAD**-0.5)
    fresh = jnp.where(own, fresh, -jnp.inf)
    largest = jnp.maximum(
        jnp.max(cached, axis=1, keepdims=True), jnp.max(fresh, axis=1, keepdims=True)
    )
    cached = jnp.exp(cached - largest)
    fresh = jnp.exp(fresh - largest)
    total = jnp.sum(cached, axis=1, keepdims=True) + jnp.sum(fresh, axis=1, keepdims=True)
    cached = cached / total
    attended = dot((fresh / total).astype(jnp.bfloat16), rows_of(range(heads, 2 * heads)))
    row_session = lax.broadcasted_iota(jnp.int32, (rows, window), 0) % sessions
    for session in range(0, sessions, 2):
        weights = jnp.concatenate(
            [jnp.where(row_session == session + more, cached, 0.0) for more in range(2)], axis=1
        )
        values = cache_ref[session : session + 2].reshape(2 * window, width)
        attended += dot(weights.astype(jnp.bfloat16), values)
    for head in range(heads):
        for q in range(GROUP):
            row, column = (head * GROUP + q) * sessions, (head * GROUP + q) * HEAD
            out_ref[:, column : column + HEAD] = attended[
                row : row + sessions, head * HEAD : (head + 1) * HEAD
            ].astype(jnp.bfloat16)


def attend(got, queries, scores, cache_value, near, capacity):
    return pl.pallas_call(
        functools.partial(attend_kernel, near, capacity),
        out_shape=jax.ShapeDtypeStruct(
            (cache_value.shape[0], queries.shape[1] * GROUP), jnp.bfloat16
        ),
        in_specs=[VMEM] * (3 + len(got)),
        out_specs=VMEM,
        compiler_params=params(8),
        cost_estimate=cost(4 * queries.shape[0] * cache_value.size, 2 * cache_value.size),
        name="attend",
    )(queries, scores, cache_value, *got)


def project(frame_rows, ln_gain, w_key, w_value, k_bias, v_bias):
    values32 = frame_rows.astype(jnp.float32)
    partial_squares = jnp.sum(values32 * values32, axis=1)
    squares = lax.psum(partial_squares, "mp")
    inverse_rms = lax.rsqrt(squares / (frame_rows.shape[1] * lax.axis_size("mp")) + epsilon)
    normed = (values32 * inverse_rms[:, None] * ln_gain[None, :]).astype(jnp.bfloat16)
    part_key = jnp.dot(normed, w_key, preferred_element_type=jnp.float32)
    part_value = jnp.dot(normed, w_value, preferred_element_type=jnp.float32)
    key_sums, value_sums = (
        lax.psum_scatter(part_key, "mp", scatter_dimension=1, tiled=True),
        lax.psum_scatter(part_value, "mp", scatter_dimension=1, tiled=True),
    )
    new_keys = (key_sums + k_bias[None, :]).astype(jnp.bfloat16)
    new_values = (value_sums + v_bias[None, :]).astype(jnp.bfloat16)
    return (new_keys, new_values)


def slot_sources(token_session, per_shard, partition_count, capacity):
    row_count = token_session.shape[0]
    target = token_session // per_shard
    one_hot = (target[:, None] == jnp.arange(partition_count, dtype=jnp.int32)[None, :]).astype(
        jnp.int32
    )
    order_in = jnp.sum((jnp.cumsum(one_hot, axis=0) - one_hot) * one_hot, axis=1)
    slot_index = target * capacity + order_in
    matches = (
        slot_index[None, :] == jnp.arange(partition_count * capacity, dtype=jnp.int32)[:, None]
    )
    source = jnp.sum(jnp.where(matches, jnp.arange(row_count, dtype=jnp.int32)[None, :], 0), axis=1)
    filled = jnp.any(matches, axis=1)
    sessions = jnp.where(filled, jnp.mod(token_session[source], per_shard), -1)
    return (source, filled, sessions)


def general(
    frames,
    token_session,
    ln_gain,
    w_key,
    w_value,
    k_bias,
    v_bias,
    queries,
    cache_key,
    cache_value,
    cache_start,
    cache_len,
):
    partition_count = lax.axis_size(("grp", "seq"))
    per_shard = queries.shape[0]
    rows_here = frames.shape[0]
    capacity = max(2, 5 * rows_here // (2 * partition_count) + 1)
    source, filled, sessions = slot_sources(token_session, per_shard, partition_count, capacity)
    session_slots = sessions.reshape(partition_count, capacity)
    nothing = jnp.zeros((), jnp.bfloat16)
    own_keys, own_values = project(frames, ln_gain, w_key, w_value, k_bias, v_bias)
    send_keys = jnp.where(filled[:, None], own_keys[source], nothing).reshape(
        partition_count, capacity, -1
    )
    send_values = jnp.where(filled[:, None], own_values[source], nothing).reshape(
        partition_count, capacity, -1
    )
    got_keys, got_values, got_sessions = (
        lax.all_to_all(send_keys, ("grp", "seq"), split_axis=0, concat_axis=0, tiled=True),
        lax.all_to_all(send_values, ("grp", "seq"), split_axis=0, concat_axis=0, tiled=True),
        lax.all_to_all(session_slots, ("grp", "seq"), split_axis=0, concat_axis=0, tiled=True),
    )
    new_keys = got_keys.reshape(partition_count * capacity, -1)
    new_values = got_values.reshape(partition_count * capacity, -1)
    new_sessions = got_sessions.reshape(-1)
    heads_kv = new_keys.shape[1] // HEAD
    window = cache_key.shape[1]
    score_scale = HEAD ** (-0.5)
    query_heads = queries.reshape(per_shard, heads_kv, GROUP, HEAD)
    cached_keys = cache_key.reshape(per_shard, window, heads_kv, HEAD)
    cached_values = cache_value.reshape(per_shard, window, heads_kv, HEAD)
    fresh_keys = new_keys.reshape(-1, heads_kv, HEAD)
    fresh_values = new_values.reshape(-1, heads_kv, HEAD)
    cached_scores = (
        jnp.einsum("sghd,swgd->sghw", query_heads, cached_keys, preferred_element_type=jnp.float32)
        * score_scale
    )
    positions = jnp.arange(window, dtype=jnp.int32)
    live_slots = jnp.mod(positions[None, :] - cache_start[:, None], window) < cache_len[:, None]
    cached_scores = jnp.where(live_slots[:, None, None, :], cached_scores, -jnp.inf)
    fresh_scores = (
        jnp.einsum("sghd,ngd->sghn", query_heads, fresh_keys, preferred_element_type=jnp.float32)
        * score_scale
    )
    own_rows = new_sessions[None, :] == jnp.arange(per_shard, dtype=jnp.int32)[:, None]
    fresh_scores = jnp.where(own_rows[:, None, None, :], fresh_scores, -jnp.inf)
    largest = jnp.maximum(jnp.max(cached_scores, axis=3), jnp.max(fresh_scores, axis=3))
    cached_exp = jnp.exp(cached_scores - largest[..., None])
    fresh_exp = jnp.exp(fresh_scores - largest[..., None])
    totals = jnp.sum(cached_exp, axis=3) + jnp.sum(fresh_exp, axis=3)
    cached_weights = (cached_exp / totals[..., None]).astype(jnp.bfloat16)
    fresh_weights = (fresh_exp / totals[..., None]).astype(jnp.bfloat16)
    attended = jnp.einsum(
        "sghw,swgd->sghd", cached_weights, cached_values, preferred_element_type=jnp.float32
    )
    attended = attended + jnp.einsum(
        "sghn,ngd->sghd", fresh_weights, fresh_values, preferred_element_type=jnp.float32
    )
    return attended.reshape(per_shard, -1).astype(jnp.bfloat16)


def local(
    frames,
    token_session,
    ln_gain,
    w_key,
    w_value,
    k_bias,
    v_bias,
    queries,
    cache_key,
    cache_value,
    cache_start,
    cache_len,
):
    partitions = lax.axis_size(("grp", "seq"))
    shares = lax.axis_size("mp")
    per_shard = queries.shape[0]
    rows = frames.shape[0]
    capacity = max(2, 5 * rows // (2 * partitions) + 1)
    stages = stage_masks(lax.axis_size("grp"), lax.axis_size("seq"))
    if stages is None or shares != 2 or per_shard % 8 or capacity % 16 or partitions * capacity % HEAD:
        return general(
            frames, token_session, ln_gain, w_key, w_value, k_bias, v_bias, queries, cache_key, cache_value,
            cache_start, cache_len,
        )
    swap = [(0, 1), (1, 0)]
    index = lax.axis_index("mp").astype(jnp.int32).reshape(1)
    here = lax.axis_index(("grp", "seq")).astype(jnp.int32).reshape(1)
    own, held = partial_squares(frames)
    other = lax.ppermute(own, "mp", swap)
    held_key, held_value, pick, ids = beside(
        here, token_session[None, :], w_key, w_value, (partitions, per_shard, capacity, stages)
    )
    normed, sent = send_products(
        index, held, own, other, ln_gain[None, :], held_key, held_value, frames.shape[1] * shares
    )
    arrived = lax.ppermute(sent, "mp", swap)
    kept = keep_products(index, normed, held_key, held_value)
    blocks = pack(pick, ids, kept, arrived, k_bias[None, :], v_bias[None, :], len(stages[0]))

    def step(arrays, masks):
        pairs = [[(i, i ^ mask) for i in range(partitions)] for mask in masks]
        sent = [lax.ppermute(a, ("grp", "seq"), p) for a, p in zip(arrays[1:], pairs[1:])]
        return [arrays[0], *sent]

    near, far = stages
    vectors = 2 * cache_key.shape[2] // HEAD
    queries, *blocks = lax.optimization_barrier((queries, *blocks))
    scores, laid = cached_scores(cache_start[None, :], cache_len[None, :], queries, cache_key)
    mid = regroup(step(blocks, near), len(far), vectors, capacity)
    return attend(step(mid, far), laid, scores, cache_value, len(near), capacity)


def solution(mesh):
    return jax.shard_map(
        local,
        mesh=mesh,
        in_specs=(
            P(("grp", "seq"), "mp"),
            P(("grp", "seq")),
            P("mp"),
            P("mp", None),
            P("mp", None),
            P("mp"),
            P("mp"),
            P(("grp", "seq"), "mp"),
            P(("grp", "seq"), None, "mp"),
            P(("grp", "seq"), None, "mp"),
            P(("grp", "seq")),
            P(("grp", "seq")),
        ),
        out_specs=P(("grp", "seq"), "mp"),
        check_vma=False,
    )
```

```python
import functools

import jax
import jax.numpy as jnp
from jax import lax
from jax.experimental import pallas as pl
from jax.experimental.pallas import tpu as pltpu
from jax.sharding import PartitionSpec as P

HEAD = 128
GROUP = 8

epsilon = 1e-06


def params(mib):
    return pltpu.CompilerParams(vmem_limit_bytes=mib << 20)


def cost(flops, nbytes):
    return pl.CostEstimate(flops=flops, bytes_accessed=nbytes, transcendentals=0)


def nt_dot(a, b):
    return lax.dot_general(a, b, (((1,), (1,)), ((), ())), preferred_element_type=jnp.float32)


def dot(a, b):
    return jnp.dot(a, b, preferred_element_type=jnp.float32)


SMEM = pl.BlockSpec(memory_space=pltpu.SMEM)
VMEM = pl.BlockSpec(memory_space=pltpu.VMEM)
HBM = pl.BlockSpec(memory_space=pltpu.HBM)


def in_hbm(array):
    return pltpu.with_memory_space_constraint(array, pltpu.HBM)


def squares_kernel(frames_ref, out_ref, held_ref, arrived):
    chunks, columns = arrived.shape[0], frames_ref.shape[1]
    wide = columns // chunks
    copies = []
    for chunk in range(chunks):
        part = (slice(None), pl.ds(chunk * wide, wide))
        copies.append(
            pltpu.make_async_copy(frames_ref.at[part], held_ref.at[part], arrived.at[chunk])
        )
        copies[-1].start()
    total = None
    for chunk in range(chunks):
        copies[chunk].wait()
        for at in range(chunk * wide, (chunk + 1) * wide, HEAD):
            part = held_ref[:, at : at + HEAD].astype(jnp.float32)
            part = part * part
            total = part if total is None else total + part
    out_ref[...] = total


def partial_squares(frames):
    rows, columns = frames.shape
    chunks = 2 if columns % (2 * HEAD) == 0 else 1
    return pl.pallas_call(
        squares_kernel,
        out_shape=(
            jax.ShapeDtypeStruct((rows, HEAD), jnp.float32),
            jax.ShapeDtypeStruct(frames.shape, frames.dtype),
        ),
        in_specs=[HBM],
        out_specs=(VMEM, VMEM),
        scratch_shapes=[pltpu.SemaphoreType.DMA((chunks,))],
        compiler_params=params(8),
        cost_estimate=cost(2 * rows * columns, 2 * rows * columns),
        name="partial_squares",
    )(in_hbm(frames))


def products(normed_ref, half, key_ref, value_ref, out_ref):
    width = key_ref.shape[1] // 2
    columns = pl.ds(pl.multiple_of(half * width, width), width)
    out_ref[:, :width] = dot(normed_ref[...], key_ref[:, columns])
    out_ref[:, width:] = dot(normed_ref[...], value_ref[:, columns])


def send_kernel(
    features, index_ref, frames_ref, own_ref, other_ref, gain_ref, key_ref, value_ref, normed_ref, out_ref
):
    squares = jnp.sum(own_ref[...] + other_ref[...], axis=1, keepdims=True)
    inverse_rms = lax.rsqrt(squares / features + epsilon)
    normed_ref[...] = (
        frames_ref[...].astype(jnp.float32) * inverse_rms * gain_ref[...]
    ).astype(jnp.bfloat16)
    products(normed_ref, 1 - index_ref[0], key_ref, value_ref, out_ref)


def send_products(index, frames, own, other, gain, key, value, features):
    rows, columns = frames.shape
    width = key.shape[1]
    return pl.pallas_call(
        functools.partial(send_kernel, features),
        out_shape=(
            jax.ShapeDtypeStruct(frames.shape, jnp.bfloat16),
            jax.ShapeDtypeStruct((rows, width), jnp.float32),
        ),
        in_specs=[SMEM] + [VMEM] * 6,
        out_specs=(VMEM, VMEM),
        compiler_params=params(16),
        cost_estimate=cost(2 * rows * columns * width, 2 * key.size),
        name="send_products",
    )(index, frames, own, other, gain, key, value)


def keep_kernel(index_ref, normed_ref, key_ref, value_ref, out_ref):
    products(normed_ref, index_ref[0], key_ref, value_ref, out_ref)


def keep_products(index, normed, key, value):
    rows, columns = normed.shape
    width = key.shape[1]
    return pl.pallas_call(
        keep_kernel,
        out_shape=jax.ShapeDtypeStruct((rows, width), jnp.float32),
        in_specs=[SMEM] + [VMEM] * 3,
        out_specs=VMEM,
        compiler_params=params(16),
        cost_estimate=cost(2 * rows * columns * width, 2 * key.size),
        name="keep_products",
    )(index, normed, key, value)


def max_bits(masks):
    return functools.reduce(lambda a, b: a | b, masks)


def stage_masks(groups, members):
    if groups & (groups - 1) or members & (members - 1) or members < 4:
        return None
    near = sorted((g * members + m for g in range(groups) for m in range(2)), reverse=True)
    far = sorted(range(0, members, 2), reverse=True)
    return tuple((0, masks[0], *masks[-2:0:-1]) for masks in (near, far))


def route(per_shard, capacity, stages, here, session, pick_ref, ids_ref):
    slots, rows = pick_ref.shape
    partitions = slots // capacity
    near, far = stages
    target = lax.div(session, per_shard)
    local = session - target * per_shard
    apart = target ^ here
    step = [
        sum(jnp.where((apart & max_bits(masks)) == mask, at, 0) for at, mask in enumerate(masks))
        for masks in stages
    ]
    leaves = step[0] * len(far) + step[1]
    lands = step[1] * len(near) + step[0]
    to = lax.broadcasted_iota(jnp.int32, (partitions, rows), 0) == leaves
    to = to.astype(jnp.float32)
    earlier = lax.broadcasted_iota(jnp.int32, (rows, rows), 0) < lax.broadcasted_iota(
        jnp.int32, (rows, rows), 1
    )
    ahead = dot(to.astype(jnp.bfloat16), earlier.astype(jnp.bfloat16))
    order = jnp.sum(to * ahead, axis=0, keepdims=True).astype(jnp.int32)
    place = lax.broadcasted_iota(jnp.int32, (slots, rows), 0)
    pick_ref[...] = (place == leaves * capacity + order).astype(jnp.bfloat16)
    lane = lands * capacity + order
    parts = slots // HEAD
    block = lax.broadcasted_iota(jnp.int32, (partitions * parts, rows), 0)
    named = block == leaves * parts + lane // HEAD
    named = jnp.where(named, (local + 1).astype(jnp.float32), 0.0).astype(jnp.bfloat16)
    spot = lax.broadcasted_iota(jnp.int32, (HEAD, rows), 0) == lane % HEAD
    ids_ref[...] = nt_dot(named, spot.astype(jnp.bfloat16))


def queries_of(queries_ref, head):
    columns = [
        queries_ref[:, at * HEAD : (at + 1) * HEAD].astype(jnp.float32)
        for at in range(head * GROUP, (head + 1) * GROUP)
    ]
    return jnp.concatenate(columns, axis=0).astype(jnp.bfloat16)


def score_cache(start_ref, len_ref, queries_ref, key_ref, out_ref, laid_ref):
    sessions, window, width = key_ref.shape
    heads, rows = width // HEAD, GROUP * sessions

    def by_row(ref):
        mine = lax.broadcasted_iota(jnp.int32, (rows, sessions), 0) % sessions
        mine = mine == lax.broadcasted_iota(jnp.int32, (rows, sessions), 1)
        values = jnp.where(mine, ref[...].astype(jnp.float32), 0.0)
        return jnp.sum(values, axis=1, keepdims=True).astype(jnp.int32)

    since = lax.broadcasted_iota(jnp.int32, (rows, window), 1) - by_row(start_ref)
    since = jnp.where(since < 0, since + window, since)
    live = since < by_row(len_ref)
    row_session = lax.broadcasted_iota(jnp.int32, (rows, window), 0) % sessions
    laid_ref[...] = jnp.zeros_like(laid_ref)
    for head in range(heads):
        query = queries_of(queries_ref, head)
        laid_ref[head * rows : (head + 1) * rows, head * HEAD : (head + 1) * HEAD] = query
        total = jnp.zeros((rows, window), jnp.float32)
        for session in range(sessions):
            key = key_ref[session, :, head * HEAD : (head + 1) * HEAD]
            total = jnp.where(row_session == session, nt_dot(query, key), total)
        total = jnp.where(live, total * (HEAD**-0.5), -jnp.inf)
        out_ref[head * rows : (head + 1) * rows] = total


def beside_kernel(
    per_shard,
    capacity,
    stages,
    here_ref,
    session_ref,
    w_key_ref,
    w_value_ref,
    held_key_ref,
    held_value_ref,
    pick_ref,
    ids_ref,
    session,
    arrived,
):
    copies = []
    for at, (source, held) in enumerate(
        (
            (session_ref, session),
            (w_key_ref, held_key_ref),
            (w_value_ref, held_value_ref),
        )
    ):
        copies.append(pltpu.make_async_copy(source, held, arrived.at[at]))
        copies[-1].start()
    copies[0].wait()
    route(per_shard, capacity, stages, here_ref[0], session[...], pick_ref, ids_ref)
    for copy in copies[1:]:
        copy.wait()


def beside(here, session, w_key, w_value, sizes):
    partitions, per_shard, capacity, stages = sizes
    slots, rows = partitions * capacity, session.shape[1]
    return pl.pallas_call(
        functools.partial(beside_kernel, per_shard, capacity, stages),
        out_shape=(
            jax.ShapeDtypeStruct(w_key.shape, w_key.dtype),
            jax.ShapeDtypeStruct(w_value.shape, w_value.dtype),
            jax.ShapeDtypeStruct((slots, rows), jnp.bfloat16),
            jax.ShapeDtypeStruct((partitions * slots // HEAD, HEAD), jnp.float32),
        ),
        in_specs=[SMEM] + [HBM] * 3,
        out_specs=(VMEM,) * 4,
        scratch_shapes=[pltpu.VMEM(session.shape, session.dtype), pltpu.SemaphoreType.DMA((3,))],
        compiler_params=params(24),
        cost_estimate=cost(4 * rows * rows * slots, 4 * w_key.size),
        name="beside",
    )(here, in_hbm(session), in_hbm(w_key), in_hbm(w_value))


def cached_scores(start, length, queries, cache_key):
    sessions, window, width = cache_key.shape
    rows = width // HEAD * GROUP * sessions
    return pl.pallas_call(
        score_cache,
        out_shape=(
            jax.ShapeDtypeStruct((rows, window), jnp.float32),
            jax.ShapeDtypeStruct((rows, width), jnp.bfloat16),
        ),
        in_specs=[VMEM] * 4,
        out_specs=(VMEM, VMEM),
        compiler_params=params(8),
        cost_estimate=cost(2 * GROUP * sessions * cache_key.size, 2 * cache_key.size),
        name="cached_scores",
    )(start, length, queries, cache_key)


def pack_kernel(pick_ref, ids_ref, kept_ref, got_ref, key_bias_ref, value_bias_ref, *out_refs):
    width = key_bias_ref.shape[1]
    sums = kept_ref[...] + got_ref[...]
    key = (sums[:, :width] + key_bias_ref[...]).astype(jnp.bfloat16)
    value = (sums[:, width:] + value_bias_ref[...]).astype(jnp.bfloat16)
    tall = pick_ref.shape[0] // len(out_refs)
    at = 0
    for source in (key, value):
        laid = dot(pick_ref[...], source).astype(jnp.bfloat16)
        for column in range(0, width, HEAD):
            for step, out_ref in enumerate(out_refs):
                out_ref[at : at + tall, :] = laid[
                    step * tall : (step + 1) * tall, column : column + HEAD
                ]
            at += tall
    named = ids_ref.shape[0] // len(out_refs)
    for step, out_ref in enumerate(out_refs):
        out_ref[at:, :] = ids_ref[step * named : (step + 1) * named, :].astype(jnp.bfloat16)


def pack(pick, ids, kept, got, key_bias, value_bias, near):
    rows, width = kept.shape
    slots = pick.shape[0]
    tall = (width // HEAD * slots + ids.shape[0]) // near
    return pl.pallas_call(
        pack_kernel,
        out_shape=[jax.ShapeDtypeStruct((tall, HEAD), jnp.bfloat16)] * near,
        in_specs=[VMEM] * 6,
        out_specs=[VMEM] * near,
        compiler_params=params(8),
        cost_estimate=cost(2 * rows * width * slots, 8 * rows * width),
        name="pack",
    )(pick, ids, kept, got, key_bias, value_bias)


def regroup_kernel(near, vectors, capacity, *refs):
    got_refs, out_refs = refs[:near], refs[near:]
    far = len(out_refs)
    for vector in range(vectors):
        for step, out_ref in enumerate(out_refs):
            for first, got_ref in enumerate(got_refs):
                to, at = (vector * near + first) * capacity, (vector * far + step) * capacity
                out_ref[to : to + capacity, :] = got_ref[at : at + capacity, :]
    ids = sum(ref[vectors * far * capacity :, :].astype(jnp.float32) for ref in got_refs)
    for out_ref in out_refs:
        out_ref[vectors * near * capacity :, :] = ids.astype(jnp.bfloat16)


def regroup(blocks, far, vectors, capacity):
    near = len(blocks)
    tall = blocks[0].shape[0] + vectors * capacity * (near - far)
    return pl.pallas_call(
        functools.partial(regroup_kernel, near, vectors, capacity),
        out_shape=[jax.ShapeDtypeStruct((tall, HEAD), jnp.bfloat16)] * far,
        in_specs=[VMEM] * near,
        out_specs=[VMEM] * far,
        compiler_params=params(8),
        cost_estimate=cost(0, 4 * near * blocks[0].size),
        name="regroup",
    )(*blocks)


def attend_kernel(near, capacity, queries_ref, score_ref, cache_ref, *refs):
    *got_refs, out_ref = refs
    rows, window = score_ref.shape
    sessions, _, width = cache_ref.shape
    heads = width // HEAD
    tall = near * capacity
    slots = len(got_refs) * tall
    parts = slots // HEAD
    ids = [
        sum(
            ref[2 * heads * tall :, :].astype(jnp.float32)[step * parts + part : step * parts + part + 1]
            for step, ref in enumerate(got_refs)
        )
        for part in range(parts)
    ]
    ids = jnp.concatenate(ids, axis=1).astype(jnp.int32)
    own = lax.broadcasted_iota(jnp.int32, (rows, slots), 0) % sessions + 1 == ids

    def rows_of(vectors):
        columns = []
        for vector in vectors:
            part = slice(vector * tall, (vector + 1) * tall)
            columns.append(jnp.concatenate([ref[part, :] for ref in got_refs], axis=0))
        return jnp.concatenate(columns, axis=1)

    cached = score_ref[...]
    fresh = nt_dot(queries_ref[...], rows_of(range(heads))) * (HEAD**-0.5)
    fresh = jnp.where(own, fresh, -jnp.inf)
    largest = jnp.maximum(
        jnp.max(cached, axis=1, keepdims=True), jnp.max(fresh, axis=1, keepdims=True)
    )
    cached = jnp.exp(cached - largest)
    fresh = jnp.exp(fresh - largest)
    total = jnp.sum(cached, axis=1, keepdims=True) + jnp.sum(fresh, axis=1, keepdims=True)
    cached = cached / total
    attended = dot((fresh / total).astype(jnp.bfloat16), rows_of(range(heads, 2 * heads)))
    row_session = lax.broadcasted_iota(jnp.int32, (rows, window), 0) % sessions
    for session in range(0, sessions, 2):
        weights = jnp.concatenate(
            [jnp.where(row_session == session + more, cached, 0.0) for more in range(2)], axis=1
        )
        values = cache_ref[session : session + 2].reshape(2 * window, width)
        attended += dot(weights.astype(jnp.bfloat16), values)
    for head in range(heads):
        for q in range(GROUP):
            row, column = (head * GROUP + q) * sessions, (head * GROUP + q) * HEAD
            out_ref[:, column : column + HEAD] = attended[
                row : row + sessions, head * HEAD : (head + 1) * HEAD
            ].astype(jnp.bfloat16)


def attend(got, queries, scores, cache_value, near, capacity):
    return pl.pallas_call(
        functools.partial(attend_kernel, near, capacity),
        out_shape=jax.ShapeDtypeStruct(
            (cache_value.shape[0], queries.shape[1] * GROUP), jnp.bfloat16
        ),
        in_specs=[VMEM] * (3 + len(got)),
        out_specs=VMEM,
        compiler_params=params(8),
        cost_estimate=cost(4 * queries.shape[0] * cache_value.size, 2 * cache_value.size),
        name="attend",
    )(queries, scores, cache_value, *got)


def project(frame_rows, ln_gain, w_key, w_value, k_bias, v_bias):
    values32 = frame_rows.astype(jnp.float32)
    partial_squares = jnp.sum(values32 * values32, axis=1)
    squares = lax.psum(partial_squares, "mp")
    inverse_rms = lax.rsqrt(squares / (frame_rows.shape[1] * lax.axis_size("mp")) + epsilon)
    normed = (values32 * inverse_rms[:, None] * ln_gain[None, :]).astype(jnp.bfloat16)
    part_key = jnp.dot(normed, w_key, preferred_element_type=jnp.float32)
    part_value = jnp.dot(normed, w_value, preferred_element_type=jnp.float32)
    key_sums, value_sums = (
        lax.psum_scatter(part_key, "mp", scatter_dimension=1, tiled=True),
        lax.psum_scatter(part_value, "mp", scatter_dimension=1, tiled=True),
    )
    new_keys = (key_sums + k_bias[None, :]).astype(jnp.bfloat16)
    new_values = (value_sums + v_bias[None, :]).astype(jnp.bfloat16)
    return (new_keys, new_values)


def slot_sources(token_session, per_shard, partition_count, capacity):
    row_count = token_session.shape[0]
    target = token_session // per_shard
    one_hot = (target[:, None] == jnp.arange(partition_count, dtype=jnp.int32)[None, :]).astype(
        jnp.int32
    )
    order_in = jnp.sum((jnp.cumsum(one_hot, axis=0) - one_hot) * one_hot, axis=1)
    slot_index = target * capacity + order_in
    matches = (
        slot_index[None, :] == jnp.arange(partition_count * capacity, dtype=jnp.int32)[:, None]
    )
    source = jnp.sum(jnp.where(matches, jnp.arange(row_count, dtype=jnp.int32)[None, :], 0), axis=1)
    filled = jnp.any(matches, axis=1)
    sessions = jnp.where(filled, jnp.mod(token_session[source], per_shard), -1)
    return (source, filled, sessions)


def general(
    frames,
    token_session,
    ln_gain,
    w_key,
    w_value,
    k_bias,
    v_bias,
    queries,
    cache_key,
    cache_value,
    cache_start,
    cache_len,
):
    partition_count = lax.axis_size(("grp", "seq"))
    per_shard = queries.shape[0]
    rows_here = frames.shape[0]
    capacity = max(2, 5 * rows_here // (2 * partition_count) + 1)
    source, filled, sessions = slot_sources(token_session, per_shard, partition_count, capacity)
    session_slots = sessions.reshape(partition_count, capacity)
    nothing = jnp.zeros((), jnp.bfloat16)
    own_keys, own_values = project(frames, ln_gain, w_key, w_value, k_bias, v_bias)
    send_keys = jnp.where(filled[:, None], own_keys[source], nothing).reshape(
        partition_count, capacity, -1
    )
    send_values = jnp.where(filled[:, None], own_values[source], nothing).reshape(
        partition_count, capacity, -1
    )
    got_keys, got_values, got_sessions = (
        lax.all_to_all(send_keys, ("grp", "seq"), split_axis=0, concat_axis=0, tiled=True),
        lax.all_to_all(send_values, ("grp", "seq"), split_axis=0, concat_axis=0, tiled=True),
        lax.all_to_all(session_slots, ("grp", "seq"), split_axis=0, concat_axis=0, tiled=True),
    )
    new_keys = got_keys.reshape(partition_count * capacity, -1)
    new_values = got_values.reshape(partition_count * capacity, -1)
    new_sessions = got_sessions.reshape(-1)
    heads_kv = new_keys.shape[1] // HEAD
    window = cache_key.shape[1]
    score_scale = HEAD ** (-0.5)
    query_heads = queries.reshape(per_shard, heads_kv, GROUP, HEAD)
    cached_keys = cache_key.reshape(per_shard, window, heads_kv, HEAD)
    cached_values = cache_value.reshape(per_shard, window, heads_kv, HEAD)
    fresh_keys = new_keys.reshape(-1, heads_kv, HEAD)
    fresh_values = new_values.reshape(-1, heads_kv, HEAD)
    cached_scores = (
        jnp.einsum("sghd,swgd->sghw", query_heads, cached_keys, preferred_element_type=jnp.float32)
        * score_scale
    )
    positions = jnp.arange(window, dtype=jnp.int32)
    live_slots = jnp.mod(positions[None, :] - cache_start[:, None], window) < cache_len[:, None]
    cached_scores = jnp.where(live_slots[:, None, None, :], cached_scores, -jnp.inf)
    fresh_scores = (
        jnp.einsum("sghd,ngd->sghn", query_heads, fresh_keys, preferred_element_type=jnp.float32)
        * score_scale
    )
    own_rows = new_sessions[None, :] == jnp.arange(per_shard, dtype=jnp.int32)[:, None]
    fresh_scores = jnp.where(own_rows[:, None, None, :], fresh_scores, -jnp.inf)
    largest = jnp.maximum(jnp.max(cached_scores, axis=3), jnp.max(fresh_scores, axis=3))
    cached_exp = jnp.exp(cached_scores - largest[..., None])
    fresh_exp = jnp.exp(fresh_scores - largest[..., None])
    totals = jnp.sum(cached_exp, axis=3) + jnp.sum(fresh_exp, axis=3)
    cached_weights = (cached_exp / totals[..., None]).astype(jnp.bfloat16)
    fresh_weights = (fresh_exp / totals[..., None]).astype(jnp.bfloat16)
    attended = jnp.einsum(
        "sghw,swgd->sghd", cached_weights, cached_values, preferred_element_type=jnp.float32
    )
    attended = attended + jnp.einsum(
        "sghn,ngd->sghd", fresh_weights, fresh_values, preferred_element_type=jnp.float32
    )
    return attended.reshape(per_shard, -1).astype(jnp.bfloat16)


def local(
    frames,
    token_session,
    ln_gain,
    w_key,
    w_value,
    k_bias,
    v_bias,
    queries,
    cache_key,
    cache_value,
    cache_start,
    cache_len,
):
    partitions = lax.axis_size(("grp", "seq"))
    shares = lax.axis_size("mp")
    per_shard = queries.shape[0]
    rows = frames.shape[0]
    capacity = max(2, 5 * rows // (2 * partitions) + 1)
    stages = stage_masks(lax.axis_size("grp"), lax.axis_size("seq"))
    if stages is None or shares != 2 or per_shard % 8 or capacity % 16 or partitions * capacity % HEAD:
        return general(
            frames, token_session, ln_gain, w_key, w_value, k_bias, v_bias, queries, cache_key, cache_value,
            cache_start, cache_len,
        )
    swap = [(0, 1), (1, 0)]
    index = lax.axis_index("mp").astype(jnp.int32).reshape(1)
    here = lax.axis_index(("grp", "seq")).astype(jnp.int32).reshape(1)
    own, held = partial_squares(frames)
    other = lax.ppermute(own, "mp", swap)
    held_key, held_value, pick, ids = beside(
        here, token_session[None, :], w_key, w_value, (partitions, per_shard, capacity, stages)
    )
    normed, sent = send_products(
        index, held, own, other, ln_gain[None, :], held_key, held_value, frames.shape[1] * shares
    )
    arrived = lax.ppermute(sent, "mp", swap)
    kept = keep_products(index, normed, held_key, held_value)
    blocks = pack(pick, ids, kept, arrived, k_bias[None, :], v_bias[None, :], len(stages[0]))

    def step(arrays, masks):
        pairs = [[(i, i ^ mask) for i in range(partitions)] for mask in masks]
        sent = [lax.ppermute(a, ("grp", "seq"), p) for a, p in zip(arrays[1:], pairs[1:])]
        return [arrays[0], *sent]

    near, far = stages
    vectors = 2 * cache_key.shape[2] // HEAD
    queries, *blocks = lax.optimization_barrier((queries, *blocks))
    scores, laid = cached_scores(cache_start[None, :], cache_len[None, :], queries, cache_key)
    mid = regroup(step(blocks, near), len(far), vectors, capacity)
    return attend(step(mid, far), laid, scores, cache_value, len(near), capacity)


def solution(mesh):
    return jax.shard_map(
        local,
        mesh=mesh,
        in_specs=(
            P(("grp", "seq"), "mp"),
            P(("grp", "seq")),
            P("mp"),
            P("mp", None),
            P("mp", None),
            P("mp"),
            P("mp"),
            P(("grp", "seq"), "mp"),
            P(("grp", "seq"), None, "mp"),
            P(("grp", "seq"), None, "mp"),
            P(("grp", "seq")),
            P(("grp", "seq")),
        ),
        out_specs=P(("grp", "seq"), "mp"),
        check_vma=False,
    )
```

```python
import functools

import jax
import jax.numpy as jnp
from jax import lax
from jax.experimental import pallas as pl
from jax.experimental.pallas import tpu as pltpu
from jax.sharding import PartitionSpec as P

HEAD = 128
GROUP = 8

epsilon = 1e-06


def params(mib):
    return pltpu.CompilerParams(vmem_limit_bytes=mib << 20)


def cost(flops, nbytes):
    return pl.CostEstimate(flops=flops, bytes_accessed=nbytes, transcendentals=0)


def nt_dot(a, b):
    return lax.dot_general(a, b, (((1,), (1,)), ((), ())), preferred_element_type=jnp.float32)


def dot(a, b):
    return jnp.dot(a, b, preferred_element_type=jnp.float32)


SMEM = pl.BlockSpec(memory_space=pltpu.SMEM)
VMEM = pl.BlockSpec(memory_space=pltpu.VMEM)
HBM = pl.BlockSpec(memory_space=pltpu.HBM)


def in_hbm(array):
    return pltpu.with_memory_space_constraint(array, pltpu.HBM)


def squares_kernel(frames_ref, out_ref, held_ref, arrived):
    chunks, columns = arrived.shape[0], frames_ref.shape[1]
    wide = columns // chunks
    copies = []
    for chunk in range(chunks):
        part = (slice(None), pl.ds(chunk * wide, wide))
        copies.append(
            pltpu.make_async_copy(frames_ref.at[part], held_ref.at[part], arrived.at[chunk])
        )
        copies[-1].start()
    total = None
    for chunk in range(chunks):
        copies[chunk].wait()
        for at in range(chunk * wide, (chunk + 1) * wide, HEAD):
            part = held_ref[:, at : at + HEAD].astype(jnp.float32)
            part = part * part
            total = part if total is None else total + part
    out_ref[...] = total


def partial_squares(frames):
    rows, columns = frames.shape
    chunks = 2 if columns % (2 * HEAD) == 0 else 1
    return pl.pallas_call(
        squares_kernel,
        out_shape=(
            jax.ShapeDtypeStruct((rows, HEAD), jnp.float32),
            jax.ShapeDtypeStruct(frames.shape, frames.dtype),
        ),
        in_specs=[HBM],
        out_specs=(VMEM, VMEM),
        scratch_shapes=[pltpu.SemaphoreType.DMA((chunks,))],
        compiler_params=params(8),
        cost_estimate=cost(2 * rows * columns, 2 * rows * columns),
        name="partial_squares",
    )(in_hbm(frames))


def products(normed_ref, half, key_ref, value_ref, out_ref):
    width = key_ref.shape[1] // 2
    columns = pl.ds(pl.multiple_of(half * width, width), width)
    out_ref[:, :width] = dot(normed_ref[...], key_ref[:, columns])
    out_ref[:, width:] = dot(normed_ref[...], value_ref[:, columns])


def send_kernel(
    features, index_ref, frames_ref, own_ref, other_ref, gain_ref, key_ref, value_ref, normed_ref, out_ref
):
    squares = jnp.sum(own_ref[...] + other_ref[...], axis=1, keepdims=True)
    inverse_rms = lax.rsqrt(squares / features + epsilon)
    normed_ref[...] = (
        frames_ref[...].astype(jnp.float32) * inverse_rms * gain_ref[...]
    ).astype(jnp.bfloat16)
    products(normed_ref, 1 - index_ref[0], key_ref, value_ref, out_ref)


def send_products(index, frames, own, other, gain, key, value, features):
    rows, columns = frames.shape
    width = key.shape[1]
    return pl.pallas_call(
        functools.partial(send_kernel, features),
        out_shape=(
            jax.ShapeDtypeStruct(frames.shape, jnp.bfloat16),
            jax.ShapeDtypeStruct((rows, width), jnp.float32),
        ),
        in_specs=[SMEM] + [VMEM] * 6,
        out_specs=(VMEM, VMEM),
        compiler_params=params(16),
        cost_estimate=cost(2 * rows * columns * width, 2 * key.size),
        name="send_products",
    )(index, frames, own, other, gain, key, value)


def keep_kernel(index_ref, normed_ref, key_ref, value_ref, out_ref):
    products(normed_ref, index_ref[0], key_ref, value_ref, out_ref)


def keep_products(index, normed, key, value):
    rows, columns = normed.shape
    width = key.shape[1]
    return pl.pallas_call(
        keep_kernel,
        out_shape=jax.ShapeDtypeStruct((rows, width), jnp.float32),
        in_specs=[SMEM] + [VMEM] * 3,
        out_specs=VMEM,
        compiler_params=params(16),
        cost_estimate=cost(2 * rows * columns * width, 2 * key.size),
        name="keep_products",
    )(index, normed, key, value)


def first_masks(groups, members):
    if groups & (groups - 1) or members & (members - 1) or members < 4:
        return None
    masks = [group * members + low for group in range(groups) for low in range(2)]
    return (0, masks[-1], *masks[1:-1])


def ring_place(device, members):
    upper = (device & (members - 1)) >> 1
    place = upper
    for shift in range(1, (members // 2).bit_length() - 1):
        place = place ^ (upper >> shift)
    return place


def second_pairs(partitions, members):
    line = members // 2
    devices = range(partitions)
    at = {(d // members, d & 1, ring_place(d, members)): d for d in devices}
    return [
        [(d, at[d // members, d & 1, (ring_place(d, members) + up) % line]) for d in devices]
        for up in range(line)
    ]


def route(per_shard, capacity, near, members, here, session, pick_ref, ids_ref):
    slots, rows = pick_ref.shape
    partitions = slots // capacity
    line = members // 2
    target = lax.div(session, per_shard)
    local = session - target * per_shard
    apart = (target ^ here) & functools.reduce(lambda a, b: a | b, near)
    first = sum(jnp.where(apart == mask, at, 0) for at, mask in enumerate(near))
    second = (ring_place(target, members) - ring_place(here, members)) & (line - 1)
    leaves, lands = first * line + second, second * len(near) + first
    to = lax.broadcasted_iota(jnp.int32, (partitions, rows), 0) == leaves
    to = to.astype(jnp.float32)
    earlier = lax.broadcasted_iota(jnp.int32, (rows, rows), 0) < lax.broadcasted_iota(
        jnp.int32, (rows, rows), 1
    )
    ahead = dot(to.astype(jnp.bfloat16), earlier.astype(jnp.bfloat16))
    order = jnp.sum(to * ahead, axis=0, keepdims=True).astype(jnp.int32)
    place = lax.broadcasted_iota(jnp.int32, (slots, rows), 0)
    pick_ref[...] = (place == leaves * capacity + order).astype(jnp.bfloat16)
    lane = lands * capacity + order
    parts = slots // HEAD
    block = lax.broadcasted_iota(jnp.int32, (partitions * parts, rows), 0)
    named = block == leaves * parts + lane // HEAD
    named = jnp.where(named, (local + 1).astype(jnp.float32), 0.0).astype(jnp.bfloat16)
    spot = lax.broadcasted_iota(jnp.int32, (HEAD, rows), 0) == lane % HEAD
    ids_ref[...] = nt_dot(named, spot.astype(jnp.bfloat16))


def queries_of(queries_ref, head):
    columns = [
        queries_ref[:, at * HEAD : (at + 1) * HEAD].astype(jnp.float32)
        for at in range(head * GROUP, (head + 1) * GROUP)
    ]
    return jnp.concatenate(columns, axis=0).astype(jnp.bfloat16)


def score_cache(start_ref, len_ref, queries_ref, key_ref, out_ref, laid_ref):
    sessions, window, width = key_ref.shape
    heads, rows = width // HEAD, GROUP * sessions

    def by_row(ref):
        mine = lax.broadcasted_iota(jnp.int32, (rows, sessions), 0) % sessions
        mine = mine == lax.broadcasted_iota(jnp.int32, (rows, sessions), 1)
        values = jnp.where(mine, ref[...].astype(jnp.float32), 0.0)
        return jnp.sum(values, axis=1, keepdims=True).astype(jnp.int32)

    since = lax.broadcasted_iota(jnp.int32, (rows, window), 1) - by_row(start_ref)
    since = jnp.where(since < 0, since + window, since)
    live = since < by_row(len_ref)
    row_session = lax.broadcasted_iota(jnp.int32, (rows, window), 0) % sessions
    laid_ref[...] = jnp.zeros_like(laid_ref)
    for head in range(heads):
        query = queries_of(queries_ref, head)
        laid_ref[head * rows : (head + 1) * rows, head * HEAD : (head + 1) * HEAD] = query
        total = jnp.zeros((rows, window), jnp.float32)
        for session in range(sessions):
            key = key_ref[session, :, head * HEAD : (head + 1) * HEAD]
            total = jnp.where(row_session == session, nt_dot(query, key), total)
        total = jnp.where(live, total * (HEAD**-0.5), -jnp.inf)
        out_ref[head * rows : (head + 1) * rows] = total


def beside_kernel(
    per_shard,
    capacity,
    near,
    members,
    here_ref,
    session_ref,
    w_key_ref,
    w_value_ref,
    held_key_ref,
    held_value_ref,
    pick_ref,
    ids_ref,
    session,
    arrived,
):
    copies = []
    for at, (source, held) in enumerate(
        (
            (session_ref, session),
            (w_key_ref, held_key_ref),
            (w_value_ref, held_value_ref),
        )
    ):
        copies.append(pltpu.make_async_copy(source, held, arrived.at[at]))
        copies[-1].start()
    copies[0].wait()
    route(per_shard, capacity, near, members, here_ref[0], session[...], pick_ref, ids_ref)
    for copy in copies[1:]:
        copy.wait()


def beside(here, session, w_key, w_value, sizes):
    partitions, *sizes = sizes
    slots, rows = partitions * sizes[1], session.shape[1]
    return pl.pallas_call(
        functools.partial(beside_kernel, *sizes),
        out_shape=(
            jax.ShapeDtypeStruct(w_key.shape, w_key.dtype),
            jax.ShapeDtypeStruct(w_value.shape, w_value.dtype),
            jax.ShapeDtypeStruct((slots, rows), jnp.bfloat16),
            jax.ShapeDtypeStruct((partitions * slots // HEAD, HEAD), jnp.float32),
        ),
        in_specs=[SMEM] + [HBM] * 3,
        out_specs=(VMEM,) * 4,
        scratch_shapes=[pltpu.VMEM(session.shape, session.dtype), pltpu.SemaphoreType.DMA((3,))],
        compiler_params=params(24),
        cost_estimate=cost(4 * rows * rows * slots, 4 * w_key.size),
        name="beside",
    )(here, in_hbm(session), in_hbm(w_key), in_hbm(w_value))


def cached_scores(start, length, queries, cache_key):
    sessions, window, width = cache_key.shape
    rows = width // HEAD * GROUP * sessions
    return pl.pallas_call(
        score_cache,
        out_shape=(
            jax.ShapeDtypeStruct((rows, window), jnp.float32),
            jax.ShapeDtypeStruct((rows, width), jnp.bfloat16),
        ),
        in_specs=[VMEM] * 4,
        out_specs=(VMEM, VMEM),
        compiler_params=params(8),
        cost_estimate=cost(2 * GROUP * sessions * cache_key.size, 2 * cache_key.size),
        name="cached_scores",
    )(start, length, queries, cache_key)


def pack_kernel(pick_ref, ids_ref, kept_ref, got_ref, key_bias_ref, value_bias_ref, *out_refs):
    width = key_bias_ref.shape[1]
    sums = kept_ref[...] + got_ref[...]
    key = (sums[:, :width] + key_bias_ref[...]).astype(jnp.bfloat16)
    value = (sums[:, width:] + value_bias_ref[...]).astype(jnp.bfloat16)
    tall = pick_ref.shape[0] // len(out_refs)
    at = 0
    for source in (key, value):
        laid = dot(pick_ref[...], source).astype(jnp.bfloat16)
        for column in range(0, width, HEAD):
            for step, out_ref in enumerate(out_refs):
                out_ref[at : at + tall, :] = laid[
                    step * tall : (step + 1) * tall, column : column + HEAD
                ]
            at += tall
    named = ids_ref.shape[0] // len(out_refs)
    for step, out_ref in enumerate(out_refs):
        out_ref[at:, :] = ids_ref[step * named : (step + 1) * named, :].astype(jnp.bfloat16)


def pack(pick, ids, kept, got, key_bias, value_bias, near):
    rows, width = kept.shape
    slots = pick.shape[0]
    tall = (width // HEAD * slots + ids.shape[0]) // near
    return pl.pallas_call(
        pack_kernel,
        out_shape=[jax.ShapeDtypeStruct((tall, HEAD), jnp.bfloat16)] * near,
        in_specs=[VMEM] * 6,
        out_specs=[VMEM] * near,
        compiler_params=params(8),
        cost_estimate=cost(2 * rows * width * slots, 8 * rows * width),
        name="pack",
    )(pick, ids, kept, got, key_bias, value_bias)


def regroup_kernel(near, vectors, capacity, *refs):
    got_refs, out_refs = refs[:near], refs[near:]
    far = len(out_refs)
    for vector in range(vectors):
        for step, out_ref in enumerate(out_refs):
            for first, got_ref in enumerate(got_refs):
                to, at = (vector * near + first) * capacity, (vector * far + step) * capacity
                out_ref[to : to + capacity, :] = got_ref[at : at + capacity, :]
    ids = sum(ref[vectors * far * capacity :, :].astype(jnp.float32) for ref in got_refs)
    for out_ref in out_refs:
        out_ref[vectors * near * capacity :, :] = ids.astype(jnp.bfloat16)


def regroup(blocks, far, vectors, capacity):
    near = len(blocks)
    tall = blocks[0].shape[0] + vectors * capacity * (near - far)
    return pl.pallas_call(
        functools.partial(regroup_kernel, near, vectors, capacity),
        out_shape=[jax.ShapeDtypeStruct((tall, HEAD), jnp.bfloat16)] * far,
        in_specs=[VMEM] * near,
        out_specs=[VMEM] * far,
        compiler_params=params(8),
        cost_estimate=cost(0, 4 * near * blocks[0].size),
        name="regroup",
    )(*blocks)


def attend_kernel(near, capacity, queries_ref, score_ref, cache_ref, *refs):
    *got_refs, out_ref = refs
    rows, window = score_ref.shape
    sessions, _, width = cache_ref.shape
    heads = width // HEAD
    tall = near * capacity
    slots = len(got_refs) * tall
    parts = slots // HEAD
    ids = [
        sum(
            ref[2 * heads * tall :, :].astype(jnp.float32)[step * parts + part : step * parts + part + 1]
            for step, ref in enumerate(got_refs)
        )
        for part in range(parts)
    ]
    ids = jnp.concatenate(ids, axis=1).astype(jnp.int32)
    own = lax.broadcasted_iota(jnp.int32, (rows, slots), 0) % sessions + 1 == ids

    def rows_of(vectors):
        columns = []
        for vector in vectors:
            part = slice(vector * tall, (vector + 1) * tall)
            columns.append(jnp.concatenate([ref[part, :] for ref in got_refs], axis=0))
        return jnp.concatenate(columns, axis=1)

    cached = score_ref[...]
    fresh = nt_dot(queries_ref[...], rows_of(range(heads))) * (HEAD**-0.5)
    fresh = jnp.where(own, fresh, -jnp.inf)
    largest = jnp.maximum(
        jnp.max(cached, axis=1, keepdims=True), jnp.max(fresh, axis=1, keepdims=True)
    )
    cached = jnp.exp(cached - largest)
    fresh = jnp.exp(fresh - largest)
    total = jnp.sum(cached, axis=1, keepdims=True) + jnp.sum(fresh, axis=1, keepdims=True)
    cached = cached / total
    attended = dot((fresh / total).astype(jnp.bfloat16), rows_of(range(heads, 2 * heads)))
    row_session = lax.broadcasted_iota(jnp.int32, (rows, window), 0) % sessions
    for session in range(0, sessions, 2):
        weights = jnp.concatenate(
            [jnp.where(row_session == session + more, cached, 0.0) for more in range(2)], axis=1
        )
        values = cache_ref[session : session + 2].reshape(2 * window, width)
        attended += dot(weights.astype(jnp.bfloat16), values)
    for head in range(heads):
        for q in range(GROUP):
            row, column = (head * GROUP + q) * sessions, (head * GROUP + q) * HEAD
            out_ref[:, column : column + HEAD] = attended[
                row : row + sessions, head * HEAD : (head + 1) * HEAD
            ].astype(jnp.bfloat16)


def attend(got, queries, scores, cache_value, near, capacity):
    return pl.pallas_call(
        functools.partial(attend_kernel, near, capacity),
        out_shape=jax.ShapeDtypeStruct(
            (cache_value.shape[0], queries.shape[1] * GROUP), jnp.bfloat16
        ),
        in_specs=[VMEM] * (3 + len(got)),
        out_specs=VMEM,
        compiler_params=params(8),
        cost_estimate=cost(4 * queries.shape[0] * cache_value.size, 2 * cache_value.size),
        name="attend",
    )(queries, scores, cache_value, *got)


def project(frame_rows, ln_gain, w_key, w_value, k_bias, v_bias):
    values32 = frame_rows.astype(jnp.float32)
    partial_squares = jnp.sum(values32 * values32, axis=1)
    squares = lax.psum(partial_squares, "mp")
    inverse_rms = lax.rsqrt(squares / (frame_rows.shape[1] * lax.axis_size("mp")) + epsilon)
    normed = (values32 * inverse_rms[:, None] * ln_gain[None, :]).astype(jnp.bfloat16)
    part_key = jnp.dot(normed, w_key, preferred_element_type=jnp.float32)
    part_value = jnp.dot(normed, w_value, preferred_element_type=jnp.float32)
    key_sums, value_sums = (
        lax.psum_scatter(part_key, "mp", scatter_dimension=1, tiled=True),
        lax.psum_scatter(part_value, "mp", scatter_dimension=1, tiled=True),
    )
    new_keys = (key_sums + k_bias[None, :]).astype(jnp.bfloat16)
    new_values = (value_sums + v_bias[None, :]).astype(jnp.bfloat16)
    return (new_keys, new_values)


def slot_sources(token_session, per_shard, partition_count, capacity):
    row_count = token_session.shape[0]
    target = token_session // per_shard
    one_hot = (target[:, None] == jnp.arange(partition_count, dtype=jnp.int32)[None, :]).astype(
        jnp.int32
    )
    order_in = jnp.sum((jnp.cumsum(one_hot, axis=0) - one_hot) * one_hot, axis=1)
    slot_index = target * capacity + order_in
    matches = (
        slot_index[None, :] == jnp.arange(partition_count * capacity, dtype=jnp.int32)[:, None]
    )
    source = jnp.sum(jnp.where(matches, jnp.arange(row_count, dtype=jnp.int32)[None, :], 0), axis=1)
    filled = jnp.any(matches, axis=1)
    sessions = jnp.where(filled, jnp.mod(token_session[source], per_shard), -1)
    return (source, filled, sessions)


def general(
    frames,
    token_session,
    ln_gain,
    w_key,
    w_value,
    k_bias,
    v_bias,
    queries,
    cache_key,
    cache_value,
    cache_start,
    cache_len,
):
    partition_count = lax.axis_size(("grp", "seq"))
    per_shard = queries.shape[0]
    rows_here = frames.shape[0]
    capacity = max(2, 5 * rows_here // (2 * partition_count) + 1)
    source, filled, sessions = slot_sources(token_session, per_shard, partition_count, capacity)
    session_slots = sessions.reshape(partition_count, capacity)
    nothing = jnp.zeros((), jnp.bfloat16)
    own_keys, own_values = project(frames, ln_gain, w_key, w_value, k_bias, v_bias)
    send_keys = jnp.where(filled[:, None], own_keys[source], nothing).reshape(
        partition_count, capacity, -1
    )
    send_values = jnp.where(filled[:, None], own_values[source], nothing).reshape(
        partition_count, capacity, -1
    )
    got_keys, got_values, got_sessions = (
        lax.all_to_all(send_keys, ("grp", "seq"), split_axis=0, concat_axis=0, tiled=True),
        lax.all_to_all(send_values, ("grp", "seq"), split_axis=0, concat_axis=0, tiled=True),
        lax.all_to_all(session_slots, ("grp", "seq"), split_axis=0, concat_axis=0, tiled=True),
    )
    new_keys = got_keys.reshape(partition_count * capacity, -1)
    new_values = got_values.reshape(partition_count * capacity, -1)
    new_sessions = got_sessions.reshape(-1)
    heads_kv = new_keys.shape[1] // HEAD
    window = cache_key.shape[1]
    score_scale = HEAD ** (-0.5)
    query_heads = queries.reshape(per_shard, heads_kv, GROUP, HEAD)
    cached_keys = cache_key.reshape(per_shard, window, heads_kv, HEAD)
    cached_values = cache_value.reshape(per_shard, window, heads_kv, HEAD)
    fresh_keys = new_keys.reshape(-1, heads_kv, HEAD)
    fresh_values = new_values.reshape(-1, heads_kv, HEAD)
    cached_scores = (
        jnp.einsum("sghd,swgd->sghw", query_heads, cached_keys, preferred_element_type=jnp.float32)
        * score_scale
    )
    positions = jnp.arange(window, dtype=jnp.int32)
    live_slots = jnp.mod(positions[None, :] - cache_start[:, None], window) < cache_len[:, None]
    cached_scores = jnp.where(live_slots[:, None, None, :], cached_scores, -jnp.inf)
    fresh_scores = (
        jnp.einsum("sghd,ngd->sghn", query_heads, fresh_keys, preferred_element_type=jnp.float32)
        * score_scale
    )
    own_rows = new_sessions[None, :] == jnp.arange(per_shard, dtype=jnp.int32)[:, None]
    fresh_scores = jnp.where(own_rows[:, None, None, :], fresh_scores, -jnp.inf)
    largest = jnp.maximum(jnp.max(cached_scores, axis=3), jnp.max(fresh_scores, axis=3))
    cached_exp = jnp.exp(cached_scores - largest[..., None])
    fresh_exp = jnp.exp(fresh_scores - largest[..., None])
    totals = jnp.sum(cached_exp, axis=3) + jnp.sum(fresh_exp, axis=3)
    cached_weights = (cached_exp / totals[..., None]).astype(jnp.bfloat16)
    fresh_weights = (fresh_exp / totals[..., None]).astype(jnp.bfloat16)
    attended = jnp.einsum(
        "sghw,swgd->sghd", cached_weights, cached_values, preferred_element_type=jnp.float32
    )
    attended = attended + jnp.einsum(
        "sghn,ngd->sghd", fresh_weights, fresh_values, preferred_element_type=jnp.float32
    )
    return attended.reshape(per_shard, -1).astype(jnp.bfloat16)


def local(
    frames,
    token_session,
    ln_gain,
    w_key,
    w_value,
    k_bias,
    v_bias,
    queries,
    cache_key,
    cache_value,
    cache_start,
    cache_len,
):
    partitions = lax.axis_size(("grp", "seq"))
    shares = lax.axis_size("mp")
    per_shard = queries.shape[0]
    rows = frames.shape[0]
    capacity = max(2, 5 * rows // (2 * partitions) + 1)
    members = lax.axis_size("seq")
    near = first_masks(lax.axis_size("grp"), members)
    if near is None or shares != 2 or per_shard % 8 or capacity % 16 or partitions * capacity % HEAD:
        return general(
            frames, token_session, ln_gain, w_key, w_value, k_bias, v_bias, queries, cache_key, cache_value,
            cache_start, cache_len,
        )
    swap = [(0, 1), (1, 0)]
    index = lax.axis_index("mp").astype(jnp.int32).reshape(1)
    here = lax.axis_index(("grp", "seq")).astype(jnp.int32).reshape(1)
    own, held = partial_squares(frames)
    other = lax.ppermute(own, "mp", swap)
    held_key, held_value, pick, ids = beside(
        here, token_session[None, :], w_key, w_value, (partitions, per_shard, capacity, near, members)
    )
    normed, sent = send_products(
        index, held, own, other, ln_gain[None, :], held_key, held_value, frames.shape[1] * shares
    )
    arrived = lax.ppermute(sent, "mp", swap)
    kept = keep_products(index, normed, held_key, held_value)
    blocks = pack(pick, ids, kept, arrived, k_bias[None, :], v_bias[None, :], len(near))

    def step(arrays, pairs):
        sent = [lax.ppermute(a, ("grp", "seq"), p) for a, p in zip(arrays[1:], pairs[1:])]
        return [arrays[0], *sent]

    queries, *blocks = lax.optimization_barrier((queries, *blocks))
    scores, laid = cached_scores(cache_start[None, :], cache_len[None, :], queries, cache_key)
    vectors = 2 * cache_key.shape[2] // HEAD
    blocks = step(blocks, [[(i, i ^ mask) for i in range(partitions)] for mask in near])
    blocks = regroup(blocks, members // 2, vectors, capacity)
    blocks = step(blocks, second_pairs(partitions, members))
    return attend(blocks, laid, scores, cache_value, len(near), capacity)


def solution(mesh):
    return jax.shard_map(
        local,
        mesh=mesh,
        in_specs=(
            P(("grp", "seq"), "mp"),
            P(("grp", "seq")),
            P("mp"),
            P("mp", None),
            P("mp", None),
            P("mp"),
            P("mp"),
            P(("grp", "seq"), "mp"),
            P(("grp", "seq"), None, "mp"),
            P(("grp", "seq"), None, "mp"),
            P(("grp", "seq")),
            P(("grp", "seq")),
        ),
        out_specs=P(("grp", "seq"), "mp"),
        check_vma=False,
    )
```

```python
import functools

import jax
import jax.numpy as jnp
from jax import lax
from jax.experimental import pallas as pl
from jax.experimental.pallas import tpu as pltpu
from jax.sharding import PartitionSpec as P

HEAD = 128
GROUP = 8

epsilon = 1e-06


def params(mib):
    return pltpu.CompilerParams(vmem_limit_bytes=mib << 20)


def cost(flops, nbytes):
    return pl.CostEstimate(flops=flops, bytes_accessed=nbytes, transcendentals=0)


def nt_dot(a, b):
    return lax.dot_general(a, b, (((1,), (1,)), ((), ())), preferred_element_type=jnp.float32)


def dot(a, b):
    return jnp.dot(a, b, preferred_element_type=jnp.float32)


SMEM = pl.BlockSpec(memory_space=pltpu.SMEM)
VMEM = pl.BlockSpec(memory_space=pltpu.VMEM)
HBM = pl.BlockSpec(memory_space=pltpu.HBM)


def in_hbm(array):
    return pltpu.with_memory_space_constraint(array, pltpu.HBM)


def squares_kernel(frames_ref, out_ref, held_ref, arrived):
    chunks, columns = arrived.shape[0], frames_ref.shape[1]
    wide = columns // chunks
    copies = []
    for chunk in range(chunks):
        part = (slice(None), pl.ds(chunk * wide, wide))
        copies.append(
            pltpu.make_async_copy(frames_ref.at[part], held_ref.at[part], arrived.at[chunk])
        )
        copies[-1].start()
    total = None
    for chunk in range(chunks):
        copies[chunk].wait()
        for at in range(chunk * wide, (chunk + 1) * wide, HEAD):
            part = held_ref[:, at : at + HEAD].astype(jnp.float32)
            part = part * part
            total = part if total is None else total + part
    out_ref[...] = total


def partial_squares(frames):
    rows, columns = frames.shape
    chunks = 2 if columns % (2 * HEAD) == 0 else 1
    return pl.pallas_call(
        squares_kernel,
        out_shape=(
            jax.ShapeDtypeStruct((rows, HEAD), jnp.float32),
            jax.ShapeDtypeStruct(frames.shape, frames.dtype),
        ),
        in_specs=[HBM],
        out_specs=(VMEM, VMEM),
        scratch_shapes=[pltpu.SemaphoreType.DMA((chunks,))],
        compiler_params=params(8),
        cost_estimate=cost(2 * rows * columns, 2 * rows * columns),
        name="partial_squares",
    )(in_hbm(frames))


def products(normed_ref, half, key_ref, value_ref, out_ref):
    width = key_ref.shape[1] // 2
    columns = pl.ds(pl.multiple_of(half * width, width), width)
    out_ref[:, :width] = dot(normed_ref[...], key_ref[:, columns])
    out_ref[:, width:] = dot(normed_ref[...], value_ref[:, columns])


def send_kernel(
    features, index_ref, frames_ref, own_ref, other_ref, gain_ref, key_ref, value_ref, normed_ref, out_ref
):
    squares = jnp.sum(own_ref[...] + other_ref[...], axis=1, keepdims=True)
    inverse_rms = lax.rsqrt(squares / features + epsilon)
    normed_ref[...] = (
        frames_ref[...].astype(jnp.float32) * inverse_rms * gain_ref[...]
    ).astype(jnp.bfloat16)
    products(normed_ref, 1 - index_ref[0], key_ref, value_ref, out_ref)


def send_products(index, frames, own, other, gain, key, value, features):
    rows, columns = frames.shape
    width = key.shape[1]
    return pl.pallas_call(
        functools.partial(send_kernel, features),
        out_shape=(
            jax.ShapeDtypeStruct(frames.shape, jnp.bfloat16),
            jax.ShapeDtypeStruct((rows, width), jnp.float32),
        ),
        in_specs=[SMEM] + [VMEM] * 6,
        out_specs=(VMEM, VMEM),
        compiler_params=params(16),
        cost_estimate=cost(2 * rows * columns * width, 2 * key.size),
        name="send_products",
    )(index, frames, own, other, gain, key, value)


def keep_kernel(index_ref, normed_ref, key_ref, value_ref, out_ref):
    products(normed_ref, index_ref[0], key_ref, value_ref, out_ref)


def keep_products(index, normed, key, value):
    rows, columns = normed.shape
    width = key.shape[1]
    return pl.pallas_call(
        keep_kernel,
        out_shape=jax.ShapeDtypeStruct((rows, width), jnp.float32),
        in_specs=[SMEM] + [VMEM] * 3,
        out_specs=VMEM,
        compiler_params=params(16),
        cost_estimate=cost(2 * rows * columns * width, 2 * key.size),
        name="keep_products",
    )(index, normed, key, value)


def first_masks(groups, members):
    if groups & (groups - 1) or members & (members - 1) or members < 4:
        return None
    masks = [group * members + low for group in range(groups) for low in range(2)]
    return (0, masks[-1], *masks[1:-1])


def ring_place(device, members):
    upper = (device & (members - 1)) >> 1
    place = upper
    for shift in range(1, (members // 2).bit_length() - 1):
        place = place ^ (upper >> shift)
    return place


def second_pairs(partitions, members):
    line = members // 2
    devices = range(partitions)
    at = {(d // members, d & 1, ring_place(d, members)): d for d in devices}
    return [
        [(d, at[d // members, d & 1, (ring_place(d, members) + up) % line]) for d in devices]
        for up in range(line)
    ]


def route(per_shard, capacity, near, members, here, session, pick_ref, ids_ref):
    slots, rows = pick_ref.shape
    partitions = slots // capacity
    line = members // 2
    target = lax.div(session, per_shard)
    local = session - target * per_shard
    apart = (target ^ here) & functools.reduce(lambda a, b: a | b, near)
    first = sum(jnp.where(apart == mask, at, 0) for at, mask in enumerate(near))
    second = (ring_place(target, members) - ring_place(here, members)) & (line - 1)
    leaves, lands = first * line + second, second * len(near) + first
    to = lax.broadcasted_iota(jnp.int32, (partitions, rows), 0) == leaves
    to = to.astype(jnp.float32)
    earlier = lax.broadcasted_iota(jnp.int32, (rows, rows), 0) < lax.broadcasted_iota(
        jnp.int32, (rows, rows), 1
    )
    ahead = dot(to.astype(jnp.bfloat16), earlier.astype(jnp.bfloat16))
    order = jnp.sum(to * ahead, axis=0, keepdims=True).astype(jnp.int32)
    place = lax.broadcasted_iota(jnp.int32, (slots, rows), 0)
    pick_ref[...] = (place == leaves * capacity + order).astype(jnp.bfloat16)
    lane = lands * capacity + order
    parts = slots // HEAD
    block = lax.broadcasted_iota(jnp.int32, (ids_ref.shape[0], rows), 0)
    named = block == first * (ids_ref.shape[0] // len(near)) + second * parts + lane // HEAD
    named = jnp.where(named, (local + 1).astype(jnp.float32), 0.0).astype(jnp.bfloat16)
    spot = lax.broadcasted_iota(jnp.int32, (HEAD, rows), 0) == lane % HEAD
    ids_ref[...] = nt_dot(named, spot.astype(jnp.bfloat16))


def queries_of(queries_ref, head):
    columns = [
        queries_ref[:, at * HEAD : (at + 1) * HEAD].astype(jnp.float32)
        for at in range(head * GROUP, (head + 1) * GROUP)
    ]
    return jnp.concatenate(columns, axis=0).astype(jnp.bfloat16)


def score_cache(start_ref, len_ref, queries_ref, key_ref, out_ref, laid_ref):
    sessions, window, width = key_ref.shape
    heads, rows = width // HEAD, GROUP * sessions

    def by_row(ref):
        mine = lax.broadcasted_iota(jnp.int32, (rows, sessions), 0) % sessions
        mine = mine == lax.broadcasted_iota(jnp.int32, (rows, sessions), 1)
        values = jnp.where(mine, ref[...].astype(jnp.float32), 0.0)
        return jnp.sum(values, axis=1, keepdims=True).astype(jnp.int32)

    since = lax.broadcasted_iota(jnp.int32, (rows, window), 1) - by_row(start_ref)
    since = jnp.where(since < 0, since + window, since)
    live = since < by_row(len_ref)
    row_session = lax.broadcasted_iota(jnp.int32, (rows, window), 0) % sessions
    laid_ref[...] = jnp.zeros_like(laid_ref)
    for head in range(heads):
        query = queries_of(queries_ref, head)
        laid_ref[head * rows : (head + 1) * rows, head * HEAD : (head + 1) * HEAD] = query
        total = jnp.zeros((rows, window), jnp.float32)
        for session in range(sessions):
            key = key_ref[session, :, head * HEAD : (head + 1) * HEAD]
            total = jnp.where(row_session == session, nt_dot(query, key), total)
        total = jnp.where(live, total * (HEAD**-0.5), -jnp.inf)
        out_ref[head * rows : (head + 1) * rows] = total


def beside_kernel(
    per_shard,
    capacity,
    near,
    members,
    here_ref,
    session_ref,
    w_key_ref,
    w_value_ref,
    held_key_ref,
    held_value_ref,
    pick_ref,
    ids_ref,
    session,
    arrived,
):
    copies = []
    for at, (source, held) in enumerate(
        (
            (session_ref, session),
            (w_key_ref, held_key_ref),
            (w_value_ref, held_value_ref),
        )
    ):
        copies.append(pltpu.make_async_copy(source, held, arrived.at[at]))
        copies[-1].start()
    copies[0].wait()
    route(per_shard, capacity, near, members, here_ref[0], session[...], pick_ref, ids_ref)
    for copy in copies[1:]:
        copy.wait()


def beside(here, session, w_key, w_value, sizes):
    partitions, _, capacity, near, _ = sizes
    slots, rows = partitions * capacity, session.shape[1]
    id_rows = -(-partitions // len(near) * slots // (16 * HEAD)) * 16 * len(near)
    return pl.pallas_call(
        functools.partial(beside_kernel, *sizes[1:]),
        out_shape=(
            jax.ShapeDtypeStruct(w_key.shape, w_key.dtype),
            jax.ShapeDtypeStruct(w_value.shape, w_value.dtype),
            jax.ShapeDtypeStruct((slots, rows), jnp.bfloat16),
            jax.ShapeDtypeStruct((id_rows, HEAD), jnp.float32),
        ),
        in_specs=[SMEM] + [HBM] * 3,
        out_specs=(VMEM,) * 4,
        scratch_shapes=[pltpu.VMEM(session.shape, session.dtype), pltpu.SemaphoreType.DMA((3,))],
        compiler_params=params(24),
        cost_estimate=cost(4 * rows * rows * slots, 4 * w_key.size),
        name="beside",
    )(here, in_hbm(session), in_hbm(w_key), in_hbm(w_value))


def cached_scores(start, length, queries, cache_key):
    sessions, window, width = cache_key.shape
    rows = width // HEAD * GROUP * sessions
    return pl.pallas_call(
        score_cache,
        out_shape=(
            jax.ShapeDtypeStruct((rows, window), jnp.float32),
            jax.ShapeDtypeStruct((rows, width), jnp.bfloat16),
        ),
        in_specs=[VMEM] * 4,
        out_specs=(VMEM, VMEM),
        compiler_params=params(8),
        cost_estimate=cost(2 * GROUP * sessions * cache_key.size, 2 * cache_key.size),
        name="cached_scores",
    )(start, length, queries, cache_key)


def pack_kernel(pick_ref, ids_ref, kept_ref, got_ref, key_bias_ref, value_bias_ref, *out_refs):
    width = key_bias_ref.shape[1]
    sums = kept_ref[...] + got_ref[...]
    key = (sums[:, :width] + key_bias_ref[...]).astype(jnp.bfloat16)
    value = (sums[:, width:] + value_bias_ref[...]).astype(jnp.bfloat16)
    tall = pick_ref.shape[0] // len(out_refs)
    at = 0
    for source in (key, value):
        laid = dot(pick_ref[...], source).astype(jnp.bfloat16)
        for column in range(0, width, HEAD):
            for step, out_ref in enumerate(out_refs):
                out_ref[at : at + tall, :] = laid[
                    step * tall : (step + 1) * tall, column : column + HEAD
                ]
            at += tall
    named = ids_ref.shape[0] // len(out_refs)
    for step, out_ref in enumerate(out_refs):
        out_ref[at:, :] = ids_ref[step * named : (step + 1) * named, :].astype(jnp.bfloat16)


def pack(pick, ids, kept, got, key_bias, value_bias, near):
    rows, width = kept.shape
    slots = pick.shape[0]
    tall = (width // HEAD * slots + ids.shape[0]) // near
    return pl.pallas_call(
        pack_kernel,
        out_shape=[jax.ShapeDtypeStruct((tall, HEAD), jnp.bfloat16)] * near,
        in_specs=[VMEM] * 6,
        out_specs=[VMEM] * near,
        compiler_params=params(8),
        cost_estimate=cost(2 * rows * width * slots, 8 * rows * width),
        name="pack",
    )(pick, ids, kept, got, key_bias, value_bias)


def regroup_kernel(near, vectors, capacity, *refs):
    got_refs, out_refs = refs[:near], refs[near:]
    far = len(out_refs)
    for vector in range(vectors):
        for step, out_ref in enumerate(out_refs):
            for first, got_ref in enumerate(got_refs):
                to, at = (vector * near + first) * capacity, (vector * far + step) * capacity
                out_ref[to : to + capacity, :] = got_ref[at : at + capacity, :]
    ids = sum(ref[vectors * far * capacity :, :].astype(jnp.float32) for ref in got_refs)
    for out_ref in out_refs:
        out_ref[vectors * near * capacity :, :] = ids.astype(jnp.bfloat16)


def regroup(blocks, far, vectors, capacity):
    near = len(blocks)
    tall = blocks[0].shape[0] + vectors * capacity * (near - far)
    return pl.pallas_call(
        functools.partial(regroup_kernel, near, vectors, capacity),
        out_shape=[jax.ShapeDtypeStruct((tall, HEAD), jnp.bfloat16)] * far,
        in_specs=[VMEM] * near,
        out_specs=[VMEM] * far,
        compiler_params=params(8),
        cost_estimate=cost(0, 4 * near * blocks[0].size),
        name="regroup",
    )(*blocks)


def attend_kernel(near, capacity, queries_ref, score_ref, cache_ref, *refs):
    *got_refs, out_ref = refs
    rows, window = score_ref.shape
    sessions, _, width = cache_ref.shape
    heads = width // HEAD
    tall = near * capacity
    slots = len(got_refs) * tall
    parts = slots // HEAD
    ids = [
        sum(
            ref[2 * heads * tall :, :].astype(jnp.float32)[step * parts + part : step * parts + part + 1]
            for step, ref in enumerate(got_refs)
        )
        for part in range(parts)
    ]
    ids = jnp.concatenate(ids, axis=1).astype(jnp.int32)
    own = lax.broadcasted_iota(jnp.int32, (rows, slots), 0) % sessions + 1 == ids

    def rows_of(vectors):
        columns = []
        for vector in vectors:
            part = slice(vector * tall, (vector + 1) * tall)
            columns.append(jnp.concatenate([ref[part, :] for ref in got_refs], axis=0))
        return jnp.concatenate(columns, axis=1)

    cached = score_ref[...]
    fresh = nt_dot(queries_ref[...], rows_of(range(heads))) * (HEAD**-0.5)
    fresh = jnp.where(own, fresh, -jnp.inf)
    largest = jnp.maximum(
        jnp.max(cached, axis=1, keepdims=True), jnp.max(fresh, axis=1, keepdims=True)
    )
    cached = jnp.exp(cached - largest)
    fresh = jnp.exp(fresh - largest)
    total = jnp.sum(cached, axis=1, keepdims=True) + jnp.sum(fresh, axis=1, keepdims=True)
    cached = cached / total
    attended = dot((fresh / total).astype(jnp.bfloat16), rows_of(range(heads, 2 * heads)))
    row_session = lax.broadcasted_iota(jnp.int32, (rows, window), 0) % sessions
    for session in range(0, sessions, 2):
        weights = jnp.concatenate(
            [jnp.where(row_session == session + more, cached, 0.0) for more in range(2)], axis=1
        )
        values = cache_ref[session : session + 2].reshape(2 * window, width)
        attended += dot(weights.astype(jnp.bfloat16), values)
    for head in range(heads):
        for q in range(GROUP):
            row, column = (head * GROUP + q) * sessions, (head * GROUP + q) * HEAD
            out_ref[:, column : column + HEAD] = attended[
                row : row + sessions, head * HEAD : (head + 1) * HEAD
            ].astype(jnp.bfloat16)


def attend(got, queries, scores, cache_value, near, capacity):
    return pl.pallas_call(
        functools.partial(attend_kernel, near, capacity),
        out_shape=jax.ShapeDtypeStruct(
            (cache_value.shape[0], queries.shape[1] * GROUP), jnp.bfloat16
        ),
        in_specs=[VMEM] * (3 + len(got)),
        out_specs=VMEM,
        compiler_params=params(8),
        cost_estimate=cost(4 * queries.shape[0] * cache_value.size, 2 * cache_value.size),
        name="attend",
    )(queries, scores, cache_value, *got)


def project(frame_rows, ln_gain, w_key, w_value, k_bias, v_bias):
    values32 = frame_rows.astype(jnp.float32)
    partial_squares = jnp.sum(values32 * values32, axis=1)
    squares = lax.psum(partial_squares, "mp")
    inverse_rms = lax.rsqrt(squares / (frame_rows.shape[1] * lax.axis_size("mp")) + epsilon)
    normed = (values32 * inverse_rms[:, None] * ln_gain[None, :]).astype(jnp.bfloat16)
    part_key = jnp.dot(normed, w_key, preferred_element_type=jnp.float32)
    part_value = jnp.dot(normed, w_value, preferred_element_type=jnp.float32)
    key_sums, value_sums = (
        lax.psum_scatter(part_key, "mp", scatter_dimension=1, tiled=True),
        lax.psum_scatter(part_value, "mp", scatter_dimension=1, tiled=True),
    )
    new_keys = (key_sums + k_bias[None, :]).astype(jnp.bfloat16)
    new_values = (value_sums + v_bias[None, :]).astype(jnp.bfloat16)
    return (new_keys, new_values)


def slot_sources(token_session, per_shard, partition_count, capacity):
    row_count = token_session.shape[0]
    target = token_session // per_shard
    one_hot = (target[:, None] == jnp.arange(partition_count, dtype=jnp.int32)[None, :]).astype(
        jnp.int32
    )
    order_in = jnp.sum((jnp.cumsum(one_hot, axis=0) - one_hot) * one_hot, axis=1)
    slot_index = target * capacity + order_in
    matches = (
        slot_index[None, :] == jnp.arange(partition_count * capacity, dtype=jnp.int32)[:, None]
    )
    source = jnp.sum(jnp.where(matches, jnp.arange(row_count, dtype=jnp.int32)[None, :], 0), axis=1)
    filled = jnp.any(matches, axis=1)
    sessions = jnp.where(filled, jnp.mod(token_session[source], per_shard), -1)
    return (source, filled, sessions)


def general(
    frames,
    token_session,
    ln_gain,
    w_key,
    w_value,
    k_bias,
    v_bias,
    queries,
    cache_key,
    cache_value,
    cache_start,
    cache_len,
):
    partition_count = lax.axis_size(("grp", "seq"))
    per_shard = queries.shape[0]
    rows_here = frames.shape[0]
    capacity = max(2, 5 * rows_here // (2 * partition_count) + 1)
    source, filled, sessions = slot_sources(token_session, per_shard, partition_count, capacity)
    session_slots = sessions.reshape(partition_count, capacity)
    nothing = jnp.zeros((), jnp.bfloat16)
    own_keys, own_values = project(frames, ln_gain, w_key, w_value, k_bias, v_bias)
    send_keys = jnp.where(filled[:, None], own_keys[source], nothing).reshape(
        partition_count, capacity, -1
    )
    send_values = jnp.where(filled[:, None], own_values[source], nothing).reshape(
        partition_count, capacity, -1
    )
    got_keys, got_values, got_sessions = (
        lax.all_to_all(send_keys, ("grp", "seq"), split_axis=0, concat_axis=0, tiled=True),
        lax.all_to_all(send_values, ("grp", "seq"), split_axis=0, concat_axis=0, tiled=True),
        lax.all_to_all(session_slots, ("grp", "seq"), split_axis=0, concat_axis=0, tiled=True),
    )
    new_keys = got_keys.reshape(partition_count * capacity, -1)
    new_values = got_values.reshape(partition_count * capacity, -1)
    new_sessions = got_sessions.reshape(-1)
    heads_kv = new_keys.shape[1] // HEAD
    window = cache_key.shape[1]
    score_scale = HEAD ** (-0.5)
    query_heads = queries.reshape(per_shard, heads_kv, GROUP, HEAD)
    cached_keys = cache_key.reshape(per_shard, window, heads_kv, HEAD)
    cached_values = cache_value.reshape(per_shard, window, heads_kv, HEAD)
    fresh_keys = new_keys.reshape(-1, heads_kv, HEAD)
    fresh_values = new_values.reshape(-1, heads_kv, HEAD)
    cached_scores = (
        jnp.einsum("sghd,swgd->sghw", query_heads, cached_keys, preferred_element_type=jnp.float32)
        * score_scale
    )
    positions = jnp.arange(window, dtype=jnp.int32)
    live_slots = jnp.mod(positions[None, :] - cache_start[:, None], window) < cache_len[:, None]
    cached_scores = jnp.where(live_slots[:, None, None, :], cached_scores, -jnp.inf)
    fresh_scores = (
        jnp.einsum("sghd,ngd->sghn", query_heads, fresh_keys, preferred_element_type=jnp.float32)
        * score_scale
    )
    own_rows = new_sessions[None, :] == jnp.arange(per_shard, dtype=jnp.int32)[:, None]
    fresh_scores = jnp.where(own_rows[:, None, None, :], fresh_scores, -jnp.inf)
    largest = jnp.maximum(jnp.max(cached_scores, axis=3), jnp.max(fresh_scores, axis=3))
    cached_exp = jnp.exp(cached_scores - largest[..., None])
    fresh_exp = jnp.exp(fresh_scores - largest[..., None])
    totals = jnp.sum(cached_exp, axis=3) + jnp.sum(fresh_exp, axis=3)
    cached_weights = (cached_exp / totals[..., None]).astype(jnp.bfloat16)
    fresh_weights = (fresh_exp / totals[..., None]).astype(jnp.bfloat16)
    attended = jnp.einsum(
        "sghw,swgd->sghd", cached_weights, cached_values, preferred_element_type=jnp.float32
    )
    attended = attended + jnp.einsum(
        "sghn,ngd->sghd", fresh_weights, fresh_values, preferred_element_type=jnp.float32
    )
    return attended.reshape(per_shard, -1).astype(jnp.bfloat16)


def local(
    frames,
    token_session,
    ln_gain,
    w_key,
    w_value,
    k_bias,
    v_bias,
    queries,
    cache_key,
    cache_value,
    cache_start,
    cache_len,
):
    partitions = lax.axis_size(("grp", "seq"))
    shares = lax.axis_size("mp")
    per_shard = queries.shape[0]
    rows = frames.shape[0]
    capacity = max(2, 5 * rows // (2 * partitions) + 1)
    members = lax.axis_size("seq")
    near = first_masks(lax.axis_size("grp"), members)
    if near is None or shares != 2 or per_shard % 8 or capacity % 16 or partitions * capacity % HEAD:
        return general(
            frames, token_session, ln_gain, w_key, w_value, k_bias, v_bias, queries, cache_key, cache_value,
            cache_start, cache_len,
        )
    swap = [(0, 1), (1, 0)]
    index = lax.axis_index("mp").astype(jnp.int32).reshape(1)
    here = lax.axis_index(("grp", "seq")).astype(jnp.int32).reshape(1)
    own, held = partial_squares(frames)
    other = lax.ppermute(own, "mp", swap)
    held_key, held_value, pick, ids = beside(
        here, token_session[None, :], w_key, w_value, (partitions, per_shard, capacity, near, members)
    )
    normed, sent = send_products(
        index, held, own, other, ln_gain[None, :], held_key, held_value, frames.shape[1] * shares
    )
    arrived = lax.ppermute(sent, "mp", swap)
    kept = keep_products(index, normed, held_key, held_value)
    blocks = pack(pick, ids, kept, arrived, k_bias[None, :], v_bias[None, :], len(near))

    def step(arrays, pairs):
        sent = [lax.ppermute(a, ("grp", "seq"), p) for a, p in zip(arrays[1:], pairs[1:])]
        return [arrays[0], *sent]

    queries, *blocks = lax.optimization_barrier((queries, *blocks))
    scores, laid = cached_scores(cache_start[None, :], cache_len[None, :], queries, cache_key)
    vectors = 2 * cache_key.shape[2] // HEAD
    blocks = step(blocks, [[(i, i ^ mask) for i in range(partitions)] for mask in near])
    blocks = regroup(blocks, members // 2, vectors, capacity)
    blocks = step(blocks, second_pairs(partitions, members))
    return attend(blocks, laid, scores, cache_value, len(near), capacity)


def solution(mesh):
    return jax.shard_map(
        local,
        mesh=mesh,
        in_specs=(
            P(("grp", "seq"), "mp"),
            P(("grp", "seq")),
            P("mp"),
            P("mp", None),
            P("mp", None),
            P("mp"),
            P("mp"),
            P(("grp", "seq"), "mp"),
            P(("grp", "seq"), None, "mp"),
            P(("grp", "seq"), None, "mp"),
            P(("grp", "seq")),
            P(("grp", "seq")),
        ),
        out_specs=P(("grp", "seq"), "mp"),
        check_vma=False,
    )
```

```python
import functools

import jax
import jax.numpy as jnp
from jax import lax
from jax.experimental import pallas as pl
from jax.experimental.pallas import tpu as pltpu
from jax.sharding import PartitionSpec as P

HEAD = 128
GROUP = 8

epsilon = 1e-06


def params(mib):
    return pltpu.CompilerParams(vmem_limit_bytes=mib << 20)


def cost(flops, nbytes):
    return pl.CostEstimate(flops=flops, bytes_accessed=nbytes, transcendentals=0)


def nt_dot(a, b):
    return lax.dot_general(a, b, (((1,), (1,)), ((), ())), preferred_element_type=jnp.float32)


def dot(a, b):
    return jnp.dot(a, b, preferred_element_type=jnp.float32)


SMEM = pl.BlockSpec(memory_space=pltpu.SMEM)
VMEM = pl.BlockSpec(memory_space=pltpu.VMEM)
HBM = pl.BlockSpec(memory_space=pltpu.HBM)


def in_hbm(array):
    return pltpu.with_memory_space_constraint(array, pltpu.HBM)


def squares_kernel(frames_ref, out_ref, held_ref, arrived):
    chunks, columns = arrived.shape[0], frames_ref.shape[1]
    wide = columns // chunks
    copies = []
    for chunk in range(chunks):
        part = (slice(None), pl.ds(chunk * wide, wide))
        copies.append(
            pltpu.make_async_copy(frames_ref.at[part], held_ref.at[part], arrived.at[chunk])
        )
        copies[-1].start()
    total = None
    for chunk in range(chunks):
        copies[chunk].wait()
        for at in range(chunk * wide, (chunk + 1) * wide, HEAD):
            part = held_ref[:, at : at + HEAD].astype(jnp.float32)
            part = part * part
            total = part if total is None else total + part
    out_ref[...] = total


def partial_squares(frames):
    rows, columns = frames.shape
    chunks = 2 if columns % (2 * HEAD) == 0 else 1
    return pl.pallas_call(
        squares_kernel,
        out_shape=(
            jax.ShapeDtypeStruct((rows, HEAD), jnp.float32),
            jax.ShapeDtypeStruct(frames.shape, frames.dtype),
        ),
        in_specs=[HBM],
        out_specs=(VMEM, VMEM),
        scratch_shapes=[pltpu.SemaphoreType.DMA((chunks,))],
        compiler_params=params(8),
        cost_estimate=cost(2 * rows * columns, 2 * rows * columns),
        name="partial_squares",
    )(in_hbm(frames))


def products(normed_ref, half, key_ref, value_ref, out_ref):
    width = key_ref.shape[1] // 2
    columns = pl.ds(pl.multiple_of(half * width, width), width)
    out_ref[:, :width] = dot(normed_ref[...], key_ref[:, columns])
    out_ref[:, width:] = dot(normed_ref[...], value_ref[:, columns])


def send_kernel(
    features, index_ref, frames_ref, own_ref, other_ref, gain_ref, key_ref, value_ref, normed_ref, out_ref
):
    squares = jnp.sum(own_ref[...] + other_ref[...], axis=1, keepdims=True)
    inverse_rms = lax.rsqrt(squares / features + epsilon)
    normed_ref[...] = (
        frames_ref[...].astype(jnp.float32) * inverse_rms * gain_ref[...]
    ).astype(jnp.bfloat16)
    products(normed_ref, 1 - index_ref[0], key_ref, value_ref, out_ref)


def send_products(index, frames, own, other, gain, key, value, features):
    rows, columns = frames.shape
    width = key.shape[1]
    return pl.pallas_call(
        functools.partial(send_kernel, features),
        out_shape=(
            jax.ShapeDtypeStruct(frames.shape, jnp.bfloat16),
            jax.ShapeDtypeStruct((rows, width), jnp.float32),
        ),
        in_specs=[SMEM] + [VMEM] * 6,
        out_specs=(VMEM, VMEM),
        compiler_params=params(16),
        cost_estimate=cost(2 * rows * columns * width, 2 * key.size),
        name="send_products",
    )(index, frames, own, other, gain, key, value)


def keep_kernel(index_ref, normed_ref, key_ref, value_ref, out_ref):
    products(normed_ref, index_ref[0], key_ref, value_ref, out_ref)


def keep_products(index, normed, key, value):
    rows, columns = normed.shape
    width = key.shape[1]
    return pl.pallas_call(
        keep_kernel,
        out_shape=jax.ShapeDtypeStruct((rows, width), jnp.float32),
        in_specs=[SMEM] + [VMEM] * 3,
        out_specs=VMEM,
        compiler_params=params(16),
        cost_estimate=cost(2 * rows * columns * width, 2 * key.size),
        name="keep_products",
    )(index, normed, key, value)


def first_masks(groups, members):
    if groups & (groups - 1) or members & (members - 1) or members < 4:
        return None
    masks = [group * members + low for group in range(groups) for low in range(2)]
    return (0, masks[-1], *masks[1:-1])


def ring_place(device, members):
    upper = (device & (members - 1)) >> 1
    place = upper
    for shift in range(1, (members // 2).bit_length() - 1):
        place = place ^ (upper >> shift)
    return place


def second_pairs(partitions, members):
    line = members // 2
    devices = range(partitions)
    at = {(d // members, d & 1, ring_place(d, members)): d for d in devices}
    return [
        [(d, at[d // members, d & 1, (ring_place(d, members) + up) % line]) for d in devices]
        for up in range(line)
    ]


def route(per_shard, capacity, near, members, here, session, pick_ref, ids_ref):
    slots, rows = pick_ref.shape
    partitions = slots // capacity
    line = members // 2
    target = lax.div(session, per_shard)
    local = session - target * per_shard
    apart = (target ^ here) & functools.reduce(lambda a, b: a | b, near)
    first = sum(jnp.where(apart == mask, at, 0) for at, mask in enumerate(near))
    second = (ring_place(target, members) - ring_place(here, members)) & (line - 1)
    leaves, lands = first * line + second, second * len(near) + first
    to = lax.broadcasted_iota(jnp.int32, (partitions, rows), 0) == leaves
    to = to.astype(jnp.float32)
    earlier = lax.broadcasted_iota(jnp.int32, (rows, rows), 0) < lax.broadcasted_iota(
        jnp.int32, (rows, rows), 1
    )
    ahead = dot(to.astype(jnp.bfloat16), earlier.astype(jnp.bfloat16))
    order = jnp.sum(to * ahead, axis=0, keepdims=True).astype(jnp.int32)
    place = lax.broadcasted_iota(jnp.int32, (slots, rows), 0)
    pick_ref[...] = (place == leaves * capacity + order).astype(jnp.bfloat16)
    lane = lands * capacity + order
    parts = slots // HEAD
    block = lax.broadcasted_iota(jnp.int32, (ids_ref.shape[0], rows), 0)
    named = block == first * (ids_ref.shape[0] // len(near)) + second * parts + lane // HEAD
    named = jnp.where(named, (local + 1).astype(jnp.float32), 0.0).astype(jnp.bfloat16)
    spot = lax.broadcasted_iota(jnp.int32, (HEAD, rows), 0) == lane % HEAD
    ids_ref[...] = nt_dot(named, spot.astype(jnp.bfloat16))


def queries_of(queries_ref, head):
    columns = [
        queries_ref[:, at * HEAD : (at + 1) * HEAD].astype(jnp.float32)
        for at in range(head * GROUP, (head + 1) * GROUP)
    ]
    return jnp.concatenate(columns, axis=0).astype(jnp.bfloat16)


def score_cache(start_ref, len_ref, queries_ref, key_ref, out_ref, laid_ref):
    sessions, window, width = key_ref.shape
    heads, rows = width // HEAD, GROUP * sessions

    def by_row(ref):
        mine = lax.broadcasted_iota(jnp.int32, (rows, sessions), 0) % sessions
        mine = mine == lax.broadcasted_iota(jnp.int32, (rows, sessions), 1)
        values = jnp.where(mine, ref[...].astype(jnp.float32), 0.0)
        return jnp.sum(values, axis=1, keepdims=True).astype(jnp.int32)

    since = lax.broadcasted_iota(jnp.int32, (rows, window), 1) - by_row(start_ref)
    since = jnp.where(since < 0, since + window, since)
    live = since < by_row(len_ref)
    row_session = lax.broadcasted_iota(jnp.int32, (rows, window), 0) % sessions
    laid_ref[...] = jnp.zeros_like(laid_ref)
    for head in range(heads):
        query = queries_of(queries_ref, head)
        laid_ref[head * rows : (head + 1) * rows, head * HEAD : (head + 1) * HEAD] = query
        total = jnp.zeros((rows, window), jnp.float32)
        for session in range(sessions):
            key = key_ref[session, :, head * HEAD : (head + 1) * HEAD]
            total = jnp.where(row_session == session, nt_dot(query, key), total)
        total = jnp.where(live, total * (HEAD**-0.5), -jnp.inf)
        out_ref[head * rows : (head + 1) * rows] = total


def beside_kernel(
    per_shard,
    capacity,
    near,
    members,
    here_ref,
    session_ref,
    w_key_ref,
    w_value_ref,
    held_key_ref,
    held_value_ref,
    pick_ref,
    ids_ref,
    session,
    arrived,
):
    copies = []
    for at, (source, held) in enumerate(
        (
            (session_ref, session),
            (w_key_ref, held_key_ref),
            (w_value_ref, held_value_ref),
        )
    ):
        copies.append(pltpu.make_async_copy(source, held, arrived.at[at]))
        copies[-1].start()
    copies[0].wait()
    route(per_shard, capacity, near, members, here_ref[0], session[...], pick_ref, ids_ref)
    for copy in copies[1:]:
        copy.wait()


def beside(here, session, w_key, w_value, sizes):
    partitions, _, capacity, near, _ = sizes
    slots, rows = partitions * capacity, session.shape[1]
    id_rows = -(-partitions // len(near) * slots // (16 * HEAD)) * 16 * len(near)
    return pl.pallas_call(
        functools.partial(beside_kernel, *sizes[1:]),
        out_shape=(
            jax.ShapeDtypeStruct(w_key.shape, w_key.dtype),
            jax.ShapeDtypeStruct(w_value.shape, w_value.dtype),
            jax.ShapeDtypeStruct((slots, rows), jnp.bfloat16),
            jax.ShapeDtypeStruct((id_rows, HEAD), jnp.float32),
        ),
        in_specs=[SMEM] + [HBM] * 3,
        out_specs=(VMEM,) * 4,
        scratch_shapes=[pltpu.VMEM(session.shape, session.dtype), pltpu.SemaphoreType.DMA((3,))],
        compiler_params=params(24),
        cost_estimate=cost(4 * rows * rows * slots, 4 * w_key.size),
        name="beside",
    )(here, in_hbm(session), in_hbm(w_key), in_hbm(w_value))


def cached_scores(start, length, queries, cache_key):
    sessions, window, width = cache_key.shape
    rows = width // HEAD * GROUP * sessions
    return pl.pallas_call(
        score_cache,
        out_shape=(
            jax.ShapeDtypeStruct((rows, window), jnp.float32),
            jax.ShapeDtypeStruct((rows, width), jnp.bfloat16),
        ),
        in_specs=[VMEM] * 4,
        out_specs=(VMEM, VMEM),
        compiler_params=params(8),
        cost_estimate=cost(2 * GROUP * sessions * cache_key.size, 2 * cache_key.size),
        name="cached_scores",
    )(start, length, queries, cache_key)


def pack_kernel(pick_ref, ids_ref, kept_ref, got_ref, key_bias_ref, value_bias_ref, *out_refs):
    width = key_bias_ref.shape[1]
    sums = kept_ref[...] + got_ref[...]
    key = (sums[:, :width] + key_bias_ref[...]).astype(jnp.bfloat16)
    value = (sums[:, width:] + value_bias_ref[...]).astype(jnp.bfloat16)
    tall = pick_ref.shape[0] // len(out_refs)
    at = 0
    for source in (key, value):
        laid = dot(pick_ref[...], source).astype(jnp.bfloat16)
        for column in range(0, width, HEAD):
            for step, out_ref in enumerate(out_refs):
                out_ref[at : at + tall, :] = laid[
                    step * tall : (step + 1) * tall, column : column + HEAD
                ]
            at += tall
    named = ids_ref.shape[0] // len(out_refs)
    for step, out_ref in enumerate(out_refs):
        out_ref[at:, :] = ids_ref[step * named : (step + 1) * named, :].astype(jnp.bfloat16)


def pack(pick, ids, kept, got, key_bias, value_bias, near):
    rows, width = kept.shape
    slots = pick.shape[0]
    tall = (width // HEAD * slots + ids.shape[0]) // near
    return pl.pallas_call(
        pack_kernel,
        out_shape=[jax.ShapeDtypeStruct((tall, HEAD), jnp.bfloat16)] * near,
        in_specs=[VMEM] * 6,
        out_specs=[VMEM] * near,
        compiler_params=params(8),
        cost_estimate=cost(2 * rows * width * slots, 8 * rows * width),
        name="pack",
    )(pick, ids, kept, got, key_bias, value_bias)


def regroup_kernel(near, vectors, capacity, *refs):
    got_refs, out_refs = refs[:near], refs[near:]
    far = len(out_refs)
    for vector in range(vectors):
        for step, out_ref in enumerate(out_refs):
            for first, got_ref in enumerate(got_refs):
                to, at = (vector * near + first) * capacity, (vector * far + step) * capacity
                out_ref[to : to + capacity, :] = got_ref[at : at + capacity, :]
    ids = sum(ref[vectors * far * capacity :, :].astype(jnp.float32) for ref in got_refs)
    for out_ref in out_refs:
        out_ref[vectors * near * capacity :, :] = ids.astype(jnp.bfloat16)


def regroup(blocks, far, vectors, capacity):
    near = len(blocks)
    tall = blocks[0].shape[0] + vectors * capacity * (near - far)
    return pl.pallas_call(
        functools.partial(regroup_kernel, near, vectors, capacity),
        out_shape=[jax.ShapeDtypeStruct((tall, HEAD), jnp.bfloat16)] * far,
        in_specs=[VMEM] * near,
        out_specs=[VMEM] * far,
        compiler_params=params(8),
        cost_estimate=cost(0, 4 * near * blocks[0].size),
        name="regroup",
    )(*blocks)


def rows_of(refs, vectors, tall):
    columns = []
    for vector in vectors:
        part = slice(vector * tall, (vector + 1) * tall)
        columns.append(jnp.concatenate([ref[part, :] for ref in refs], axis=0))
    return jnp.concatenate(columns, axis=1)


def score_fresh(refs, begin, parts, tall, heads, sessions, queries):
    rows, slots = queries.shape[0], len(refs) * tall
    first = begin * tall // HEAD
    ids = [
        sum(
            ref[2 * heads * tall :, :].astype(jnp.float32)[at : at + 1]
            for ref, at in ((ref, (begin + k) * parts + part) for k, ref in enumerate(refs))
        )
        for part in range(first, first + slots // HEAD)
    ]
    ids = jnp.concatenate(ids, axis=1).astype(jnp.int32)
    own = lax.broadcasted_iota(jnp.int32, (rows, slots), 0) % sessions + 1 == ids
    fresh = nt_dot(queries, rows_of(refs, range(heads), tall)) * (HEAD**-0.5)
    return jnp.where(own, fresh, -jnp.inf)


def early_kernel(tall, parts, sessions, queries_ref, *refs):
    *got_refs, out_ref = refs
    heads = queries_ref.shape[1] // HEAD
    out_ref[...] = score_fresh(got_refs, 0, parts, tall, heads, sessions, queries_ref[...])


def early_scores(got, queries, tall, parts, sessions):
    rows = queries.shape[0]
    return pl.pallas_call(
        functools.partial(early_kernel, tall, parts, sessions),
        out_shape=jax.ShapeDtypeStruct((rows, len(got) * tall), jnp.float32),
        in_specs=[VMEM] * (1 + len(got)),
        out_specs=VMEM,
        compiler_params=params(8),
        cost_estimate=cost(2 * rows * len(got) * tall * queries.shape[1], 2 * queries.size),
        name="early_scores",
    )(queries, *got)


def attend_kernel(near, capacity, queries_ref, score_ref, early_ref, cache_ref, *refs):
    *got_refs, out_ref = refs
    rows, window = score_ref.shape
    sessions, _, width = cache_ref.shape
    heads = width // HEAD
    tall = near * capacity
    parts = len(got_refs) * tall // HEAD
    begin = early_ref.shape[1] // tall
    cached = score_ref[...]
    late = score_fresh(got_refs[begin:], begin, parts, tall, heads, sessions, queries_ref[...])
    fresh = jnp.concatenate([early_ref[...], late], axis=1)
    largest = jnp.maximum(
        jnp.max(cached, axis=1, keepdims=True), jnp.max(fresh, axis=1, keepdims=True)
    )
    cached = jnp.exp(cached - largest)
    fresh = jnp.exp(fresh - largest)
    total = jnp.sum(cached, axis=1, keepdims=True) + jnp.sum(fresh, axis=1, keepdims=True)
    cached = cached / total
    attended = dot((fresh / total).astype(jnp.bfloat16), rows_of(got_refs, range(heads, 2 * heads), tall))
    row_session = lax.broadcasted_iota(jnp.int32, (rows, window), 0) % sessions
    for session in range(0, sessions, 2):
        weights = jnp.concatenate(
            [jnp.where(row_session == session + more, cached, 0.0) for more in range(2)], axis=1
        )
        values = cache_ref[session : session + 2].reshape(2 * window, width)
        attended += dot(weights.astype(jnp.bfloat16), values)
    for head in range(heads):
        for q in range(GROUP):
            row, column = (head * GROUP + q) * sessions, (head * GROUP + q) * HEAD
            out_ref[:, column : column + HEAD] = attended[
                row : row + sessions, head * HEAD : (head + 1) * HEAD
            ].astype(jnp.bfloat16)


def attend(got, queries, scores, early, cache_value, near, capacity):
    return pl.pallas_call(
        functools.partial(attend_kernel, near, capacity),
        out_shape=jax.ShapeDtypeStruct(
            (cache_value.shape[0], queries.shape[1] * GROUP), jnp.bfloat16
        ),
        in_specs=[VMEM] * (4 + len(got)),
        out_specs=VMEM,
        compiler_params=params(8),
        cost_estimate=cost(4 * queries.shape[0] * cache_value.size, 2 * cache_value.size),
        name="attend",
    )(queries, scores, early, cache_value, *got)


def project(frame_rows, ln_gain, w_key, w_value, k_bias, v_bias):
    values32 = frame_rows.astype(jnp.float32)
    partial_squares = jnp.sum(values32 * values32, axis=1)
    squares = lax.psum(partial_squares, "mp")
    inverse_rms = lax.rsqrt(squares / (frame_rows.shape[1] * lax.axis_size("mp")) + epsilon)
    normed = (values32 * inverse_rms[:, None] * ln_gain[None, :]).astype(jnp.bfloat16)
    part_key = jnp.dot(normed, w_key, preferred_element_type=jnp.float32)
    part_value = jnp.dot(normed, w_value, preferred_element_type=jnp.float32)
    key_sums, value_sums = (
        lax.psum_scatter(part_key, "mp", scatter_dimension=1, tiled=True),
        lax.psum_scatter(part_value, "mp", scatter_dimension=1, tiled=True),
    )
    new_keys = (key_sums + k_bias[None, :]).astype(jnp.bfloat16)
    new_values = (value_sums + v_bias[None, :]).astype(jnp.bfloat16)
    return (new_keys, new_values)


def slot_sources(token_session, per_shard, partition_count, capacity):
    row_count = token_session.shape[0]
    target = token_session // per_shard
    one_hot = (target[:, None] == jnp.arange(partition_count, dtype=jnp.int32)[None, :]).astype(
        jnp.int32
    )
    order_in = jnp.sum((jnp.cumsum(one_hot, axis=0) - one_hot) * one_hot, axis=1)
    slot_index = target * capacity + order_in
    matches = (
        slot_index[None, :] == jnp.arange(partition_count * capacity, dtype=jnp.int32)[:, None]
    )
    source = jnp.sum(jnp.where(matches, jnp.arange(row_count, dtype=jnp.int32)[None, :], 0), axis=1)
    filled = jnp.any(matches, axis=1)
    sessions = jnp.where(filled, jnp.mod(token_session[source], per_shard), -1)
    return (source, filled, sessions)


def general(
    frames,
    token_session,
    ln_gain,
    w_key,
    w_value,
    k_bias,
    v_bias,
    queries,
    cache_key,
    cache_value,
    cache_start,
    cache_len,
):
    partition_count = lax.axis_size(("grp", "seq"))
    per_shard = queries.shape[0]
    rows_here = frames.shape[0]
    capacity = max(2, 5 * rows_here // (2 * partition_count) + 1)
    source, filled, sessions = slot_sources(token_session, per_shard, partition_count, capacity)
    session_slots = sessions.reshape(partition_count, capacity)
    nothing = jnp.zeros((), jnp.bfloat16)
    own_keys, own_values = project(frames, ln_gain, w_key, w_value, k_bias, v_bias)
    send_keys = jnp.where(filled[:, None], own_keys[source], nothing).reshape(
        partition_count, capacity, -1
    )
    send_values = jnp.where(filled[:, None], own_values[source], nothing).reshape(
        partition_count, capacity, -1
    )
    got_keys, got_values, got_sessions = (
        lax.all_to_all(send_keys, ("grp", "seq"), split_axis=0, concat_axis=0, tiled=True),
        lax.all_to_all(send_values, ("grp", "seq"), split_axis=0, concat_axis=0, tiled=True),
        lax.all_to_all(session_slots, ("grp", "seq"), split_axis=0, concat_axis=0, tiled=True),
    )
    new_keys = got_keys.reshape(partition_count * capacity, -1)
    new_values = got_values.reshape(partition_count * capacity, -1)
    new_sessions = got_sessions.reshape(-1)
    heads_kv = new_keys.shape[1] // HEAD
    window = cache_key.shape[1]
    score_scale = HEAD ** (-0.5)
    query_heads = queries.reshape(per_shard, heads_kv, GROUP, HEAD)
    cached_keys = cache_key.reshape(per_shard, window, heads_kv, HEAD)
    cached_values = cache_value.reshape(per_shard, window, heads_kv, HEAD)
    fresh_keys = new_keys.reshape(-1, heads_kv, HEAD)
    fresh_values = new_values.reshape(-1, heads_kv, HEAD)
    cached_scores = (
        jnp.einsum("sghd,swgd->sghw", query_heads, cached_keys, preferred_element_type=jnp.float32)
        * score_scale
    )
    positions = jnp.arange(window, dtype=jnp.int32)
    live_slots = jnp.mod(positions[None, :] - cache_start[:, None], window) < cache_len[:, None]
    cached_scores = jnp.where(live_slots[:, None, None, :], cached_scores, -jnp.inf)
    fresh_scores = (
        jnp.einsum("sghd,ngd->sghn", query_heads, fresh_keys, preferred_element_type=jnp.float32)
        * score_scale
    )
    own_rows = new_sessions[None, :] == jnp.arange(per_shard, dtype=jnp.int32)[:, None]
    fresh_scores = jnp.where(own_rows[:, None, None, :], fresh_scores, -jnp.inf)
    largest = jnp.maximum(jnp.max(cached_scores, axis=3), jnp.max(fresh_scores, axis=3))
    cached_exp = jnp.exp(cached_scores - largest[..., None])
    fresh_exp = jnp.exp(fresh_scores - largest[..., None])
    totals = jnp.sum(cached_exp, axis=3) + jnp.sum(fresh_exp, axis=3)
    cached_weights = (cached_exp / totals[..., None]).astype(jnp.bfloat16)
    fresh_weights = (fresh_exp / totals[..., None]).astype(jnp.bfloat16)
    attended = jnp.einsum(
        "sghw,swgd->sghd", cached_weights, cached_values, preferred_element_type=jnp.float32
    )
    attended = attended + jnp.einsum(
        "sghn,ngd->sghd", fresh_weights, fresh_values, preferred_element_type=jnp.float32
    )
    return attended.reshape(per_shard, -1).astype(jnp.bfloat16)


def local(
    frames,
    token_session,
    ln_gain,
    w_key,
    w_value,
    k_bias,
    v_bias,
    queries,
    cache_key,
    cache_value,
    cache_start,
    cache_len,
):
    partitions = lax.axis_size(("grp", "seq"))
    shares = lax.axis_size("mp")
    per_shard = queries.shape[0]
    rows = frames.shape[0]
    capacity = max(2, 5 * rows // (2 * partitions) + 1)
    members = lax.axis_size("seq")
    near = first_masks(lax.axis_size("grp"), members)
    if near is None or shares != 2 or per_shard % 8 or capacity % 16 or partitions * capacity % (2 * HEAD):
        return general(
            frames, token_session, ln_gain, w_key, w_value, k_bias, v_bias, queries, cache_key, cache_value,
            cache_start, cache_len,
        )
    swap = [(0, 1), (1, 0)]
    index = lax.axis_index("mp").astype(jnp.int32).reshape(1)
    here = lax.axis_index(("grp", "seq")).astype(jnp.int32).reshape(1)
    own, held = partial_squares(frames)
    other = lax.ppermute(own, "mp", swap)
    held_key, held_value, pick, ids = beside(
        here, token_session[None, :], w_key, w_value, (partitions, per_shard, capacity, near, members)
    )
    normed, sent = send_products(
        index, held, own, other, ln_gain[None, :], held_key, held_value, frames.shape[1] * shares
    )
    arrived = lax.ppermute(sent, "mp", swap)
    kept = keep_products(index, normed, held_key, held_value)
    blocks = pack(pick, ids, kept, arrived, k_bias[None, :], v_bias[None, :], len(near))

    def step(arrays, pairs):
        sent = [lax.ppermute(a, ("grp", "seq"), p) for a, p in zip(arrays[1:], pairs[1:])]
        return [arrays[0], *sent]

    queries, *blocks = lax.optimization_barrier((queries, *blocks))
    scores, laid = cached_scores(cache_start[None, :], cache_len[None, :], queries, cache_key)
    vectors = 2 * cache_key.shape[2] // HEAD
    blocks = step(blocks, [[(i, i ^ mask) for i in range(partitions)] for mask in near])
    blocks = regroup(blocks, members // 2, vectors, capacity)
    blocks = step(blocks, second_pairs(partitions, members))
    tall, line = len(near) * capacity, members // 2
    early = early_scores(blocks[: line // 2], laid, tall, line * tall // HEAD, per_shard)
    return attend(blocks, laid, scores, early, cache_value, len(near), capacity)


def solution(mesh):
    return jax.shard_map(
        local,
        mesh=mesh,
        in_specs=(
            P(("grp", "seq"), "mp"),
            P(("grp", "seq")),
            P("mp"),
            P("mp", None),
            P("mp", None),
            P("mp"),
            P("mp"),
            P(("grp", "seq"), "mp"),
            P(("grp", "seq"), None, "mp"),
            P(("grp", "seq"), None, "mp"),
            P(("grp", "seq")),
            P(("grp", "seq")),
        ),
        out_specs=P(("grp", "seq"), "mp"),
        check_vma=False,
    )
```

```python
import functools

import jax
import jax.numpy as jnp
from jax import lax
from jax.experimental import pallas as pl
from jax.experimental.pallas import tpu as pltpu
from jax.sharding import PartitionSpec as P

HEAD = 128
GROUP = 8

epsilon = 1e-06


def params(mib):
    return pltpu.CompilerParams(vmem_limit_bytes=mib << 20)


def cost(flops, nbytes):
    return pl.CostEstimate(flops=flops, bytes_accessed=nbytes, transcendentals=0)


def nt_dot(a, b):
    return lax.dot_general(a, b, (((1,), (1,)), ((), ())), preferred_element_type=jnp.float32)


def dot(a, b):
    return jnp.dot(a, b, preferred_element_type=jnp.float32)


SMEM = pl.BlockSpec(memory_space=pltpu.SMEM)
VMEM = pl.BlockSpec(memory_space=pltpu.VMEM)
HBM = pl.BlockSpec(memory_space=pltpu.HBM)


def in_hbm(array):
    return pltpu.with_memory_space_constraint(array, pltpu.HBM)


def squares_kernel(frames_ref, out_ref, held_ref, arrived):
    chunks, columns = arrived.shape[0], frames_ref.shape[1]
    wide = columns // chunks
    copies = []
    for chunk in range(chunks):
        part = (slice(None), pl.ds(chunk * wide, wide))
        copies.append(
            pltpu.make_async_copy(frames_ref.at[part], held_ref.at[part], arrived.at[chunk])
        )
        copies[-1].start()
    total = None
    for chunk in range(chunks):
        copies[chunk].wait()
        for at in range(chunk * wide, (chunk + 1) * wide, HEAD):
            part = held_ref[:, at : at + HEAD].astype(jnp.float32)
            part = part * part
            total = part if total is None else total + part
    out_ref[...] = total


def partial_squares(frames):
    rows, columns = frames.shape
    chunks = 2 if columns % (2 * HEAD) == 0 else 1
    return pl.pallas_call(
        squares_kernel,
        out_shape=(
            jax.ShapeDtypeStruct((rows, HEAD), jnp.float32),
            jax.ShapeDtypeStruct(frames.shape, frames.dtype),
        ),
        in_specs=[HBM],
        out_specs=(VMEM, VMEM),
        scratch_shapes=[pltpu.SemaphoreType.DMA((chunks,))],
        compiler_params=params(8),
        cost_estimate=cost(2 * rows * columns, 2 * rows * columns),
        name="partial_squares",
    )(in_hbm(frames))


def products(normed_ref, half, key_ref, value_ref, out_ref):
    width = key_ref.shape[1] // 2
    columns = pl.ds(pl.multiple_of(half * width, width), width)
    out_ref[:, :width] = dot(normed_ref[...], key_ref[:, columns])
    out_ref[:, width:] = dot(normed_ref[...], value_ref[:, columns])


def send_kernel(
    features, index_ref, frames_ref, own_ref, other_ref, gain_ref, key_ref, value_ref, normed_ref, out_ref
):
    squares = jnp.sum(own_ref[...] + other_ref[...], axis=1, keepdims=True)
    inverse_rms = lax.rsqrt(squares / features + epsilon)
    normed_ref[...] = (
        frames_ref[...].astype(jnp.float32) * inverse_rms * gain_ref[...]
    ).astype(jnp.bfloat16)
    products(normed_ref, 1 - index_ref[0], key_ref, value_ref, out_ref)


def send_products(index, frames, own, other, gain, key, value, features):
    rows, columns = frames.shape
    width = key.shape[1]
    return pl.pallas_call(
        functools.partial(send_kernel, features),
        out_shape=(
            jax.ShapeDtypeStruct(frames.shape, jnp.bfloat16),
            jax.ShapeDtypeStruct((rows, width), jnp.float32),
        ),
        in_specs=[SMEM] + [VMEM] * 6,
        out_specs=(VMEM, VMEM),
        compiler_params=params(16),
        cost_estimate=cost(2 * rows * columns * width, 2 * key.size),
        name="send_products",
    )(index, frames, own, other, gain, key, value)


def keep_kernel(index_ref, normed_ref, key_ref, value_ref, out_ref):
    products(normed_ref, index_ref[0], key_ref, value_ref, out_ref)


def keep_products(index, normed, key, value):
    rows, columns = normed.shape
    width = key.shape[1]
    return pl.pallas_call(
        keep_kernel,
        out_shape=jax.ShapeDtypeStruct((rows, width), jnp.float32),
        in_specs=[SMEM] + [VMEM] * 3,
        out_specs=VMEM,
        compiler_params=params(16),
        cost_estimate=cost(2 * rows * columns * width, 2 * key.size),
        name="keep_products",
    )(index, normed, key, value)


def first_masks(groups, members):
    if groups & (groups - 1) or members & (members - 1) or members < 4:
        return None
    masks = [group * members + low for group in range(groups) for low in range(2)]
    return (0, masks[-1], *masks[1:-1])


def ring_place(device, members):
    upper = (device & (members - 1)) >> 1
    place = upper
    for shift in range(1, (members // 2).bit_length() - 1):
        place = place ^ (upper >> shift)
    return place


def second_pairs(partitions, members):
    line = members // 2
    devices = range(partitions)
    at = {(d // members, d & 1, ring_place(d, members)): d for d in devices}
    return [
        [(d, at[d // members, d & 1, (ring_place(d, members) + up) % line]) for d in devices]
        for up in range(line)
    ]


def route(per_shard, capacity, near, members, here, session, pick_ref, ids_ref):
    slots, rows = pick_ref.shape
    partitions = slots // capacity
    line = members // 2
    target = lax.div(session, per_shard)
    local = session - target * per_shard
    apart = (target ^ here) & functools.reduce(lambda a, b: a | b, near)
    first = sum(jnp.where(apart == mask, at, 0) for at, mask in enumerate(near))
    second = (ring_place(target, members) - ring_place(here, members)) & (line - 1)
    leaves, lands = first * line + second, second * len(near) + first
    to = lax.broadcasted_iota(jnp.int32, (partitions, rows), 0) == leaves
    to = to.astype(jnp.float32)
    earlier = lax.broadcasted_iota(jnp.int32, (rows, rows), 0) < lax.broadcasted_iota(
        jnp.int32, (rows, rows), 1
    )
    ahead = dot(to.astype(jnp.bfloat16), earlier.astype(jnp.bfloat16))
    order = jnp.sum(to * ahead, axis=0, keepdims=True).astype(jnp.int32)
    place = lax.broadcasted_iota(jnp.int32, (slots, rows), 0)
    pick_ref[...] = (place == leaves * capacity + order).astype(jnp.bfloat16)
    lane = lands * capacity + order
    parts = slots // HEAD
    block = lax.broadcasted_iota(jnp.int32, (ids_ref.shape[0], rows), 0)
    named = block == first * (ids_ref.shape[0] // len(near)) + second * parts + lane // HEAD
    named = jnp.where(named, (local + 1).astype(jnp.float32), 0.0).astype(jnp.bfloat16)
    spot = lax.broadcasted_iota(jnp.int32, (HEAD, rows), 0) == lane % HEAD
    ids_ref[...] = nt_dot(named, spot.astype(jnp.bfloat16))


def queries_of(queries_ref, head):
    columns = [
        queries_ref[:, at * HEAD : (at + 1) * HEAD].astype(jnp.float32)
        for at in range(head * GROUP, (head + 1) * GROUP)
    ]
    return jnp.concatenate(columns, axis=0).astype(jnp.bfloat16)


def score_cache(start_ref, len_ref, queries_ref, key_ref, out_ref, laid_ref):
    sessions, window, width = key_ref.shape
    heads, rows = width // HEAD, GROUP * sessions

    def by_row(ref):
        mine = lax.broadcasted_iota(jnp.int32, (rows, sessions), 0) % sessions
        mine = mine == lax.broadcasted_iota(jnp.int32, (rows, sessions), 1)
        values = jnp.where(mine, ref[...].astype(jnp.float32), 0.0)
        return jnp.sum(values, axis=1, keepdims=True).astype(jnp.int32)

    since = lax.broadcasted_iota(jnp.int32, (rows, window), 1) - by_row(start_ref)
    since = jnp.where(since < 0, since + window, since)
    live = since < by_row(len_ref)
    row_session = lax.broadcasted_iota(jnp.int32, (rows, window), 0) % sessions
    laid_ref[...] = jnp.zeros_like(laid_ref)
    for head in range(heads):
        query = queries_of(queries_ref, head)
        laid_ref[head * rows : (head + 1) * rows, head * HEAD : (head + 1) * HEAD] = query
        total = jnp.zeros((rows, window), jnp.float32)
        for session in range(sessions):
            key = key_ref[session, :, head * HEAD : (head + 1) * HEAD]
            total = jnp.where(row_session == session, nt_dot(query, key), total)
        total = jnp.where(live, total * (HEAD**-0.5), -jnp.inf)
        out_ref[head * rows : (head + 1) * rows] = total


def beside_kernel(
    per_shard,
    capacity,
    near,
    members,
    here_ref,
    session_ref,
    w_key_ref,
    w_value_ref,
    gain_ref,
    key_bias_ref,
    value_bias_ref,
    held_key_ref,
    held_value_ref,
    held_gain_ref,
    held_key_bias_ref,
    held_value_bias_ref,
    pick_ref,
    ids_ref,
    session,
    arrived,
):
    copies = []
    for at, (source, held) in enumerate(
        (
            (session_ref, session),
            (w_key_ref, held_key_ref),
            (w_value_ref, held_value_ref),
            (gain_ref, held_gain_ref),
            (key_bias_ref, held_key_bias_ref),
            (value_bias_ref, held_value_bias_ref),
        )
    ):
        copies.append(pltpu.make_async_copy(source, held, arrived.at[at]))
        copies[-1].start()
    copies[0].wait()
    route(per_shard, capacity, near, members, here_ref[0], session[...], pick_ref, ids_ref)
    for copy in copies[1:]:
        copy.wait()


def beside(here, session, weights, sizes):
    partitions, _, capacity, near, _ = sizes
    slots, rows = partitions * capacity, session.shape[1]
    id_rows = -(-partitions // len(near) * slots // (16 * HEAD)) * 16 * len(near)
    return pl.pallas_call(
        functools.partial(beside_kernel, *sizes[1:]),
        out_shape=(
            *(jax.ShapeDtypeStruct(array.shape, array.dtype) for array in weights),
            jax.ShapeDtypeStruct((slots, rows), jnp.bfloat16),
            jax.ShapeDtypeStruct((id_rows, HEAD), jnp.float32),
        ),
        in_specs=[SMEM] + [HBM] * (1 + len(weights)),
        out_specs=(VMEM,) * (2 + len(weights)),
        scratch_shapes=[
            pltpu.VMEM(session.shape, session.dtype),
            pltpu.SemaphoreType.DMA((1 + len(weights),)),
        ],
        compiler_params=params(24),
        cost_estimate=cost(4 * rows * rows * slots, 4 * weights[0].size),
        name="beside",
    )(here, in_hbm(session), *map(in_hbm, weights))


def cached_scores(start, length, queries, cache_key):
    sessions, window, width = cache_key.shape
    rows = width // HEAD * GROUP * sessions
    return pl.pallas_call(
        score_cache,
        out_shape=(
            jax.ShapeDtypeStruct((rows, window), jnp.float32),
            jax.ShapeDtypeStruct((rows, width), jnp.bfloat16),
        ),
        in_specs=[VMEM] * 4,
        out_specs=(VMEM, VMEM),
        compiler_params=params(8),
        cost_estimate=cost(2 * GROUP * sessions * cache_key.size, 2 * cache_key.size),
        name="cached_scores",
    )(start, length, queries, cache_key)


def pack_kernel(pick_ref, ids_ref, kept_ref, got_ref, key_bias_ref, value_bias_ref, *out_refs):
    width = key_bias_ref.shape[1]
    sums = kept_ref[...] + got_ref[...]
    key = (sums[:, :width] + key_bias_ref[...]).astype(jnp.bfloat16)
    value = (sums[:, width:] + value_bias_ref[...]).astype(jnp.bfloat16)
    tall = pick_ref.shape[0] // len(out_refs)
    at = 0
    for source in (key, value):
        laid = dot(pick_ref[...], source).astype(jnp.bfloat16)
        for column in range(0, width, HEAD):
            for step, out_ref in enumerate(out_refs):
                out_ref[at : at + tall, :] = laid[
                    step * tall : (step + 1) * tall, column : column + HEAD
                ]
            at += tall
    named = ids_ref.shape[0] // len(out_refs)
    for step, out_ref in enumerate(out_refs):
        out_ref[at:, :] = ids_ref[step * named : (step + 1) * named, :].astype(jnp.bfloat16)


def pack(pick, ids, kept, got, key_bias, value_bias, near):
    rows, width = kept.shape
    slots = pick.shape[0]
    tall = (width // HEAD * slots + ids.shape[0]) // near
    return pl.pallas_call(
        pack_kernel,
        out_shape=[jax.ShapeDtypeStruct((tall, HEAD), jnp.bfloat16)] * near,
        in_specs=[VMEM] * 6,
        out_specs=[VMEM] * near,
        compiler_params=params(8),
        cost_estimate=cost(2 * rows * width * slots, 8 * rows * width),
        name="pack",
    )(pick, ids, kept, got, key_bias, value_bias)


def regroup_kernel(near, vectors, capacity, *refs):
    got_refs, out_refs = refs[:near], refs[near:]
    far = len(out_refs)
    for vector in range(vectors):
        for step, out_ref in enumerate(out_refs):
            for first, got_ref in enumerate(got_refs):
                to, at = (vector * near + first) * capacity, (vector * far + step) * capacity
                out_ref[to : to + capacity, :] = got_ref[at : at + capacity, :]
    ids = sum(ref[vectors * far * capacity :, :].astype(jnp.float32) for ref in got_refs)
    for out_ref in out_refs:
        out_ref[vectors * near * capacity :, :] = ids.astype(jnp.bfloat16)


def regroup(blocks, far, vectors, capacity):
    near = len(blocks)
    tall = blocks[0].shape[0] + vectors * capacity * (near - far)
    return pl.pallas_call(
        functools.partial(regroup_kernel, near, vectors, capacity),
        out_shape=[jax.ShapeDtypeStruct((tall, HEAD), jnp.bfloat16)] * far,
        in_specs=[VMEM] * near,
        out_specs=[VMEM] * far,
        compiler_params=params(8),
        cost_estimate=cost(0, 4 * near * blocks[0].size),
        name="regroup",
    )(*blocks)


def attend_kernel(near, capacity, queries_ref, score_ref, cache_ref, *refs):
    *got_refs, out_ref = refs
    rows, window = score_ref.shape
    sessions, _, width = cache_ref.shape
    heads = width // HEAD
    tall = near * capacity
    slots = len(got_refs) * tall
    parts = slots // HEAD
    ids = [
        sum(
            ref[2 * heads * tall :, :].astype(jnp.float32)[step * parts + part : step * parts + part + 1]
            for step, ref in enumerate(got_refs)
        )
        for part in range(parts)
    ]
    ids = jnp.concatenate(ids, axis=1).astype(jnp.int32)
    own = lax.broadcasted_iota(jnp.int32, (rows, slots), 0) % sessions + 1 == ids

    def rows_of(vectors):
        columns = []
        for vector in vectors:
            part = slice(vector * tall, (vector + 1) * tall)
            columns.append(jnp.concatenate([ref[part, :] for ref in got_refs], axis=0))
        return jnp.concatenate(columns, axis=1)

    cached = score_ref[...]
    fresh = nt_dot(queries_ref[...], rows_of(range(heads))) * (HEAD**-0.5)
    fresh = jnp.where(own, fresh, -jnp.inf)
    largest = jnp.maximum(
        jnp.max(cached, axis=1, keepdims=True), jnp.max(fresh, axis=1, keepdims=True)
    )
    cached = jnp.exp(cached - largest)
    fresh = jnp.exp(fresh - largest)
    total = jnp.sum(cached, axis=1, keepdims=True) + jnp.sum(fresh, axis=1, keepdims=True)
    cached = cached / total
    attended = dot((fresh / total).astype(jnp.bfloat16), rows_of(range(heads, 2 * heads)))
    row_session = lax.broadcasted_iota(jnp.int32, (rows, window), 0) % sessions
    for session in range(0, sessions, 2):
        weights = jnp.concatenate(
            [jnp.where(row_session == session + more, cached, 0.0) for more in range(2)], axis=1
        )
        values = cache_ref[session : session + 2].reshape(2 * window, width)
        attended += dot(weights.astype(jnp.bfloat16), values)
    for head in range(heads):
        for q in range(GROUP):
            row, column = (head * GROUP + q) * sessions, (head * GROUP + q) * HEAD
            out_ref[:, column : column + HEAD] = attended[
                row : row + sessions, head * HEAD : (head + 1) * HEAD
            ].astype(jnp.bfloat16)


def attend(got, queries, scores, cache_value, near, capacity):
    return pl.pallas_call(
        functools.partial(attend_kernel, near, capacity),
        out_shape=jax.ShapeDtypeStruct(
            (cache_value.shape[0], queries.shape[1] * GROUP), jnp.bfloat16
        ),
        in_specs=[VMEM] * (3 + len(got)),
        out_specs=VMEM,
        compiler_params=params(8),
        cost_estimate=cost(4 * queries.shape[0] * cache_value.size, 2 * cache_value.size),
        name="attend",
    )(queries, scores, cache_value, *got)


def project(frame_rows, ln_gain, w_key, w_value, k_bias, v_bias):
    values32 = frame_rows.astype(jnp.float32)
    partial_squares = jnp.sum(values32 * values32, axis=1)
    squares = lax.psum(partial_squares, "mp")
    inverse_rms = lax.rsqrt(squares / (frame_rows.shape[1] * lax.axis_size("mp")) + epsilon)
    normed = (values32 * inverse_rms[:, None] * ln_gain[None, :]).astype(jnp.bfloat16)
    part_key = jnp.dot(normed, w_key, preferred_element_type=jnp.float32)
    part_value = jnp.dot(normed, w_value, preferred_element_type=jnp.float32)
    key_sums, value_sums = (
        lax.psum_scatter(part_key, "mp", scatter_dimension=1, tiled=True),
        lax.psum_scatter(part_value, "mp", scatter_dimension=1, tiled=True),
    )
    new_keys = (key_sums + k_bias[None, :]).astype(jnp.bfloat16)
    new_values = (value_sums + v_bias[None, :]).astype(jnp.bfloat16)
    return (new_keys, new_values)


def slot_sources(token_session, per_shard, partition_count, capacity):
    row_count = token_session.shape[0]
    target = token_session // per_shard
    one_hot = (target[:, None] == jnp.arange(partition_count, dtype=jnp.int32)[None, :]).astype(
        jnp.int32
    )
    order_in = jnp.sum((jnp.cumsum(one_hot, axis=0) - one_hot) * one_hot, axis=1)
    slot_index = target * capacity + order_in
    matches = (
        slot_index[None, :] == jnp.arange(partition_count * capacity, dtype=jnp.int32)[:, None]
    )
    source = jnp.sum(jnp.where(matches, jnp.arange(row_count, dtype=jnp.int32)[None, :], 0), axis=1)
    filled = jnp.any(matches, axis=1)
    sessions = jnp.where(filled, jnp.mod(token_session[source], per_shard), -1)
    return (source, filled, sessions)


def general(
    frames,
    token_session,
    ln_gain,
    w_key,
    w_value,
    k_bias,
    v_bias,
    queries,
    cache_key,
    cache_value,
    cache_start,
    cache_len,
):
    partition_count = lax.axis_size(("grp", "seq"))
    per_shard = queries.shape[0]
    rows_here = frames.shape[0]
    capacity = max(2, 5 * rows_here // (2 * partition_count) + 1)
    source, filled, sessions = slot_sources(token_session, per_shard, partition_count, capacity)
    session_slots = sessions.reshape(partition_count, capacity)
    nothing = jnp.zeros((), jnp.bfloat16)
    own_keys, own_values = project(frames, ln_gain, w_key, w_value, k_bias, v_bias)
    send_keys = jnp.where(filled[:, None], own_keys[source], nothing).reshape(
        partition_count, capacity, -1
    )
    send_values = jnp.where(filled[:, None], own_values[source], nothing).reshape(
        partition_count, capacity, -1
    )
    got_keys, got_values, got_sessions = (
        lax.all_to_all(send_keys, ("grp", "seq"), split_axis=0, concat_axis=0, tiled=True),
        lax.all_to_all(send_values, ("grp", "seq"), split_axis=0, concat_axis=0, tiled=True),
        lax.all_to_all(session_slots, ("grp", "seq"), split_axis=0, concat_axis=0, tiled=True),
    )
    new_keys = got_keys.reshape(partition_count * capacity, -1)
    new_values = got_values.reshape(partition_count * capacity, -1)
    new_sessions = got_sessions.reshape(-1)
    heads_kv = new_keys.shape[1] // HEAD
    window = cache_key.shape[1]
    score_scale = HEAD ** (-0.5)
    query_heads = queries.reshape(per_shard, heads_kv, GROUP, HEAD)
    cached_keys = cache_key.reshape(per_shard, window, heads_kv, HEAD)
    cached_values = cache_value.reshape(per_shard, window, heads_kv, HEAD)
    fresh_keys = new_keys.reshape(-1, heads_kv, HEAD)
    fresh_values = new_values.reshape(-1, heads_kv, HEAD)
    cached_scores = (
        jnp.einsum("sghd,swgd->sghw", query_heads, cached_keys, preferred_element_type=jnp.float32)
        * score_scale
    )
    positions = jnp.arange(window, dtype=jnp.int32)
    live_slots = jnp.mod(positions[None, :] - cache_start[:, None], window) < cache_len[:, None]
    cached_scores = jnp.where(live_slots[:, None, None, :], cached_scores, -jnp.inf)
    fresh_scores = (
        jnp.einsum("sghd,ngd->sghn", query_heads, fresh_keys, preferred_element_type=jnp.float32)
        * score_scale
    )
    own_rows = new_sessions[None, :] == jnp.arange(per_shard, dtype=jnp.int32)[:, None]
    fresh_scores = jnp.where(own_rows[:, None, None, :], fresh_scores, -jnp.inf)
    largest = jnp.maximum(jnp.max(cached_scores, axis=3), jnp.max(fresh_scores, axis=3))
    cached_exp = jnp.exp(cached_scores - largest[..., None])
    fresh_exp = jnp.exp(fresh_scores - largest[..., None])
    totals = jnp.sum(cached_exp, axis=3) + jnp.sum(fresh_exp, axis=3)
    cached_weights = (cached_exp / totals[..., None]).astype(jnp.bfloat16)
    fresh_weights = (fresh_exp / totals[..., None]).astype(jnp.bfloat16)
    attended = jnp.einsum(
        "sghw,swgd->sghd", cached_weights, cached_values, preferred_element_type=jnp.float32
    )
    attended = attended + jnp.einsum(
        "sghn,ngd->sghd", fresh_weights, fresh_values, preferred_element_type=jnp.float32
    )
    return attended.reshape(per_shard, -1).astype(jnp.bfloat16)


def local(
    frames,
    token_session,
    ln_gain,
    w_key,
    w_value,
    k_bias,
    v_bias,
    queries,
    cache_key,
    cache_value,
    cache_start,
    cache_len,
):
    partitions = lax.axis_size(("grp", "seq"))
    shares = lax.axis_size("mp")
    per_shard = queries.shape[0]
    rows = frames.shape[0]
    capacity = max(2, 5 * rows // (2 * partitions) + 1)
    members = lax.axis_size("seq")
    near = first_masks(lax.axis_size("grp"), members)
    if near is None or shares != 2 or per_shard % 8 or capacity % 16 or partitions * capacity % HEAD:
        return general(
            frames, token_session, ln_gain, w_key, w_value, k_bias, v_bias, queries, cache_key, cache_value,
            cache_start, cache_len,
        )
    swap = [(0, 1), (1, 0)]
    index = lax.axis_index("mp").astype(jnp.int32).reshape(1)
    here = lax.axis_index(("grp", "seq")).astype(jnp.int32).reshape(1)
    own, held = partial_squares(frames)
    other = lax.ppermute(own, "mp", swap)
    weights = (w_key, w_value, ln_gain[None, :], k_bias[None, :], v_bias[None, :])
    held_key, held_value, gain, key_bias, value_bias, pick, ids = beside(
        here, token_session[None, :], weights, (partitions, per_shard, capacity, near, members)
    )
    normed, sent = send_products(
        index, held, own, other, gain, held_key, held_value, frames.shape[1] * shares
    )
    arrived = lax.ppermute(sent, "mp", swap)
    kept = keep_products(index, normed, held_key, held_value)
    blocks = pack(pick, ids, kept, arrived, key_bias, value_bias, len(near))

    def step(arrays, pairs):
        sent = [lax.ppermute(a, ("grp", "seq"), p) for a, p in zip(arrays[1:], pairs[1:])]
        return [arrays[0], *sent]

    queries, *blocks = lax.optimization_barrier((queries, *blocks))
    scores, laid = cached_scores(cache_start[None, :], cache_len[None, :], queries, cache_key)
    vectors = 2 * cache_key.shape[2] // HEAD
    blocks = step(blocks, [[(i, i ^ mask) for i in range(partitions)] for mask in near])
    blocks = regroup(blocks, members // 2, vectors, capacity)
    blocks = step(blocks, second_pairs(partitions, members))
    return attend(blocks, laid, scores, cache_value, len(near), capacity)


def solution(mesh):
    return jax.shard_map(
        local,
        mesh=mesh,
        in_specs=(
            P(("grp", "seq"), "mp"),
            P(("grp", "seq")),
            P("mp"),
            P("mp", None),
            P("mp", None),
            P("mp"),
            P("mp"),
            P(("grp", "seq"), "mp"),
            P(("grp", "seq"), None, "mp"),
            P(("grp", "seq"), None, "mp"),
            P(("grp", "seq")),
            P(("grp", "seq")),
        ),
        out_specs=P(("grp", "seq"), "mp"),
        check_vma=False,
    )
```

```python
import functools

import jax
import jax.numpy as jnp
from jax import lax
from jax.experimental import pallas as pl
from jax.experimental.pallas import tpu as pltpu
from jax.sharding import PartitionSpec as P

HEAD = 128
GROUP = 8

epsilon = 1e-06


def params(mib):
    return pltpu.CompilerParams(vmem_limit_bytes=mib << 20)


def cost(flops, nbytes):
    return pl.CostEstimate(flops=flops, bytes_accessed=nbytes, transcendentals=0)


def nt_dot(a, b):
    return lax.dot_general(a, b, (((1,), (1,)), ((), ())), preferred_element_type=jnp.float32)


def dot(a, b):
    return jnp.dot(a, b, preferred_element_type=jnp.float32)


SMEM = pl.BlockSpec(memory_space=pltpu.SMEM)
VMEM = pl.BlockSpec(memory_space=pltpu.VMEM)
HBM = pl.BlockSpec(memory_space=pltpu.HBM)


def in_hbm(array):
    return pltpu.with_memory_space_constraint(array, pltpu.HBM)


def squares_kernel(frames_ref, out_ref, held_ref, arrived):
    chunks, columns = arrived.shape[0], frames_ref.shape[1]
    wide = columns // chunks
    copies = []
    for chunk in range(chunks):
        part = (slice(None), pl.ds(chunk * wide, wide))
        copies.append(
            pltpu.make_async_copy(frames_ref.at[part], held_ref.at[part], arrived.at[chunk])
        )
        copies[-1].start()
    total = None
    for chunk in range(chunks):
        copies[chunk].wait()
        for at in range(chunk * wide, (chunk + 1) * wide, HEAD):
            part = held_ref[:, at : at + HEAD].astype(jnp.float32)
            part = part * part
            total = part if total is None else total + part
    out_ref[...] = total


def partial_squares(frames):
    rows, columns = frames.shape
    chunks = 2 if columns % (2 * HEAD) == 0 else 1
    return pl.pallas_call(
        squares_kernel,
        out_shape=(
            jax.ShapeDtypeStruct((rows, HEAD), jnp.float32),
            jax.ShapeDtypeStruct(frames.shape, frames.dtype),
        ),
        in_specs=[HBM],
        out_specs=(VMEM, VMEM),
        scratch_shapes=[pltpu.SemaphoreType.DMA((chunks,))],
        compiler_params=params(8),
        cost_estimate=cost(2 * rows * columns, 2 * rows * columns),
        name="partial_squares",
    )(in_hbm(frames))


def products(normed_ref, half, key_ref, value_ref, out_ref):
    width = key_ref.shape[1] // 2
    columns = pl.ds(pl.multiple_of(half * width, width), width)
    out_ref[:, :width] = dot(normed_ref[...], key_ref[:, columns])
    out_ref[:, width:] = dot(normed_ref[...], value_ref[:, columns])


def send_kernel(
    features, index_ref, frames_ref, own_ref, other_ref, gain_ref, key_ref, value_ref, normed_ref, out_ref
):
    squares = jnp.sum(own_ref[...] + other_ref[...], axis=1, keepdims=True)
    inverse_rms = lax.rsqrt(squares / features + epsilon)
    normed_ref[...] = (
        frames_ref[...].astype(jnp.float32) * inverse_rms * gain_ref[...]
    ).astype(jnp.bfloat16)
    products(normed_ref, 1 - index_ref[0], key_ref, value_ref, out_ref)


def send_products(index, frames, own, other, gain, key, value, features):
    rows, columns = frames.shape
    width = key.shape[1]
    return pl.pallas_call(
        functools.partial(send_kernel, features),
        out_shape=(
            jax.ShapeDtypeStruct(frames.shape, jnp.bfloat16),
            jax.ShapeDtypeStruct((rows, width), jnp.float32),
        ),
        in_specs=[SMEM] + [VMEM] * 6,
        out_specs=(VMEM, VMEM),
        compiler_params=params(16),
        cost_estimate=cost(2 * rows * columns * width, 2 * key.size),
        name="send_products",
    )(index, frames, own, other, gain, key, value)


def keep_kernel(index_ref, normed_ref, key_ref, value_ref, out_ref):
    products(normed_ref, index_ref[0], key_ref, value_ref, out_ref)


def keep_products(index, normed, key, value):
    rows, columns = normed.shape
    width = key.shape[1]
    return pl.pallas_call(
        keep_kernel,
        out_shape=jax.ShapeDtypeStruct((rows, width), jnp.float32),
        in_specs=[SMEM] + [VMEM] * 3,
        out_specs=VMEM,
        compiler_params=params(16),
        cost_estimate=cost(2 * rows * columns * width, 2 * key.size),
        name="keep_products",
    )(index, normed, key, value)


def first_masks(groups, members):
    if groups & (groups - 1) or members & (members - 1) or members < 4:
        return None
    masks = [group * members + low for group in range(groups) for low in range(2)]
    return (0, masks[-1], *masks[1:-1])


def ring_place(device, members):
    upper = (device & (members - 1)) >> 1
    place = upper
    for shift in range(1, (members // 2).bit_length() - 1):
        place = place ^ (upper >> shift)
    return place


def second_pairs(partitions, members):
    line = members // 2
    devices = range(partitions)
    at = {(d // members, d & 1, ring_place(d, members)): d for d in devices}
    return [
        [(d, at[d // members, d & 1, (ring_place(d, members) + up) % line]) for d in devices]
        for up in range(line)
    ]


def route(per_shard, capacity, near, members, here, session, pick_ref, ids_ref):
    slots, rows = pick_ref.shape
    partitions = slots // capacity
    line = members // 2
    target = lax.div(session, per_shard)
    local = session - target * per_shard
    apart = (target ^ here) & functools.reduce(lambda a, b: a | b, near)
    first = sum(jnp.where(apart == mask, at, 0) for at, mask in enumerate(near))
    second = (ring_place(target, members) - ring_place(here, members)) & (line - 1)
    leaves, lands = first * line + second, second * len(near) + first
    to = lax.broadcasted_iota(jnp.int32, (partitions, rows), 0) == leaves
    to = to.astype(jnp.float32)
    earlier = lax.broadcasted_iota(jnp.int32, (rows, rows), 0) < lax.broadcasted_iota(
        jnp.int32, (rows, rows), 1
    )
    ahead = dot(to.astype(jnp.bfloat16), earlier.astype(jnp.bfloat16))
    order = jnp.sum(to * ahead, axis=0, keepdims=True).astype(jnp.int32)
    place = lax.broadcasted_iota(jnp.int32, (slots, rows), 0)
    pick_ref[...] = (place == leaves * capacity + order).astype(jnp.bfloat16)
    lane = lands * capacity + order
    parts = slots // HEAD
    block = lax.broadcasted_iota(jnp.int32, (ids_ref.shape[0], rows), 0)
    named = block == first * (ids_ref.shape[0] // len(near)) + second * parts + lane // HEAD
    named = jnp.where(named, (local + 1).astype(jnp.float32), 0.0).astype(jnp.bfloat16)
    spot = lax.broadcasted_iota(jnp.int32, (HEAD, rows), 0) == lane % HEAD
    ids_ref[...] = nt_dot(named, spot.astype(jnp.bfloat16))


def queries_of(queries_ref, head):
    columns = [
        queries_ref[:, at * HEAD : (at + 1) * HEAD].astype(jnp.float32)
        for at in range(head * GROUP, (head + 1) * GROUP)
    ]
    return jnp.concatenate(columns, axis=0).astype(jnp.bfloat16)


def score_cache(start_ref, len_ref, queries_ref, key_ref, out_ref, laid_ref):
    sessions, window, width = key_ref.shape
    heads, rows = width // HEAD, GROUP * sessions

    def by_row(ref):
        mine = lax.broadcasted_iota(jnp.int32, (rows, sessions), 0) % sessions
        mine = mine == lax.broadcasted_iota(jnp.int32, (rows, sessions), 1)
        values = jnp.where(mine, ref[...].astype(jnp.float32), 0.0)
        return jnp.sum(values, axis=1, keepdims=True).astype(jnp.int32)

    since = lax.broadcasted_iota(jnp.int32, (rows, window), 1) - by_row(start_ref)
    since = jnp.where(since < 0, since + window, since)
    live = since < by_row(len_ref)
    row_session = lax.broadcasted_iota(jnp.int32, (rows, window), 0) % sessions
    laid_ref[...] = jnp.zeros_like(laid_ref)
    for head in range(heads):
        query = queries_of(queries_ref, head)
        laid_ref[head * rows : (head + 1) * rows, head * HEAD : (head + 1) * HEAD] = query
        total = jnp.zeros((rows, window), jnp.float32)
        for session in range(sessions):
            key = key_ref[session, :, head * HEAD : (head + 1) * HEAD]
            total = jnp.where(row_session == session, nt_dot(query, key), total)
        total = jnp.where(live, total * (HEAD**-0.5), -jnp.inf)
        out_ref[head * rows : (head + 1) * rows] = total


def beside_kernel(
    per_shard,
    capacity,
    near,
    members,
    here_ref,
    session_ref,
    w_key_ref,
    w_value_ref,
    held_key_ref,
    held_value_ref,
    pick_ref,
    ids_ref,
    session,
    arrived,
):
    copies = []
    for at, (source, held) in enumerate(
        (
            (w_key_ref, held_key_ref),
            (w_value_ref, held_value_ref),
            (session_ref, session),
        )
    ):
        copies.append(pltpu.make_async_copy(source, held, arrived.at[at]))
        copies[-1].start()
    copies[2].wait()
    route(per_shard, capacity, near, members, here_ref[0], session[...], pick_ref, ids_ref)
    for copy in copies[:2]:
        copy.wait()


def beside(here, session, w_key, w_value, sizes):
    partitions, _, capacity, near, _ = sizes
    slots, rows = partitions * capacity, session.shape[1]
    id_rows = -(-partitions // len(near) * slots // (16 * HEAD)) * 16 * len(near)
    return pl.pallas_call(
        functools.partial(beside_kernel, *sizes[1:]),
        out_shape=(
            jax.ShapeDtypeStruct(w_key.shape, w_key.dtype),
            jax.ShapeDtypeStruct(w_value.shape, w_value.dtype),
            jax.ShapeDtypeStruct((slots, rows), jnp.bfloat16),
            jax.ShapeDtypeStruct((id_rows, HEAD), jnp.float32),
        ),
        in_specs=[SMEM] + [HBM] * 3,
        out_specs=(VMEM,) * 4,
        scratch_shapes=[pltpu.VMEM(session.shape, session.dtype), pltpu.SemaphoreType.DMA((3,))],
        compiler_params=params(24),
        cost_estimate=cost(4 * rows * rows * slots, 4 * w_key.size),
        name="beside",
    )(here, in_hbm(session), in_hbm(w_key), in_hbm(w_value))


def cached_scores(start, length, queries, cache_key):
    sessions, window, width = cache_key.shape
    rows = width // HEAD * GROUP * sessions
    return pl.pallas_call(
        score_cache,
        out_shape=(
            jax.ShapeDtypeStruct((rows, window), jnp.float32),
            jax.ShapeDtypeStruct((rows, width), jnp.bfloat16),
        ),
        in_specs=[VMEM] * 4,
        out_specs=(VMEM, VMEM),
        compiler_params=params(8),
        cost_estimate=cost(2 * GROUP * sessions * cache_key.size, 2 * cache_key.size),
        name="cached_scores",
    )(start, length, queries, cache_key)


def pack_kernel(pick_ref, ids_ref, kept_ref, got_ref, key_bias_ref, value_bias_ref, *out_refs):
    width = key_bias_ref.shape[1]
    sums = kept_ref[...] + got_ref[...]
    key = (sums[:, :width] + key_bias_ref[...]).astype(jnp.bfloat16)
    value = (sums[:, width:] + value_bias_ref[...]).astype(jnp.bfloat16)
    tall = pick_ref.shape[0] // len(out_refs)
    at = 0
    for source in (key, value):
        laid = dot(pick_ref[...], source).astype(jnp.bfloat16)
        for column in range(0, width, HEAD):
            for step, out_ref in enumerate(out_refs):
                out_ref[at : at + tall, :] = laid[
                    step * tall : (step + 1) * tall, column : column + HEAD
                ]
            at += tall
    named = ids_ref.shape[0] // len(out_refs)
    for step, out_ref in enumerate(out_refs):
        out_ref[at:, :] = ids_ref[step * named : (step + 1) * named, :].astype(jnp.bfloat16)


def pack(pick, ids, kept, got, key_bias, value_bias, near):
    rows, width = kept.shape
    slots = pick.shape[0]
    tall = (width // HEAD * slots + ids.shape[0]) // near
    return pl.pallas_call(
        pack_kernel,
        out_shape=[jax.ShapeDtypeStruct((tall, HEAD), jnp.bfloat16)] * near,
        in_specs=[VMEM] * 6,
        out_specs=[VMEM] * near,
        compiler_params=params(8),
        cost_estimate=cost(2 * rows * width * slots, 8 * rows * width),
        name="pack",
    )(pick, ids, kept, got, key_bias, value_bias)


def regroup_kernel(near, vectors, capacity, *refs):
    got_refs, out_refs = refs[:near], refs[near:]
    far = len(out_refs)
    for vector in range(vectors):
        for step, out_ref in enumerate(out_refs):
            for first, got_ref in enumerate(got_refs):
                to, at = (vector * near + first) * capacity, (vector * far + step) * capacity
                out_ref[to : to + capacity, :] = got_ref[at : at + capacity, :]
    ids = sum(ref[vectors * far * capacity :, :].astype(jnp.float32) for ref in got_refs)
    for out_ref in out_refs:
        out_ref[vectors * near * capacity :, :] = ids.astype(jnp.bfloat16)


def regroup(blocks, far, vectors, capacity):
    near = len(blocks)
    tall = blocks[0].shape[0] + vectors * capacity * (near - far)
    return pl.pallas_call(
        functools.partial(regroup_kernel, near, vectors, capacity),
        out_shape=[jax.ShapeDtypeStruct((tall, HEAD), jnp.bfloat16)] * far,
        in_specs=[VMEM] * near,
        out_specs=[VMEM] * far,
        compiler_params=params(8),
        cost_estimate=cost(0, 4 * near * blocks[0].size),
        name="regroup",
    )(*blocks)


def attend_kernel(near, capacity, queries_ref, score_ref, cache_ref, *refs):
    *got_refs, out_ref = refs
    rows, window = score_ref.shape
    sessions, _, width = cache_ref.shape
    heads = width // HEAD
    tall = near * capacity
    slots = len(got_refs) * tall
    parts = slots // HEAD
    ids = [
        sum(
            ref[2 * heads * tall :, :].astype(jnp.float32)[step * parts + part : step * parts + part + 1]
            for step, ref in enumerate(got_refs)
        )
        for part in range(parts)
    ]
    ids = jnp.concatenate(ids, axis=1).astype(jnp.int32)
    own = lax.broadcasted_iota(jnp.int32, (rows, slots), 0) % sessions + 1 == ids

    def rows_of(vectors):
        columns = []
        for vector in vectors:
            part = slice(vector * tall, (vector + 1) * tall)
            columns.append(jnp.concatenate([ref[part, :] for ref in got_refs], axis=0))
        return jnp.concatenate(columns, axis=1)

    cached = score_ref[...]
    fresh = nt_dot(queries_ref[...], rows_of(range(heads))) * (HEAD**-0.5)
    fresh = jnp.where(own, fresh, -jnp.inf)
    largest = jnp.maximum(
        jnp.max(cached, axis=1, keepdims=True), jnp.max(fresh, axis=1, keepdims=True)
    )
    cached = jnp.exp(cached - largest)
    fresh = jnp.exp(fresh - largest)
    total = jnp.sum(cached, axis=1, keepdims=True) + jnp.sum(fresh, axis=1, keepdims=True)
    share = 1.0 / total
    cached = cached * share
    attended = dot((fresh * share).astype(jnp.bfloat16), rows_of(range(heads, 2 * heads)))
    row_session = lax.broadcasted_iota(jnp.int32, (rows, window), 0) % sessions
    for session in range(0, sessions, 2):
        weights = jnp.concatenate(
            [jnp.where(row_session == session + more, cached, 0.0) for more in range(2)], axis=1
        )
        values = cache_ref[session : session + 2].reshape(2 * window, width)
        attended += dot(weights.astype(jnp.bfloat16), values)
    for head in range(heads):
        for q in range(GROUP):
            row, column = (head * GROUP + q) * sessions, (head * GROUP + q) * HEAD
            out_ref[:, column : column + HEAD] = attended[
                row : row + sessions, head * HEAD : (head + 1) * HEAD
            ].astype(jnp.bfloat16)


def attend(got, queries, scores, cache_value, near, capacity):
    return pl.pallas_call(
        functools.partial(attend_kernel, near, capacity),
        out_shape=jax.ShapeDtypeStruct(
            (cache_value.shape[0], queries.shape[1] * GROUP), jnp.bfloat16
        ),
        in_specs=[VMEM] * (3 + len(got)),
        out_specs=VMEM,
        compiler_params=params(8),
        cost_estimate=cost(4 * queries.shape[0] * cache_value.size, 2 * cache_value.size),
        name="attend",
    )(queries, scores, cache_value, *got)


def project(frame_rows, ln_gain, w_key, w_value, k_bias, v_bias):
    values32 = frame_rows.astype(jnp.float32)
    partial_squares = jnp.sum(values32 * values32, axis=1)
    squares = lax.psum(partial_squares, "mp")
    inverse_rms = lax.rsqrt(squares / (frame_rows.shape[1] * lax.axis_size("mp")) + epsilon)
    normed = (values32 * inverse_rms[:, None] * ln_gain[None, :]).astype(jnp.bfloat16)
    part_key = jnp.dot(normed, w_key, preferred_element_type=jnp.float32)
    part_value = jnp.dot(normed, w_value, preferred_element_type=jnp.float32)
    key_sums, value_sums = (
        lax.psum_scatter(part_key, "mp", scatter_dimension=1, tiled=True),
        lax.psum_scatter(part_value, "mp", scatter_dimension=1, tiled=True),
    )
    new_keys = (key_sums + k_bias[None, :]).astype(jnp.bfloat16)
    new_values = (value_sums + v_bias[None, :]).astype(jnp.bfloat16)
    return (new_keys, new_values)


def slot_sources(token_session, per_shard, partition_count, capacity):
    row_count = token_session.shape[0]
    target = token_session // per_shard
    one_hot = (target[:, None] == jnp.arange(partition_count, dtype=jnp.int32)[None, :]).astype(
        jnp.int32
    )
    order_in = jnp.sum((jnp.cumsum(one_hot, axis=0) - one_hot) * one_hot, axis=1)
    slot_index = target * capacity + order_in
    matches = (
        slot_index[None, :] == jnp.arange(partition_count * capacity, dtype=jnp.int32)[:, None]
    )
    source = jnp.sum(jnp.where(matches, jnp.arange(row_count, dtype=jnp.int32)[None, :], 0), axis=1)
    filled = jnp.any(matches, axis=1)
    sessions = jnp.where(filled, jnp.mod(token_session[source], per_shard), -1)
    return (source, filled, sessions)


def general(
    frames,
    token_session,
    ln_gain,
    w_key,
    w_value,
    k_bias,
    v_bias,
    queries,
    cache_key,
    cache_value,
    cache_start,
    cache_len,
):
    partition_count = lax.axis_size(("grp", "seq"))
    per_shard = queries.shape[0]
    rows_here = frames.shape[0]
    capacity = max(2, 5 * rows_here // (2 * partition_count) + 1)
    source, filled, sessions = slot_sources(token_session, per_shard, partition_count, capacity)
    session_slots = sessions.reshape(partition_count, capacity)
    nothing = jnp.zeros((), jnp.bfloat16)
    own_keys, own_values = project(frames, ln_gain, w_key, w_value, k_bias, v_bias)
    send_keys = jnp.where(filled[:, None], own_keys[source], nothing).reshape(
        partition_count, capacity, -1
    )
    send_values = jnp.where(filled[:, None], own_values[source], nothing).reshape(
        partition_count, capacity, -1
    )
    got_keys, got_values, got_sessions = (
        lax.all_to_all(send_keys, ("grp", "seq"), split_axis=0, concat_axis=0, tiled=True),
        lax.all_to_all(send_values, ("grp", "seq"), split_axis=0, concat_axis=0, tiled=True),
        lax.all_to_all(session_slots, ("grp", "seq"), split_axis=0, concat_axis=0, tiled=True),
    )
    new_keys = got_keys.reshape(partition_count * capacity, -1)
    new_values = got_values.reshape(partition_count * capacity, -1)
    new_sessions = got_sessions.reshape(-1)
    heads_kv = new_keys.shape[1] // HEAD
    window = cache_key.shape[1]
    score_scale = HEAD ** (-0.5)
    query_heads = queries.reshape(per_shard, heads_kv, GROUP, HEAD)
    cached_keys = cache_key.reshape(per_shard, window, heads_kv, HEAD)
    cached_values = cache_value.reshape(per_shard, window, heads_kv, HEAD)
    fresh_keys = new_keys.reshape(-1, heads_kv, HEAD)
    fresh_values = new_values.reshape(-1, heads_kv, HEAD)
    cached_scores = (
        jnp.einsum("sghd,swgd->sghw", query_heads, cached_keys, preferred_element_type=jnp.float32)
        * score_scale
    )
    positions = jnp.arange(window, dtype=jnp.int32)
    live_slots = jnp.mod(positions[None, :] - cache_start[:, None], window) < cache_len[:, None]
    cached_scores = jnp.where(live_slots[:, None, None, :], cached_scores, -jnp.inf)
    fresh_scores = (
        jnp.einsum("sghd,ngd->sghn", query_heads, fresh_keys, preferred_element_type=jnp.float32)
        * score_scale
    )
    own_rows = new_sessions[None, :] == jnp.arange(per_shard, dtype=jnp.int32)[:, None]
    fresh_scores = jnp.where(own_rows[:, None, None, :], fresh_scores, -jnp.inf)
    largest = jnp.maximum(jnp.max(cached_scores, axis=3), jnp.max(fresh_scores, axis=3))
    cached_exp = jnp.exp(cached_scores - largest[..., None])
    fresh_exp = jnp.exp(fresh_scores - largest[..., None])
    totals = jnp.sum(cached_exp, axis=3) + jnp.sum(fresh_exp, axis=3)
    cached_weights = (cached_exp / totals[..., None]).astype(jnp.bfloat16)
    fresh_weights = (fresh_exp / totals[..., None]).astype(jnp.bfloat16)
    attended = jnp.einsum(
        "sghw,swgd->sghd", cached_weights, cached_values, preferred_element_type=jnp.float32
    )
    attended = attended + jnp.einsum(
        "sghn,ngd->sghd", fresh_weights, fresh_values, preferred_element_type=jnp.float32
    )
    return attended.reshape(per_shard, -1).astype(jnp.bfloat16)


def local(
    frames,
    token_session,
    ln_gain,
    w_key,
    w_value,
    k_bias,
    v_bias,
    queries,
    cache_key,
    cache_value,
    cache_start,
    cache_len,
):
    partitions = lax.axis_size(("grp", "seq"))
    shares = lax.axis_size("mp")
    per_shard = queries.shape[0]
    rows = frames.shape[0]
    capacity = max(2, 5 * rows // (2 * partitions) + 1)
    members = lax.axis_size("seq")
    near = first_masks(lax.axis_size("grp"), members)
    if near is None or shares != 2 or per_shard % 8 or capacity % 16 or partitions * capacity % HEAD:
        return general(
            frames, token_session, ln_gain, w_key, w_value, k_bias, v_bias, queries, cache_key, cache_value,
            cache_start, cache_len,
        )
    swap = [(0, 1), (1, 0)]
    index = lax.axis_index("mp").astype(jnp.int32).reshape(1)
    here = lax.axis_index(("grp", "seq")).astype(jnp.int32).reshape(1)
    own, held = partial_squares(frames)
    other = lax.ppermute(own, "mp", swap)
    held_key, held_value, pick, ids = beside(
        here, token_session[None, :], w_key, w_value, (partitions, per_shard, capacity, near, members)
    )
    normed, sent = send_products(
        index, held, own, other, ln_gain[None, :], held_key, held_value, frames.shape[1] * shares
    )
    arrived = lax.ppermute(sent, "mp", swap)
    kept = keep_products(index, normed, held_key, held_value)
    blocks = pack(pick, ids, kept, arrived, k_bias[None, :], v_bias[None, :], len(near))

    def step(arrays, pairs):
        sent = [lax.ppermute(a, ("grp", "seq"), p) for a, p in zip(arrays[1:], pairs[1:])]
        return [arrays[0], *sent]

    queries, *blocks = lax.optimization_barrier((queries, *blocks))
    scores, laid = cached_scores(cache_start[None, :], cache_len[None, :], queries, cache_key)
    vectors = 2 * cache_key.shape[2] // HEAD
    blocks = step(blocks, [[(i, i ^ mask) for i in range(partitions)] for mask in near])
    blocks = regroup(blocks, members // 2, vectors, capacity)
    blocks = step(blocks, second_pairs(partitions, members))
    return attend(blocks, laid, scores, cache_value, len(near), capacity)


def solution(mesh):
    return jax.shard_map(
        local,
        mesh=mesh,
        in_specs=(
            P(("grp", "seq"), "mp"),
            P(("grp", "seq")),
            P("mp"),
            P("mp", None),
            P("mp", None),
            P("mp"),
            P("mp"),
            P(("grp", "seq"), "mp"),
            P(("grp", "seq"), None, "mp"),
            P(("grp", "seq"), None, "mp"),
            P(("grp", "seq")),
            P(("grp", "seq")),
        ),
        out_specs=P(("grp", "seq"), "mp"),
        check_vma=False,
    )
```
